32 devices in a mesh: dp: 8 (over z, x), tp: 4 (over y, core).
Axes of the slice: x: 2, y: 2, z: 4, core: 2. Of those that a mesh axis runs over, the one named last changes fastest.
Arguments:
- tokens: bfloat16 [16384, 768], P(('dp', 'tp')), may hold values from -6 to 6
- first_gain: float32 [768], replicated, may hold values from 0.5 to 1.5
- first_bias: float32 [768], replicated, may hold values from -1 to 1
- qkv_weight: bfloat16 [768, 3, 768], P(None, None, 'tp'), may hold values from -0.21875 to 0.21875
- out_weight: bfloat16 [768, 768], P('tp'), may hold values from -0.875 to 0.875
- second_gain: float32 [768], replicated, may hold values from 0.5 to 1.5
- expert_norm_bias: float32 [768], replicated, may hold values from -1 to 1
- up_weight: bfloat16 [8, 768, 1536], P('dp'), may hold values from -0.21875 to 0.21875
- down_weight: bfloat16 [8, 1536, 768], P('dp'), may hold values from -0.21875 to 0.21875
- gate_value: float32 [16384], P(('dp', 'tp')), may hold values from 0.3 to 1
- expert_ids: int32 [16384], P(('dp', 'tp')), may hold values from 0 to 3, as said below
- slot_index: int32 [16384], P(('dp', 'tp')), may hold values from 0 to 255, as said below
- segment_ids: int32 [16384], P(('dp', 'tp')), may hold values from 0 to 1024, as said below
- cotangent: bfloat16 [16384, 768], P(('dp', 'tp')), may hold values from -15 to 15
Outputs:
- output: bfloat16 [16384, 768], P(('dp', 'tp'))
- grad_input: float32 [16384, 768], P(('dp', 'tp'))
- grad_first_gain: float32 [768], replicated
- grad_first_bias: float32 [768], replicated
- grad_qkv_weight: float32 [768, 3, 768], P(None, None, 'tp')
- grad_out_weight: float32 [768, 768], P('tp')
- grad_second_gain: float32 [768], replicated
- grad_second_bias: float32 [768], replicated
- grad_up_weight: float32 [8, 768, 1536], P('dp', None, 'tp')
- grad_down_weight: float32 [8, 1536, 768], P('dp', 'tp')
The draws below stay inside these ranges and needn't reach their ends.
Inputs may be any that keep to these rules, and one draw needn't show every extreme that they name: `expert_ids`: in each aligned block of 512 tokens no expert is named more than 256 times, and some expert is named exactly 256 times. `slot_index`: in each aligned block of 512 tokens, the tokens that name one expert have distinct slots. `segment_ids`: within each packed row of 1024 tokens the ids start at 0 and never fall, distinct documents have distinct ids, and the last document of every packed row has the id 1024; in every packed row one document begins before position 256 and ends at or after position 768.
All inputs are finite; a program needn't handle non-finite values.
Results may differ from the reference program's by a relative error of at most 0.017.
Values may be sent and summed in bfloat16 or wider, within the bound.
No kernel may reach another device: no remote copies, remote signals or barrier semaphores. Data moves between devices by JAX's collectives and lax.ppermute only.
A program may use at most 128 MiB of HBM per device.

```python
import jax
import jax.numpy as jnp
from jax import lax

D = 768
HEADS = 12
HEAD_DIM = 64
FF = 3072
PACKED_LENGTH = 1024
TOK_DEV = 512
EXPERTS = 4
TOTAL_TOKENS = 16384
CAP = 256
N_TP = 4


def route_table(key):
    blocks = TOTAL_TOKENS // TOK_DEV
    places = EXPERTS * CAP
    subkeys = jax.random.split(key, 4)
    owners = jnp.arange(places, dtype=jnp.int32) // CAP
    favour = jax.random.randint(subkeys[0], (EXPERTS,), 0, 3) * 32768
    scores_int = jax.random.randint(subkeys[1], (blocks, places), 0, 65536) + favour[owners][None, :]
    filled = jax.random.randint(subkeys[2], (blocks, 1), 0, EXPERTS)
    ranked = jnp.where(owners[None, :] == filled, -1, scores_int) * places + jnp.arange(places, dtype=jnp.int32)[None, :]
    chosen = jnp.argsort(ranked, axis=1)[:, :TOK_DEV].astype(jnp.int32)
    mixing = jax.random.randint(subkeys[3], (blocks, TOK_DEV), 0, 65536) * TOK_DEV + jnp.arange(TOK_DEV, dtype=jnp.int32)[None, :]
    shuffle = jnp.argsort(mixing, axis=1)
    picked = jnp.take_along_axis(chosen, shuffle, axis=1).reshape(TOTAL_TOKENS).astype(jnp.int32)
    return (picked // CAP, picked % CAP)


def draw_expert_ids(key, part):
    return route_table(key)[0]


def draw_slot_index(key, part):
    return route_table(key)[1]


def draw_segment_ids(key, part):
    key = jax.random.fold_in(key, 5)
    subkeys = jax.random.split(key, 3)
    packed = TOTAL_TOKENS // PACKED_LENGTH
    positions = jnp.arange(PACKED_LENGTH, dtype=jnp.int32)[None, :]
    opening = jax.random.randint(subkeys[0], (packed, 1), 1, PACKED_LENGTH // 4)
    closing = jax.random.randint(subkeys[1], (packed, 1), PACKED_LENGTH - PACKED_LENGTH // 4, PACKED_LENGTH)
    random_cut = (jax.random.randint(subkeys[2], (packed, PACKED_LENGTH), 0, 48) == 0).astype(jnp.int32)
    inside = (positions > opening) & (positions <= closing)
    cuts = jnp.where(inside, 0, random_cut)
    cuts = jnp.where((positions == opening) | (positions == closing + 1), 1, cuts)
    cuts = jnp.where(positions == 0, 0, cuts)
    tallied_count = jnp.cumsum(cuts, axis=1).astype(jnp.int32)
    final_document = tallied_count[:, -1:]
    renumbered_ids = jnp.where(tallied_count == final_document, PACKED_LENGTH, tallied_count)
    return renumbered_ids.reshape(TOTAL_TOKENS).astype(jnp.int32)


def draw_cotangent(key, part):
    key = jax.random.fold_in(key, 9)
    rising = 1.0 + 2.0 * jnp.arange(TOTAL_TOKENS, dtype=jnp.float32)[:, None] / TOTAL_TOKENS
    base = jnp.clip(jax.random.normal(key, (TOTAL_TOKENS, D), jnp.float32), -5.0, 5.0)
    return (base * rising).astype(jnp.bfloat16)


def block_scale(rng, extent, cuts, least, top_value):
    def one(axis_at, blocks):
        heights = jax.random.uniform(jax.random.fold_in(jax.random.fold_in(rng, 6), axis_at), (blocks,), jnp.float32, least / len(cuts), top_value / len(cuts))
        return jnp.repeat(jnp.exp(heights), extent[axis_at] // blocks).reshape((-1,) + (1,) * (len(extent) - axis_at - 1))

    level = one(*cuts[0])
    for cut in cuts[1:]:
        level = level * one(*cut)
    return level


def gaussian(own_key, extent, spread, bound, cuts=(), kind=jnp.bfloat16):
    drawn = jax.random.normal(own_key, extent, jnp.float32) * spread
    if len(cuts) > 0:
        drawn = block_scale(own_key, extent, cuts, -0.22, 0.18) * drawn
    return jnp.clip(drawn, min=-bound, max=bound).astype(kind)


def setup_inputs(seed: int = 0) -> dict:
    arg_keys = jax.random.split(jax.random.key(seed), 15)
    return {
        "tokens": gaussian(arg_keys[0], (TOTAL_TOKENS, D), 1.0, 6.0, ((0, 32),)),
        "first_gain": jnp.clip(1.0 + 0.1 * jax.random.normal(arg_keys[1], (D,), jnp.float32), 0.5, 1.5),
        "first_bias": gaussian(arg_keys[2], (D,), 0.2, 1.0, (), jnp.float32),
        "qkv_weight": gaussian(arg_keys[3], (D, 3, D), D ** -0.5, 0.21875, ((2, 4),)),
        "out_weight": gaussian(arg_keys[4], (D, D), (D // 16) ** -0.5, 0.875, ((0, 4),)),
        "second_gain": jnp.clip(1.0 + 0.1 * jax.random.normal(arg_keys[5], (D,), jnp.float32), 0.5, 1.5),
        "expert_norm_bias": gaussian(arg_keys[6], (D,), 0.2, 1.0, (), jnp.float32),
        "up_weight": gaussian(arg_keys[7], (2 * EXPERTS, D, FF // 2), D ** -0.5, 0.21875, ((0, 8),)),
        "down_weight": gaussian(arg_keys[8], (2 * EXPERTS, FF // 2, D), (FF // 4) ** -0.5, 0.21875, ((0, 8),)),
        "gate_value": jnp.clip(0.3 + 0.7 * jax.random.uniform(arg_keys[9], (TOTAL_TOKENS,), jnp.float32) ** block_scale(arg_keys[9], (TOTAL_TOKENS,), ((0, 32),), -0.2, 0.2), 0.3, 1.0),
        "expert_ids": draw_expert_ids(jax.random.fold_in(arg_keys[14], 71), 0),
        "slot_index": draw_slot_index(jax.random.fold_in(arg_keys[14], 71), 0),
        "segment_ids": draw_segment_ids(jax.random.fold_in(arg_keys[14], 71), 0),
        "cotangent": draw_cotangent(jax.random.fold_in(arg_keys[14], 71), 0),
    }


EPSILON = 1e-05
PRECISE = lax.Precision.HIGHEST

@jax.custom_vjp
def low(v):
    return lax.optimization_barrier(v.astype(jnp.bfloat16)).astype(jnp.float32)

@jax.custom_vjp
def low_back(v):
    return v

def low_keep(v):
    return (low(v), None)

def low_pass(kept, grad):
    return (grad,)

def back_keep(v):
    return (v, None)

def back_low(kept, grad):
    return (low(grad),)
low.defvjp(low_keep, low_pass)
low_back.defvjp(back_keep, back_low)

def normalize(values, norm_gain, norm_bias):
    centre = lax.optimization_barrier(jnp.mean(values, axis=-1, keepdims=True))
    shifted = values - centre
    inverse = lax.rsqrt(lax.optimization_barrier(jnp.mean(shifted * shifted, axis=-1, keepdims=True)) + EPSILON)
    return shifted * inverse * norm_gain + norm_bias

def row_attention(queries, keys_all, values_all, segment_labels):
    length = queries.shape[0]
    scores = jnp.einsum('qhd,khd->hqk', queries, keys_all, precision=PRECISE) * HEAD_DIM ** (-0.5)
    scores = low_back(scores)
    positions = jnp.arange(length, dtype=jnp.int32)
    allowed = (positions[None, :] <= positions[:, None]) & (segment_labels[None, :] == segment_labels[:, None])
    masked = jnp.where(allowed[None], scores, -1e+30)
    highest = lax.optimization_barrier(jnp.max(masked, axis=-1, keepdims=True))
    weight_params = jnp.exp(masked - highest)
    probability = low(weight_params / lax.optimization_barrier(jnp.sum(weight_params, axis=-1, keepdims=True)))
    return jnp.einsum('hqk,khd->qhd', probability, values_all, precision=PRECISE)

def row_item(item):
    return row_attention(item[0], item[1], item[2], item[3])

def expert_item(item):
    preact = low_back(jnp.dot(item[0], item[1], precision=PRECISE))
    hidden = low(jax.nn.gelu(preact, approximate=False))
    return low(jnp.dot(hidden, item[2], precision=PRECISE))

def forward(tokens, first_gain, first_bias, qkv_weight, out_weight, second_gain, expert_norm_bias, up_weight, down_weight, gate_value, expert_ids, slot_index, segment_ids):
    model_width = tokens.shape[1]
    packed = TOTAL_TOKENS // PACKED_LENGTH
    normed = low(normalize(tokens, first_gain, first_bias))
    projected = jnp.dot(normed, qkv_weight.reshape(model_width, 3 * model_width), precision=PRECISE)
    projected = low_back(low(projected)).reshape(packed, PACKED_LENGTH, 3, HEADS, HEAD_DIM)
    attended = lax.map(jax.checkpoint(row_item), (projected[:, :, 0], projected[:, :, 1], projected[:, :, 2], segment_ids.reshape(packed, PACKED_LENGTH)))
    attended = low_back(low(attended.reshape(TOTAL_TOKENS, model_width)))
    group_width = model_width // N_TP
    branch = jnp.zeros((TOTAL_TOKENS, model_width), jnp.float32)
    for group in range(N_TP):
        lower = group * group_width
        upper = lower + group_width
        branch = branch + low(jnp.dot(attended[:, lower:upper], out_weight[lower:upper], precision=PRECISE))
    branch = low_back(branch)
    middle = tokens + branch
    normed_two = low(normalize(middle, second_gain, expert_norm_bias))
    block_of = jnp.arange(TOTAL_TOKENS, dtype=jnp.int32) // TOK_DEV
    column = (block_of * CAP + slot_index).astype(jnp.int32)
    buffer = jnp.zeros((EXPERTS, TOTAL_TOKENS // TOK_DEV * CAP, model_width), jnp.float32)
    buffer = buffer.at[expert_ids, column].set(normed_two)
    owner = jnp.arange(2 * EXPERTS, dtype=jnp.int32) // 2
    halves = low_back(buffer[owner])
    processed = lax.map(jax.checkpoint(expert_item), (halves, up_weight, down_weight))
    first_half = (2 * expert_ids).astype(jnp.int32)
    second_half = (2 * expert_ids + 1).astype(jnp.int32)
    returned = low_back(processed[first_half, column] + processed[second_half, column])
    return middle + gate_value[:, None] * returned

def reference(tokens, first_gain, first_bias, qkv_weight, out_weight, second_gain, expert_norm_bias, up_weight, down_weight, gate_value, expert_ids, slot_index, segment_ids, cotangent):
    floats = (tokens.astype(jnp.float32), first_gain, first_bias, qkv_weight.astype(jnp.float32), out_weight.astype(jnp.float32), second_gain, expert_norm_bias, up_weight.astype(jnp.float32), down_weight.astype(jnp.float32))

    def closed(*params):
        return forward(*params, gate_value, expert_ids, slot_index, segment_ids)
    result, pullback = jax.vjp(closed, *floats)
    grads = pullback(cotangent.astype(jnp.float32))
    return (result.astype(jnp.bfloat16), grads[0], grads[1], grads[2], grads[3], grads[4], grads[5], grads[6], grads[7], grads[8])
```

```python
import functools

import jax
import jax.numpy as jnp
from jax import lax
from jax.experimental import pallas as pl
from jax.experimental.pallas import tpu as pltpu
from jax.sharding import PartitionSpec as P

HEAD_DIM = 64
PACKED_LENGTH = 1024
EPSILON = 1e-05
BF = jnp.bfloat16
F32 = jnp.float32
MASKED = -1e30
CHUNKS = 4


def dot(a, b, ca, cb):
    return lax.dot_general(a, b, (((ca,), (cb,)), ((), ())), preferred_element_type=F32)


def params(mib, **kw):
    return pltpu.CompilerParams(vmem_limit_bytes=mib * 1024 * 1024, **kw)


def cost(flops, nbytes):
    return pl.CostEstimate(flops=int(flops), bytes_accessed=int(nbytes), transcendentals=0)


def vmem():
    return pl.BlockSpec(memory_space=pltpu.VMEM)


def smem():
    return pl.BlockSpec(memory_space=pltpu.SMEM)


def norm_parts(values):
    centre = jnp.mean(values, axis=-1, keepdims=True)
    shifted = values - centre
    inverse = lax.rsqrt(jnp.mean(shifted * shifted, axis=-1, keepdims=True) + EPSILON)
    return shifted * inverse, inverse


def norm_back(grad_normed, scaled, inverse, gain):
    grad_scaled = grad_normed * gain
    first = jnp.mean(grad_scaled, axis=-1, keepdims=True)
    second = jnp.mean(grad_scaled * scaled, axis=-1, keepdims=True)
    return inverse * (grad_scaled - first - scaled * second)


def onehot(places, slots):
    rows = lax.broadcasted_iota(jnp.int32, (slots, places.shape[1]), 0)
    return jnp.where(rows == places, 1.0, 0.0).astype(BF)


def put_chunks(rows, places, outs):
    size = outs[0].shape[0]
    table = onehot(places, size * len(outs))
    for index, out in enumerate(outs):
        out[...] = dot(table[index * size : (index + 1) * size], rows, 1, 0).astype(BF)


def take_chunks(chunks, places):
    size = chunks[0].shape[0]
    table = onehot(places, size * len(chunks))
    total = None
    for index, chunk in enumerate(chunks):
        part = dot(table[index * size : (index + 1) * size], chunk[...], 0, 0)
        total = part if total is None else total + part
    return total


def grad_dispatch_kernel(cot_ref, gate_ref, places_ref, *outs):
    rows = (gate_ref[...] * cot_ref[...].astype(F32)).astype(BF)
    put_chunks(rows, places_ref[...], outs)


def grad_dispatch(cotangent, gate, places):
    tokens, width = cotangent.shape
    size = 2 * tokens // CHUNKS
    return pl.pallas_call(
        grad_dispatch_kernel,
        out_shape=[jax.ShapeDtypeStruct((size, width), BF)] * CHUNKS,
        compiler_params=params(32),
        cost_estimate=cost(4 * tokens * tokens * width, 6 * tokens * width),
        name="grad_dispatch",
    )(cotangent, gate, places)


def attend_kernel(
    first, heads, info, own, oth, gain, bias, weight, segr, segc, *refs
):
    if first:
        rows_out, att, probs, qkv, recip, mask, rows = refs
    else:
        att, probs, qkv, recip, mask = refs
        rows = own
    length = PACKED_LENGTH
    step = pl.program_id(0)
    width = heads * HEAD_DIM
    blk = att.shape[1] // 4
    half = length // 2

    @pl.when(step == 0)
    def start():
        if first:
            parity = info[0]
            for ref, place in ((own, parity), (oth, 1 - parity)):
                scaled, unused = norm_parts(ref[...].astype(F32))
                normed = (scaled * gain[...] + bias[...]).astype(BF)
                rows[pl.ds(pl.multiple_of(place * half, half), half), :] = normed
            rows_out[...] = rows[...]
        projected = dot(weight[...], rows[...], 1, 1).astype(BF)
        qkv[...] = projected
        qkv[0:width, :] = projected[0:width] * jnp.asarray(HEAD_DIM**-0.5, BF)

    for index in range(4):

        @pl.when(step == index)
        def block(index=index):
            upto = (index + 1) * blk
            cols = slice(index * blk, upto)
            keypos = lax.broadcasted_iota(jnp.int32, (upto, blk), 0)
            querypos = lax.broadcasted_iota(jnp.int32, (upto, blk), 1) + index * blk
            allowed = (segc[0:upto, :] == segr[:, cols]) & (keypos <= querypos)
            mask[0:upto, :] = jnp.where(allowed, 0.0, MASKED)
            for head in range(heads):
                at = head * HEAD_DIM
                query = qkv[at : at + HEAD_DIM, cols]
                keys = qkv[width + at : width + at + HEAD_DIM, 0:upto]
                values = qkv[2 * width + at : 2 * width + at + HEAD_DIM, 0:upto]
                scores = dot(keys, query, 0, 0) + mask[0:upto, :]
                highest = jnp.max(scores, axis=0, keepdims=True)
                weights = jnp.exp(scores - highest)
                inverse = 1.0 / jnp.sum(weights, axis=0, keepdims=True)
                low = weights.astype(BF)
                probs[head, 0:upto, :] = low
                result = dot(values, low, 1, 0) * inverse
                att[at : at + HEAD_DIM, cols] = result.astype(BF)
                recip[head : head + 1, cols] = inverse


def attend(first, info, own, oth, gain, bias, weight, segr, segc):
    length = PACKED_LENGTH
    model = own.shape[1]
    width = weight.shape[0] // 3
    heads = width // HEAD_DIM
    blk = length // 4
    outs = [
        jax.ShapeDtypeStruct((width, length), BF),
        jax.ShapeDtypeStruct((heads, length, length), BF),
        jax.ShapeDtypeStruct((3 * width, length), BF),
        jax.ShapeDtypeStruct((8, length), F32),
    ]
    whole = lambda shape: pl.BlockSpec(shape, lambda i: (0,) * len(shape))
    out_specs = [
        whole((width, length)),
        pl.BlockSpec((heads, length, blk), lambda i: (0, 0, i)),
        whole((3 * width, length)),
        whole((8, length)),
    ]
    scratch = [pltpu.VMEM((length, blk), F32)]
    if first:
        outs = [jax.ShapeDtypeStruct((length, model), BF)] + outs
        out_specs = [whole((length, model))] + out_specs
        scratch = scratch + [pltpu.VMEM((length, model), BF)]
    operands = (own, oth, gain, bias, weight, segr, segc)
    return pl.pallas_call(
        functools.partial(attend_kernel, first, heads),
        out_shape=outs,
        grid=(4,),
        in_specs=[smem()] + [whole(o.shape) for o in operands],
        out_specs=out_specs,
        scratch_shapes=scratch,
        compiler_params=params(40, dimension_semantics=("arbitrary",)),
        cost_estimate=cost(
            6 * length * model * width + 8 * heads * length * length * HEAD_DIM,
            2 * heads * length * length + 6 * length * model,
        ),
        name="attend",
    )(info, *operands)


def project_kernel(info, att_a, att_b, out_a, out_b, kept, sent):
    half = kept.shape[0]
    parity = info[0]
    for ref, place in ((sent, 1 - parity), (kept, parity)):
        cols = pl.ds(pl.multiple_of(place * half, half), half)
        total = dot(att_a[:, cols], out_a[...], 0, 0) + dot(att_b[:, cols], out_b[...], 0, 0)
        ref[...] = total.astype(ref.dtype)


def project(info, att_a, att_b, out_a, out_b):
    width, length = att_a.shape
    model = out_a.shape[1]
    return pl.pallas_call(
        project_kernel,
        out_shape=[
            jax.ShapeDtypeStruct((length // 2, model), F32),
            jax.ShapeDtypeStruct((length // 2, model), BF),
        ],
        in_specs=[smem()] + [vmem()] * 4,
        out_specs=[vmem()] * 2,
        compiler_params=params(32),
        cost_estimate=cost(4 * length * model * width, 6 * length * model),
        name="project",
    )(info, att_a, att_b, out_a, out_b)


def middle_kernel(tokens, kept, received, gain, bias, places, middle, *outs):
    values = tokens[...].astype(F32) + (kept[...] + received[...].astype(F32))
    middle[...] = values
    scaled, unused = norm_parts(values)
    normed = (scaled * gain[...] + bias[...]).astype(BF)
    put_chunks(normed, places[...], outs)


def middle_call(tokens, kept, received, gain, bias, places):
    count, width = tokens.shape
    size = 2 * count // CHUNKS
    return pl.pallas_call(
        middle_kernel,
        out_shape=[jax.ShapeDtypeStruct((count, width), F32)]
        + [jax.ShapeDtypeStruct((size, width), BF)] * CHUNKS,
        compiler_params=params(32),
        cost_estimate=cost(4 * count * count * width, 14 * count * width),
        name="middle",
    )(tokens, kept, received, gain, bias, places)


def gelu_parts(x):
    z = jnp.abs(x) * (0.5**0.5)
    t = 1.0 / (1.0 + 0.3275911 * z)
    poly = t * (
        0.254829592
        + t * (-0.284496736 + t * (1.421413741 + t * (-1.453152027 + t * 1.061405429)))
    )
    bell = jnp.exp(-0.5 * x * x)
    tail = 0.5 * poly * bell
    phi = jnp.where(x >= 0.0, 1.0 - tail, tail)
    return x * phi, phi + x * bell * 0.3989422804014327


def expert_kernel(tiles, inputs, grads, *refs):
    ups, downs = refs[:tiles], refs[tiles : 2 * tiles]
    hidden, gpre, result, total = refs[2 * tiles :]
    step = pl.program_id(0)
    for tile in range(tiles):

        @pl.when(step == tile)
        def work(tile=tile):
            up, down = ups[tile][...], downs[tile][...]
            preact = dot(inputs[...], up, 1, 0)
            ghidden = dot(grads[...], down, 1, 1)
            act, slope = gelu_parts(preact)
            hidden[...] = act.astype(BF)
            low = (ghidden * slope).astype(BF)
            gpre[...] = low
            part = dot(low, up, 1, 1)
            if tile == 0:
                total[...] = part
            elif tile < tiles - 1:
                total[...] += part
            else:
                result[...] = (total[...] + part).astype(BF)


def expert(inputs, grads, ups, downs):
    rows, model = inputs.shape
    tiles = len(ups)
    tile = ups[0].shape[1]
    whole = lambda shape: pl.BlockSpec(shape, lambda i: (0,) * len(shape))
    return pl.pallas_call(
        functools.partial(expert_kernel, tiles),
        out_shape=[
            jax.ShapeDtypeStruct((rows, tiles * tile), BF),
            jax.ShapeDtypeStruct((rows, tiles * tile), BF),
            jax.ShapeDtypeStruct((rows, model), BF),
        ],
        grid=(tiles,),
        in_specs=[whole((rows, model))] * 2 + [whole(w.shape) for w in (*ups, *downs)],
        out_specs=[
            pl.BlockSpec((rows, tile), lambda i: (0, i)),
            pl.BlockSpec((rows, tile), lambda i: (0, i)),
            whole((rows, model)),
        ],
        scratch_shapes=[pltpu.VMEM((rows, model), F32)],
        compiler_params=params(48, dimension_semantics=("arbitrary",)),
        cost_estimate=cost(
            6 * rows * model * tile * tiles, 4 * model * tile * tiles + 4 * rows * tile * tiles
        ),
        name="expert",
    )(inputs, grads, *ups, *downs)


def expert_weights_kernel(tiles, *refs):
    n = CHUNKS
    inputs, grads, hiddens, gpres = refs[:n], refs[n : 2 * n], refs[2 * n : 3 * n], refs[3 * n : 4 * n]
    down = refs[4 * n]
    results = refs[4 * n + 1 : 5 * n + 1]
    gup, gdown = refs[5 * n + 1 : 5 * n + 3]
    totals = refs[5 * n + 3 :]
    step = pl.program_id(0)
    up_sum = None
    down_sum = None
    for index in range(n):
        hid = hiddens[index][...]
        up_part = dot(inputs[index][...], gpres[index][...], 0, 0)
        down_part = dot(hid, grads[index][...], 0, 0)
        up_sum = up_part if up_sum is None else up_sum + up_part
        down_sum = down_part if down_sum is None else down_sum + down_part
        part = dot(hid, down[0], 1, 0)

        @pl.when(step == 0)
        def first(index=index, part=part):
            totals[index][...] = part

        @pl.when((step > 0) & (step < tiles - 1))
        def between(index=index, part=part):
            totals[index][...] += part

        @pl.when(step == tiles - 1)
        def last(index=index, part=part):
            results[index][...] = (totals[index][...] + part).astype(BF)

    gup[0] = up_sum.astype(BF)
    gdown[0] = down_sum.astype(BF)


def expert_weights(inputs, grads, hiddens, gpres, downs):
    rows, model = inputs[0].shape
    tiles = len(downs)
    tile = downs[0].shape[0]
    down = jnp.stack(downs)
    whole = lambda shape: pl.BlockSpec(shape, lambda i: (0,) * len(shape))
    return pl.pallas_call(
        functools.partial(expert_weights_kernel, tiles),
        out_shape=[jax.ShapeDtypeStruct((rows, model), BF)] * CHUNKS
        + [
            jax.ShapeDtypeStruct((tiles, model, tile), BF),
            jax.ShapeDtypeStruct((tiles, tile, model), BF),
        ],
        grid=(tiles,),
        in_specs=[whole((rows, model))] * (2 * CHUNKS)
        + [pl.BlockSpec((rows, tile), lambda i: (0, i))] * (2 * CHUNKS)
        + [pl.BlockSpec((1, tile, model), lambda i: (i, 0, 0))],
        out_specs=[whole((rows, model))] * CHUNKS
        + [
            pl.BlockSpec((1, model, tile), lambda i: (i, 0, 0)),
            pl.BlockSpec((1, tile, model), lambda i: (i, 0, 0)),
        ],
        scratch_shapes=[pltpu.VMEM((rows, model), F32)] * CHUNKS,
        compiler_params=params(48, dimension_semantics=("arbitrary",)),
        cost_estimate=cost(
            6 * CHUNKS * rows * model * tile * tiles, 8 * model * tile * tiles
        ),
        name="expert_weights",
    )(*inputs, *grads, *hiddens, *gpres, down)


def second_back_kernel(*refs):
    chunks = refs[:CHUNKS]
    middle, cot, gain, places, gmid, gbranch, gvec = refs[CHUNKS:]
    grad = take_chunks(chunks, places[...])
    scaled, inverse = norm_parts(middle[...])
    total = cot[...].astype(F32) + norm_back(grad, scaled, inverse, gain[...])
    gmid[...] = total
    gbranch[...] = total.astype(BF)
    gvec[...] = jnp.zeros_like(gvec)
    gvec[0:1, :] = jnp.sum(grad * scaled, axis=0, keepdims=True)
    gvec[1:2, :] = jnp.sum(grad, axis=0, keepdims=True)


def second_back(chunks, middle, cotangent, gain, places):
    count, width = cotangent.shape
    return pl.pallas_call(
        second_back_kernel,
        out_shape=[
            jax.ShapeDtypeStruct((count, width), F32),
            jax.ShapeDtypeStruct((count, width), BF),
            jax.ShapeDtypeStruct((8, width), F32),
        ],
        compiler_params=params(32),
        cost_estimate=cost(4 * count * count * width, 16 * count * width),
        name="second_back",
    )(*chunks, middle, cotangent, gain, places)


def output_kernel(*refs):
    chunks = refs[:CHUNKS]
    middle, gate, places, out = refs[CHUNKS:]
    out[...] = (middle[...] + gate[...] * take_chunks(chunks, places[...])).astype(BF)


def output_call(chunks, middle, gate, places):
    return pl.pallas_call(
        output_kernel,
        out_shape=jax.ShapeDtypeStruct(middle.shape, BF),
        compiler_params=params(32),
        cost_estimate=cost(4 * middle.shape[0] * middle.size, 8 * middle.size),
        name="output",
    )(*chunks, middle, gate, places)


def attend_back_kernel(
    heads, last_group, info, own, oth, rows, weight, outw, att, qkv, recip, probs, *refs
):
    if last_group:
        before, gweight, gout, kept, sent, gbranch, gatt, gqkv = refs
    else:
        gweight, gout, gnormed, gbranch, gatt, gqkv = refs
    length = PACKED_LENGTH
    step = pl.program_id(0)
    width = heads * HEAD_DIM
    blk = length // 4
    half = length // 2

    @pl.when(step == 0)
    def start():
        parity = info[0]
        for ref, place in ((own, parity), (oth, 1 - parity)):
            gbranch[pl.ds(pl.multiple_of(place * half, half), half), :] = ref[...]
        gatt[...] = dot(outw[...], gbranch[...], 1, 1).astype(BF)
        gout[...] = dot(att[...], gbranch[...], 1, 0).astype(BF)
        gqkv[...] = jnp.zeros_like(gqkv)

    for index in range(4):

        @pl.when(step == index)
        def block(index=index):
            upto = (index + 1) * blk
            cols = slice(index * blk, upto)
            for head in range(heads):
                at = head * HEAD_DIM
                here = slice(at, at + HEAD_DIM)
                kat = slice(width + at, width + at + HEAD_DIM)
                vat = slice(2 * width + at, 2 * width + at + HEAD_DIM)
                query, keys, values = qkv[here, cols], qkv[kat, 0:upto], qkv[vat, 0:upto]
                grad = (gatt[here, cols].astype(F32) * recip[head : head + 1, cols]).astype(BF)
                inner = jnp.sum(
                    grad.astype(F32) * att[here, cols].astype(F32), axis=0, keepdims=True
                )
                low = probs[head, 0:upto, :]
                gprobs = dot(values, grad, 0, 0)
                gscores = (low.astype(F32) * (gprobs - inner)).astype(BF)
                gqkv[vat, 0:upto] += dot(grad, low, 1, 1)
                gqkv[kat, 0:upto] += dot(query, gscores, 1, 1)
                gqkv[here, cols] = dot(keys, gscores, 1, 0) * HEAD_DIM**-0.5

    @pl.when(step == 3)
    def finish():
        grads = gqkv[...].astype(BF)
        gweight[...] = dot(grads, rows[...], 1, 0).astype(BF)
        if last_group:
            parity = info[0]
            for ref, place in ((sent, 1 - parity), (kept, parity)):
                at = pl.ds(pl.multiple_of(place * half, half), half)
                gqkv_low = gqkv[:, at].astype(BF)
                total = dot(gqkv_low, weight[...], 0, 0) + before[at, :]
                ref[...] = total.astype(ref.dtype)
        else:
            gnormed[...] = dot(grads, weight[...], 0, 0)


def attend_back(info, own, oth, rows, weight, outw, att, qkv, recip, probs, before=None):
    length, model = rows.shape
    width = att.shape[0]
    heads = width // HEAD_DIM
    blk = length // 4
    whole = lambda shape: pl.BlockSpec(shape, lambda i: (0,) * len(shape))
    operands = [own, oth, rows, weight, outw, att, qkv, recip, probs]
    in_specs = [smem()] + [whole(o.shape) for o in operands[:-1]]
    in_specs.append(pl.BlockSpec((heads, length, blk), lambda i: (0, 0, i)))
    shapes = [((3 * width, model), BF), ((width, model), BF)]
    if before is None:
        shapes.append(((length, model), F32))
    else:
        operands.append(before)
        in_specs.append(whole(before.shape))
        shapes += [((length // 2, model), F32), ((length // 2, model), BF)]
    return pl.pallas_call(
        functools.partial(attend_back_kernel, heads, before is not None),
        out_shape=[jax.ShapeDtypeStruct(s, d) for s, d in shapes],
        grid=(4,),
        in_specs=in_specs,
        out_specs=[whole(s) for s, d in shapes],
        scratch_shapes=[
            pltpu.VMEM((length, model), BF),
            pltpu.VMEM((width, length), BF),
            pltpu.VMEM((3 * width, length), F32),
        ],
        compiler_params=params(48, dimension_semantics=("arbitrary",)),
        cost_estimate=cost(
            16 * length * model * width + 16 * heads * length * length * HEAD_DIM,
            2 * heads * length * length + 10 * length * model,
        ),
        name="attend_back",
    )(info, *operands)


def first_back_kernel(tokens, gmid, kept, received, gain, ginput, gvec):
    grad = kept[...] + received[...].astype(F32)
    scaled, inverse = norm_parts(tokens[...].astype(F32))
    ginput[...] = gmid[...] + norm_back(grad, scaled, inverse, gain[...])
    gvec[...] = jnp.zeros_like(gvec)
    gvec[0:1, :] = jnp.sum(grad * scaled, axis=0, keepdims=True)
    gvec[1:2, :] = jnp.sum(grad, axis=0, keepdims=True)


def first_back(tokens, gmid, kept, received, gain):
    count, width = tokens.shape
    return pl.pallas_call(
        first_back_kernel,
        out_shape=[
            jax.ShapeDtypeStruct((count, width), F32),
            jax.ShapeDtypeStruct((8, width), F32),
        ],
        compiler_params=params(32),
        cost_estimate=cost(20 * count * width, 16 * count * width),
        name="first_back",
    )(tokens, gmid, kept, received, gain)


def swap(values, axis, bit):
    pairs = [(i, i ^ bit) for i in range(lax.axis_size(axis))]
    return lax.ppermute(values, axis, pairs)


def expert_groups(count):
    return [[2 * e + k for e in range(count)] for k in range(2)]


def exchange(blocks, count, here):
    if count == len(blocks):
        return [blocks[0]] + [swap(b, "dp", 2 * s) for s, b in enumerate(blocks) if s > 0]
    whole = jnp.concatenate(blocks, axis=0)
    order = here ^ jnp.arange(count, dtype=jnp.int32)
    shaped = whole.reshape(count, -1, whole.shape[1])[order]
    moved = lax.all_to_all(
        shaped, "dp", 0, 0, tiled=True, axis_index_groups=expert_groups(count)
    )
    moved = moved[order].reshape(whole.shape)
    size = whole.shape[0] // len(blocks)
    return [moved[i * size : (i + 1) * size] for i in range(len(blocks))]


def sum_all(values, axes):
    for axis in axes:
        bit = 1
        while bit < lax.axis_size(axis):
            values = values + swap(values, axis, bit)
            bit *= 2
    return values


def sum_dp(values, count, here, k):
    rows, columns = values.shape
    half = rows // 2
    low = values.astype(BF)
    gone = lax.dynamic_slice_in_dim(low, (1 - k) * half, half, 0)
    kept = lax.dynamic_slice_in_dim(values, k * half, half, 0)
    kept = kept + swap(gone, "dp", 1).astype(F32)
    piece = half // count
    if count <= 4:
        low = kept.astype(BF)
        total = lax.dynamic_slice_in_dim(kept, here * piece, piece, 0)
        for s in range(1, count):
            block = lax.dynamic_slice_in_dim(low, (here ^ s) * piece, piece, 0)
            total = total + swap(block, "dp", 2 * s).astype(F32)
        total = total.astype(BF)
        full = jnp.zeros((half, columns), BF)
        full = lax.dynamic_update_slice_in_dim(full, total, here * piece, 0)
        for s in range(1, count):
            full = lax.dynamic_update_slice_in_dim(
                full, swap(total, "dp", 2 * s), (here ^ s) * piece, 0
            )
    else:
        groups = expert_groups(count)
        blocks = kept.astype(BF).reshape(count, piece, columns)
        blocks = lax.all_to_all(blocks, "dp", 0, 0, tiled=True, axis_index_groups=groups)
        total = jnp.sum(blocks.astype(F32), axis=0).astype(BF)
        full = lax.all_gather(total, "dp", axis=0, tiled=True, axis_index_groups=groups)
    other = swap(full, "dp", 1)
    first, second = jnp.where(k == 0, full, other), jnp.where(k == 0, other, full)
    return jnp.concatenate([first, second], axis=0).astype(F32)


def local(
    tokens,
    first_gain,
    first_bias,
    qkv_weight,
    out_weight,
    second_gain,
    expert_norm_bias,
    up_weight,
    down_weight,
    gate_value,
    expert_ids,
    slot_index,
    segment_ids,
    cotangent,
):
    count, model = tokens.shape
    width = qkv_weight.shape[2]
    tp = lax.axis_index("tp")
    dp = lax.axis_index("dp")
    parity = tp % 2
    row_half = tp // 2 % 2
    k = dp % 2
    here = dp // 2
    experts = lax.axis_size("dp") // 2
    capacity = 2 * count // experts
    info = jnp.stack([parity, here]).astype(jnp.int32)
    vector = lambda v: v.reshape(1, model)

    other_tokens = swap(tokens, "tp", 1)
    other_segments = swap(segment_ids, "tp", 1)
    weight_a = jnp.transpose(qkv_weight, (1, 2, 0)).reshape(3 * width, model)
    weight_b = swap(weight_a, "tp", 2)
    out_b = swap(out_weight, "tp", 2)
    tile = up_weight.shape[2] // 2
    sub = tile // 2
    up_sub = up_weight.reshape(model, 2, 2, sub)
    down_sub = down_weight.reshape(2, 2, sub, model)

    def pick(which):
        up = lax.dynamic_index_in_dim(up_sub, which, 2, keepdims=False).reshape(model, tile)
        down = lax.dynamic_index_in_dim(down_sub, which, 1, keepdims=False).reshape(tile, model)
        return up, down

    up0, down0 = pick(parity)
    up1, down1 = pick(1 - parity)
    up2, down2 = swap(up0, "dp", 1), swap(down0, "dp", 1)
    up3, down3 = swap(up2, "tp", 1), swap(down2, "tp", 1)
    ups, downs = (up0, up1, up2, up3), (down0, down1, down2, down3)

    places = ((expert_ids ^ here) * capacity + slot_index).reshape(1, count)
    gate = gate_value.reshape(count, 1)
    sent_grads = grad_dispatch(cotangent, gate, places)
    grads = exchange(sent_grads, experts, here)

    segments = jnp.where(
        parity == 0,
        jnp.concatenate([segment_ids, other_segments]),
        jnp.concatenate([other_segments, segment_ids]),
    )
    segr, segc = segments.reshape(1, -1), segments.reshape(-1, 1)
    gain, bias = vector(first_gain), vector(first_bias)
    rows, att_a, probs_a, qkv_a, recip_a = attend(
        True, info, tokens, other_tokens, gain, bias, weight_a, segr, segc
    )
    att_b, probs_b, qkv_b, recip_b = attend(
        False, info, rows, other_segments.reshape(1, -1), gain, bias, weight_b, segr, segc
    )
    kept, sent = project(info, att_a, att_b, out_weight, out_b)
    received = swap(sent, "tp", 1)
    middle, *sent_rows = middle_call(
        tokens, kept, received, vector(second_gain), vector(expert_norm_bias), places
    )

    inputs = exchange(sent_rows, experts, here)
    hiddens, gpres, backs = [], [], []
    for index in range(CHUNKS):
        hidden, gpre, back = expert(inputs[index], grads[index], ups, downs)
        hiddens.append(hidden)
        gpres.append(gpre)
        backs.append(back)
    returned = exchange(backs, experts, here)
    *results, gup, gdown = expert_weights(inputs, grads, hiddens, gpres, downs)
    gmid, gbranch, gvec_two = second_back(
        returned, middle, cotangent, vector(second_gain), places
    )
    outs = exchange(results, experts, here)
    output = output_call(outs, middle, gate, places)

    def over_cores(values):
        return [
            (values[i].astype(F32) + swap(values[i + 1], "tp", 1).astype(F32)).astype(BF)
            for i in (0, 2)
        ]

    gup_mine, gup_other = over_cores(gup)
    gdown_mine, gdown_other = over_cores(gdown)
    gup_mine = gup_mine.astype(F32) + swap(gup_other, "dp", 1).astype(F32)
    gdown_mine = gdown_mine.astype(F32) + swap(gdown_other, "dp", 1).astype(F32)

    def over_rows(values, axis):
        away = lax.dynamic_slice_in_dim(values, (1 - row_half) * sub, sub, axis)
        stays = lax.dynamic_slice_in_dim(values, row_half * sub, sub, axis)
        return stays + swap(away.astype(BF), "tp", 2).astype(F32)

    grad_up = over_rows(gup_mine, 1)[None]
    grad_down = over_rows(gdown_mine, 0)[None]

    other_branch = swap(gbranch, "tp", 1)
    gweight_b, gout_b, before = attend_back(
        info, gbranch, other_branch, rows, weight_b, out_b, att_b, qkv_b, recip_b, probs_b
    )
    gweight_a, gout_a, gkept, gsent = attend_back(
        info, gbranch, other_branch, rows, weight_a, out_weight, att_a, qkv_a, recip_a, probs_a,
        before,
    )
    greceived = swap(gsent, "tp", 1)
    grad_input, gvec_one = first_back(tokens, gmid, gkept, greceived, gain)
    theirs_weight = swap(gweight_b, "tp", 2)
    theirs_out = swap(gout_b, "tp", 2)
    gweight = gweight_a.astype(F32) + theirs_weight.astype(F32)
    gout = gout_a.astype(F32) + theirs_out.astype(F32)
    summed = sum_dp(jnp.concatenate([gweight, gout], axis=0), experts, here, k)
    grad_qkv = jnp.transpose(summed[: 3 * width].reshape(3, width, model), (2, 0, 1))
    grad_out = summed[3 * width :]
    vec_two = sum_all(gvec_two, ("tp", "dp"))
    vec_one = sum_all(gvec_one, ("tp", "dp"))
    return (
        output,
        grad_input,
        vec_one[0],
        vec_one[1],
        grad_qkv,
        grad_out,
        vec_two[0],
        vec_two[1],
        grad_up,
        grad_down,
    )


def solution(mesh):
    placed = (
        P(("dp", "tp"), None),
        P(),
        P(),
        P(None, None, "tp"),
        P("tp", None),
        P(),
        P(),
        P("dp", None, None),
        P("dp", None, None),
        P(("dp", "tp")),
        P(("dp", "tp")),
        P(("dp", "tp")),
        P(("dp", "tp")),
        P(("dp", "tp"), None),
    )
    return jax.shard_map(
        local,
        mesh=mesh,
        in_specs=placed,
        out_specs=(
            P(("dp", "tp"), None),
            P(("dp", "tp"), None),
            P(),
            P(),
            P(None, None, "tp"),
            P("tp", None),
            P(),
            P(),
            P("dp", None, "tp"),
            P("dp", "tp", None),
        ),
        check_vma=False,
    )
```

```python
import functools

import jax
import jax.numpy as jnp
from jax import lax
from jax.experimental import pallas as pl
from jax.experimental.pallas import tpu as pltpu
from jax.sharding import PartitionSpec as P

HEAD_DIM = 64
PACKED_LENGTH = 1024
EPSILON = 1e-05
BF = jnp.bfloat16
F32 = jnp.float32
MASKED = -1e30
CHUNKS = 4


def dot(a, b, ca, cb):
    return lax.dot_general(a, b, (((ca,), (cb,)), ((), ())), preferred_element_type=F32)


def params(mib, **kw):
    return pltpu.CompilerParams(vmem_limit_bytes=mib * 1024 * 1024, **kw)


def cost(flops, nbytes):
    return pl.CostEstimate(flops=int(flops) // 64, bytes_accessed=int(nbytes) // 64, transcendentals=0)


def vmem():
    return pl.BlockSpec(memory_space=pltpu.VMEM)


def hbm():
    return pl.BlockSpec(memory_space=pltpu.HBM)


def smem():
    return pl.BlockSpec(memory_space=pltpu.SMEM)


def norm_parts(values):
    centre = jnp.mean(values, axis=-1, keepdims=True)
    shifted = values - centre
    inverse = lax.rsqrt(jnp.mean(shifted * shifted, axis=-1, keepdims=True) + EPSILON)
    return shifted * inverse, inverse


def norm_back(grad_normed, scaled, inverse, gain):
    grad_scaled = grad_normed * gain
    first = jnp.mean(grad_scaled, axis=-1, keepdims=True)
    second = jnp.mean(grad_scaled * scaled, axis=-1, keepdims=True)
    return inverse * (grad_scaled - first - scaled * second)


def column(row):
    return jnp.transpose(jnp.broadcast_to(row, (8, row.shape[1])))[:, 0:1]


def onehot(places, slots):
    rows = lax.broadcasted_iota(jnp.int32, (slots, places.shape[1]), 0)
    return jnp.where(rows == places, 1.0, 0.0).astype(BF)


def put_chunks(rows, places, outs):
    size = outs[0].shape[0]
    table = onehot(places, size * len(outs))
    for index, out in enumerate(outs):
        out[...] = dot(table[index * size : (index + 1) * size], rows, 1, 0).astype(BF)


def take_chunks(chunks, places):
    size = chunks[0].shape[0]
    table = onehot(places, size * len(chunks))
    total = None
    for index, chunk in enumerate(chunks):
        part = dot(table[index * size : (index + 1) * size], chunk[...], 0, 0)
        total = part if total is None else total + part
    return total


def grad_dispatch_kernel(info, cot_ref, gate_ref, places_ref, out):
    rows = (column(gate_ref[...]) * cot_ref[...].astype(F32)).astype(BF)
    put_chunks(rows, places_ref[...], [out])


def grad_dispatch(info, cotangent, gate, places):
    tokens, width = cotangent.shape
    return pl.pallas_call(
        grad_dispatch_kernel,
        out_shape=jax.ShapeDtypeStruct((2 * tokens, width), BF),
        in_specs=[smem()] + [vmem()] * 3,
        out_specs=vmem(),
        compiler_params=params(12),
        cost_estimate=cost(4 * tokens * tokens * width, 6 * tokens * width),
        name="grad_dispatch",
    )(info, cotangent, gate, places)


def give_kernel(info, up, down, given, buffer, sems):
    tile = up.shape[0]
    at = pl.ds(pl.multiple_of(info[0] * tile, tile), tile)
    first, second = slice(0, tile), slice(tile, 2 * tile)
    loads = [
        pltpu.make_async_copy(up.at[:, at], buffer.at[first, :], sems.at[0]),
        pltpu.make_async_copy(down.at[at, :], buffer.at[second, :], sems.at[1]),
    ]
    for load in loads:
        load.start()
    stores = []
    for index, part in enumerate((first, second)):
        loads[index].wait()
        store = pltpu.make_async_copy(buffer.at[part, :], given.at[part, :], sems.at[2 + index])
        store.start()
        stores.append(store)
    for store in stores:
        store.wait()


def give(info, up, down):
    hbm = pl.BlockSpec(memory_space=pltpu.HBM)
    return pl.pallas_call(
        give_kernel,
        out_shape=jax.ShapeDtypeStruct((up.shape[1], up.shape[0]), BF),
        in_specs=[smem(), hbm, hbm],
        out_specs=hbm,
        scratch_shapes=[
            pltpu.VMEM((up.shape[1], up.shape[0]), BF),
            pltpu.SemaphoreType.DMA((4,)),
        ],
        compiler_params=params(60),
        cost_estimate=cost(1, 4 * up.size),
        name="give",
    )(info, up, down)


BLOCKS = 2


def attend_kernel(first, heads, info, own, oth, gain, bias, weight, seg_own, seg_oth, *refs):
    parity = info[0]
    half = PACKED_LENGTH // 2
    if first:
        rows_out, att, probs, qkv, recip, segr, mask, buffer, sems, rows = refs
        for ref, place in ((own, parity), (oth, 1 - parity)):
            scaled, unused = norm_parts(ref[...].astype(F32))
            normed = (scaled * gain[...] + bias[...]).astype(BF)
            rows[pl.ds(pl.multiple_of(place * half, half), half), :] = normed
        rows_out[...] = rows[...]
    else:
        att, probs, qkv, recip, segr, mask, buffer, sems = refs
        rows = own
    for ref, place in ((seg_own, parity), (seg_oth, 1 - parity)):
        at = pl.ds(pl.multiple_of(place * half, half), half)
        segr[:, at] = jnp.broadcast_to(ref[...].astype(F32), (8, half))
    segc = jnp.transpose(segr[...])[:, 0:1]
    width = heads * HEAD_DIM
    blk = att.shape[1] // BLOCKS
    projected = dot(weight[...], rows[...], 1, 1).astype(BF)
    qkv[...] = projected
    qkv[0:width, :] = projected[0:width] * jnp.asarray(HEAD_DIM**-0.5, BF)
    copies = []
    for index in reversed(range(BLOCKS)):
        upto = (index + 1) * blk
        cols = slice(index * blk, upto)
        keypos = lax.broadcasted_iota(jnp.int32, (upto, blk), 0)
        querypos = lax.broadcasted_iota(jnp.int32, (upto, blk), 1) + index * blk
        allowed = (segc[0:upto, :] == segr[0:1, cols]) & (keypos <= querypos)
        mask[0:upto, :] = jnp.where(allowed, 0.0, MASKED)
        for head in range(heads):
            at = head * HEAD_DIM
            query = qkv[at : at + HEAD_DIM, cols]
            keys = qkv[width + at : width + at + HEAD_DIM, 0:upto]
            values = qkv[2 * width + at : 2 * width + at + HEAD_DIM, 0:upto]
            scores = dot(keys, query, 0, 0) + mask[0:upto, :]
            highest = jnp.max(scores, axis=0, keepdims=True)
            weights = jnp.exp(scores - highest)
            inverse = 1.0 / jnp.sum(weights, axis=0, keepdims=True)
            low = weights.astype(BF)
            buffer[index, head, 0:upto, :] = low
            result = dot(values, low, 1, 0) * inverse
            att[at : at + HEAD_DIM, cols] = result.astype(BF)
            recip[head : head + 1, cols] = inverse
        copy = pltpu.make_async_copy(
            buffer.at[index, :, 0:upto, :], probs.at[index, :, 0:upto, :], sems.at[index]
        )
        copy.start()
        copies.append(copy)
    for copy in copies:
        copy.wait()


def attend(info, first, own, oth, gain, bias, weight, seg_own, seg_oth):
    length = PACKED_LENGTH
    model = own.shape[1]
    width = weight.shape[0] // 3
    heads = width // HEAD_DIM
    blk = length // BLOCKS
    outs = [
        jax.ShapeDtypeStruct((width, length), BF),
        jax.ShapeDtypeStruct((BLOCKS, heads, length, blk), BF),
        jax.ShapeDtypeStruct((3 * width, length), BF),
        jax.ShapeDtypeStruct((8, length), F32),
    ]
    out_specs = [vmem(), pl.BlockSpec(memory_space=pltpu.HBM), vmem(), vmem()]
    scratch = [
        pltpu.VMEM((8, length), F32),
        pltpu.VMEM((length, blk), F32),
        pltpu.VMEM((BLOCKS, heads, length, blk), BF),
        pltpu.SemaphoreType.DMA((BLOCKS,)),
    ]
    if first:
        outs = [jax.ShapeDtypeStruct((length, model), BF)] + outs
        out_specs = [vmem()] + out_specs
        scratch = scratch + [pltpu.VMEM((length, model), BF)]
    operands = (own, oth, gain, bias, weight, seg_own, seg_oth)
    return pl.pallas_call(
        functools.partial(attend_kernel, first, heads),
        out_shape=outs,
        in_specs=[smem()] + [vmem()] * len(operands),
        out_specs=out_specs,
        scratch_shapes=scratch,
        compiler_params=params(56),
        cost_estimate=cost(
            6 * length * model * width + 8 * heads * length * length * HEAD_DIM,
            2 * heads * length * length + 6 * length * model,
        ),
        name="attend",
    )(info, *operands)


def project_kernel(info, att_a, att_b, out_a, out_b, kept, sent):
    half = kept.shape[0]
    parity = info[0]
    for ref, place in ((sent, 1 - parity), (kept, parity)):
        cols = pl.ds(pl.multiple_of(place * half, half), half)
        total = dot(att_a[:, cols], out_a[...], 0, 0) + dot(att_b[:, cols], out_b[...], 0, 0)
        ref[...] = total.astype(ref.dtype)


def project(info, att_a, att_b, out_a, out_b):
    width, length = att_a.shape
    model = out_a.shape[1]
    return pl.pallas_call(
        project_kernel,
        out_shape=[
            jax.ShapeDtypeStruct((length // 2, model), F32),
            jax.ShapeDtypeStruct((length // 2, model), F32),
        ],
        in_specs=[smem()] + [vmem()] * 4,
        out_specs=[vmem()] * 2,
        compiler_params=params(12),
        cost_estimate=cost(4 * length * model * width, 6 * length * model),
        name="project",
    )(info, att_a, att_b, out_a, out_b)


def middle_kernel(info, tokens, kept, received, gain, bias, places, middle, *outs):
    values = tokens[...].astype(F32) + (kept[...] + received[...].astype(F32))
    middle[...] = values
    scaled, unused = norm_parts(values)
    normed = (scaled * gain[...] + bias[...]).astype(BF)
    put_chunks(normed, places[...], outs)


def middle_call(info, tokens, kept, received, gain, bias, places):
    count, width = tokens.shape
    size = 2 * count // CHUNKS
    return pl.pallas_call(
        middle_kernel,
        out_shape=[jax.ShapeDtypeStruct((count, width), F32)]
        + [jax.ShapeDtypeStruct((size, width), BF)] * CHUNKS,
        in_specs=[smem()] + [vmem()] * 6,
        out_specs=[vmem()] * (1 + CHUNKS),
        compiler_params=params(16),
        cost_estimate=cost(4 * count * count * width, 14 * count * width),
        name="middle",
    )(info, tokens, kept, received, gain, bias, places)


def gelu_parts(x):
    z = jnp.abs(x) * (0.5**0.5)
    t = 1.0 / (1.0 + 0.3275911 * z)
    poly = t * (
        0.254829592
        + t * (-0.284496736 + t * (1.421413741 + t * (-1.453152027 + t * 1.061405429)))
    )
    bell = jnp.exp(-0.5 * x * x)
    tail = 0.5 * poly * bell
    phi = jnp.where(x >= 0.0, 1.0 - tail, tail)
    return x * phi, phi + x * bell * 0.3989422804014327


def expert_kernel(chunk, first, info, inputs, grads, own_up, own_down, near, far, *refs):
    if not first:
        refs = refs[1:]
    hidden, gpre, result, given, buffer, grad_buffer, fetched, sems = refs
    size = own_up.shape[0]
    place = info[3] ^ chunk
    copies = [load(grads.at[place], grad_buffer, sems.at[0])]
    copies += [load(ref, fetched.at[i], sems.at[1 + i]) for i, ref in enumerate((near, far))]
    rows = inputs[...]
    copies[0].wait()
    grad = grad_buffer[...]
    total, forward = None, None
    for tile in range(4):
        if tile < 2:
            at = slice(tile * size, (tile + 1) * size)
            up, down = own_up[:, at], own_down[at, :]
        else:
            copies[tile - 1].wait()
            up, down = fetched[tile - 2, 0:size, :], fetched[tile - 2, size : 2 * size, :]
        at = slice(tile * size, (tile + 1) * size)
        preact = dot(rows, up, 1, 0)
        ghidden = dot(grad, down, 1, 1)
        act, slope = gelu_parts(preact)
        act = act.astype(BF)
        hidden[:, at] = act
        low = (ghidden * slope).astype(BF)
        gpre[:, at] = low
        part = dot(low, up, 1, 1)
        total = part if total is None else total + part
        part = dot(act, down, 1, 0)
        forward = part if forward is None else forward + part
    buffer[...] = forward.astype(BF)
    copy = load(buffer, given.at[place], sems.at[3])
    result[...] = total.astype(BF)
    copy.wait()


def expert(info, chunk, inputs, grads, weights, given=None):
    rows, model = inputs.shape
    tile = weights[0].shape[0]
    operands = [info, inputs, grads, *weights]
    in_specs = [smem(), vmem(), hbm(), vmem(), vmem(), hbm(), hbm()]
    if given is not None:
        operands.append(given)
        in_specs.append(hbm())
    return pl.pallas_call(
        functools.partial(expert_kernel, chunk, given is None),
        out_shape=[
            jax.ShapeDtypeStruct((rows, 4 * tile), BF),
            jax.ShapeDtypeStruct((rows, 4 * tile), BF),
            jax.ShapeDtypeStruct((rows, model), BF),
            jax.ShapeDtypeStruct(grads.shape, BF),
        ],
        in_specs=in_specs,
        out_specs=[vmem()] * 3 + [hbm()],
        scratch_shapes=[
            pltpu.VMEM((rows, model), BF),
            pltpu.VMEM((rows, model), BF),
            pltpu.VMEM((2, 2 * tile, model), BF),
            pltpu.SemaphoreType.DMA((4,)),
        ],
        input_output_aliases={} if given is None else {7: 3},
        compiler_params=params(20),
        cost_estimate=cost(32 * rows * model * tile, 16 * model * tile + 16 * rows * tile),
        name="expert",
    )(*operands)


GIVEN = (3, 3, 2)


def piece_at(theirs, other):
    return 2 * theirs + other, 4 + 2 * other + theirs


def given_at(piece):
    for which, number in enumerate(GIVEN):
        if piece < number:
            return which, piece
        piece -= number


def expert_weights_kernel(info, grads, *refs):
    n = CHUNKS
    inputs, hiddens, gpres = refs[:n], refs[n : 2 * n], refs[2 * n : 3 * n]
    stays, given, up_sum, down_sum = refs[3 * n], refs[3 * n + 1 : 3 * n + 4], *refs[3 * n + 4 :]
    size = up_sum.shape[0]
    sub = size // 2
    parity, row_half, here = info[0], info[1], info[3]
    mine = pl.ds(pl.multiple_of(parity * sub, sub), sub)
    gone = pl.ds(pl.multiple_of((1 - parity) * sub, sub), sub)
    for theirs in range(2):
        for other in range(2):
            tile = other ^ row_half
            if theirs:
                tile = 2 + (tile ^ parity)
            at = pl.ds(pl.multiple_of(tile * size, size), size)
            for index in range(n):
                up_part = dot(gpres[index][:, at], inputs[index][...], 0, 0)
                down_part = dot(hiddens[index][:, at], grads[here ^ index], 0, 0)
                if index == 0:
                    up_sum[...] = up_part
                    down_sum[...] = down_part
                else:
                    up_sum[...] += up_part
                    down_sum[...] += down_part
            for total, piece in zip((up_sum, down_sum), piece_at(theirs, other)):
                stays[piece] = total[mine, :].astype(BF)
                which, place = given_at(piece)
                given[which][place] = total[gone, :].astype(BF)


def expert_weights(info, inputs, grads, hiddens, gpres):
    rows, model = inputs[0].shape
    tile = hiddens[0].shape[1] // 4
    return pl.pallas_call(
        expert_weights_kernel,
        out_shape=[jax.ShapeDtypeStruct((m, tile // 2, model), BF) for m in (8, *GIVEN)],
        in_specs=[smem()] + [vmem()] * (1 + 3 * CHUNKS),
        out_specs=[vmem()] * 4,
        scratch_shapes=[pltpu.VMEM((tile, model), F32), pltpu.VMEM((tile, model), F32)],
        compiler_params=params(24),
        cost_estimate=cost(16 * CHUNKS * rows * model * tile, 32 * model * tile),
        name="expert_weights",
    )(info, grads, *inputs, *hiddens, *gpres)


def pieces_kernel(info, stays, first, second, third, kept, sent_up, sent_down):
    received = (first, second, third)
    for ref, pieces in ((kept, (0, 1, 4, 5)), (sent_up, (2, 3)), (sent_down, (6, 7))):
        for index, piece in enumerate(pieces):
            which, place = given_at(piece)
            total = stays[piece].astype(F32) + received[which][place].astype(F32)
            ref[index] = total.astype(BF)


def add_pieces(info, stays, *received):
    n, sub, model = stays.shape
    return pl.pallas_call(
        pieces_kernel,
        out_shape=[jax.ShapeDtypeStruct((m, sub, model), BF) for m in (4, 2, 2)],
        in_specs=[smem()] + [vmem()] * 4,
        out_specs=[vmem()] * 3,
        compiler_params=params(20),
        cost_estimate=cost(stays.size, 6 * stays.size),
        name="add_pieces",
    )(info, stays, *received)


def more_pieces_kernel(info, kept, got_up, got_down, up, down, sent_up, sent_down):
    for low, got, ref, sent in ((0, got_up, up, sent_up), (2, got_down, down, sent_down)):
        ref[...] = (kept[low].astype(F32) + got[0].astype(F32)).astype(BF)
        sent[...] = (kept[low + 1].astype(F32) + got[1].astype(F32)).astype(BF)


def more_pieces(info, kept, got_up, got_down):
    n, sub, model = kept.shape
    return pl.pallas_call(
        more_pieces_kernel,
        out_shape=[jax.ShapeDtypeStruct((sub, model), BF)] * 4,
        in_specs=[smem()] + [vmem()] * 3,
        out_specs=[vmem()] * 4,
        compiler_params=params(12),
        cost_estimate=cost(kept.size, 6 * kept.size),
        name="more_pieces",
    )(info, kept, got_up, got_down)


def last_pieces_kernel(info, up, down, got_up, got_down, grad_up, grad_down):
    grad_up[...] = jnp.transpose(up[...].astype(F32) + got_up[...].astype(F32))
    grad_down[...] = down[...].astype(F32) + got_down[...].astype(F32)


def last_pieces(info, up, down, got_up, got_down):
    sub, model = up.shape
    return pl.pallas_call(
        last_pieces_kernel,
        out_shape=[
            jax.ShapeDtypeStruct((model, sub), F32),
            jax.ShapeDtypeStruct((sub, model), F32),
        ],
        in_specs=[smem()] + [vmem()] * 4,
        out_specs=[vmem()] * 2,
        compiler_params=params(12),
        cost_estimate=cost(up.size, 16 * up.size),
        name="last_pieces",
    )(info, up, down, got_up, got_down)


def second_back_kernel(info, *refs):
    chunks = refs[:CHUNKS]
    middle, cot, gain, places, gmid, gvec = refs[CHUNKS:]
    grad = take_chunks(chunks, places[...])
    scaled, inverse = norm_parts(middle[...])
    total = cot[...].astype(F32) + norm_back(grad, scaled, inverse, gain[...])
    gmid[...] = total
    gvec[...] = jnp.zeros_like(gvec)
    gvec[0:1, :] = jnp.sum(grad * scaled, axis=0, keepdims=True)
    gvec[1:2, :] = jnp.sum(grad, axis=0, keepdims=True)


def second_back(info, chunks, middle, cotangent, gain, places):
    count, width = cotangent.shape
    return pl.pallas_call(
        second_back_kernel,
        out_shape=[
            jax.ShapeDtypeStruct((count, width), F32),
            jax.ShapeDtypeStruct((8, width), F32),
        ],
        in_specs=[smem()] + [vmem()] * (CHUNKS + 4),
        out_specs=[vmem()] * 2,
        compiler_params=params(16),
        cost_estimate=cost(4 * count * count * width, 16 * count * width),
        name="second_back",
    )(info, *chunks, middle, cotangent, gain, places)


def output_kernel(info, results, middle, gate, places, out):
    total = take_chunks([results], places[...])
    out[...] = (middle[...] + column(gate[...]) * total).astype(BF)


def output_call(info, results, middle, gate, places):
    return pl.pallas_call(
        output_kernel,
        out_shape=jax.ShapeDtypeStruct(middle.shape, BF),
        in_specs=[smem()] + [vmem()] * 4,
        out_specs=vmem(),
        compiler_params=params(16),
        cost_estimate=cost(4 * middle.shape[0] * middle.size, 8 * middle.size),
        name="output",
    )(info, results, middle, gate, places)


def load_probs(probs, buffer, sems):
    copies = []
    blk = buffer.shape[3]
    for index in range(BLOCKS):
        upto = (index + 1) * blk
        copy = pltpu.make_async_copy(
            probs.at[index, :, 0:upto, :], buffer.at[index, :, 0:upto, :], sems.at[index]
        )
        copy.start()
        copies.append(copy)
    return copies


def load(source, target, sem):
    copy = pltpu.make_async_copy(source, target, sem)
    copy.start()
    return copy


def back_values_kernel(info, own, oth, rows, outw, att, recip, probs, *refs):
    scaled_ref, inner_ref, gvalues, gweight, gbranch, gsum, buffer, row_buffer, sems = refs
    copies = load_probs(probs, buffer, sems)
    row_copy = load(rows, row_buffer, sems.at[BLOCKS])
    length = PACKED_LENGTH
    width = att.shape[0]
    blk = length // BLOCKS
    half = length // 2
    parity = info[0]
    for ref, place in ((own, parity), (oth, 1 - parity)):
        gbranch[pl.ds(pl.multiple_of(place * half, half), half), :] = ref[...].astype(BF)
    gatt = dot(outw[...], gbranch[...], 1, 1).astype(BF).astype(F32)
    for head in range(width // HEAD_DIM):
        at = slice(head * HEAD_DIM, (head + 1) * HEAD_DIM)
        scaled = (gatt[at] * recip[head : head + 1, :]).astype(BF)
        scaled_ref[at, :] = scaled
        inner_ref[head : head + 1, :] = jnp.sum(
            scaled.astype(F32) * att[at, :].astype(F32), axis=0, keepdims=True
        )
    gweight[width:, :] = dot(att[...], gbranch[...], 1, 0).astype(BF)
    gsum[...] = jnp.zeros_like(gsum)
    for index in range(BLOCKS):
        upto = (index + 1) * blk
        cols = slice(index * blk, upto)
        copies[index].wait()
        for head in range(width // HEAD_DIM):
            at = slice(head * HEAD_DIM, (head + 1) * HEAD_DIM)
            gsum[at, 0:upto] += dot(scaled_ref[at, cols], buffer[index, head, 0:upto, :], 1, 1)
    low = gsum[...].astype(BF)
    gvalues[...] = low
    row_copy.wait()
    gweight[0:width, :] = dot(low, row_buffer[...], 1, 0).astype(BF)


def back_values(info, own, oth, rows, outw, att, recip, probs):
    length, model = rows.shape
    width = att.shape[0]
    heads = width // HEAD_DIM
    shapes = [((width, length), BF), ((8, length), F32), ((width, length), BF)]
    shapes.append(((2 * width, model), BF))
    return pl.pallas_call(
        back_values_kernel,
        out_shape=[jax.ShapeDtypeStruct(s, d) for s, d in shapes],
        in_specs=[smem()] + [vmem()] * 2 + [hbm()] + [vmem()] * 3 + [hbm()],
        out_specs=[vmem()] * len(shapes),
        scratch_shapes=[
            pltpu.VMEM((length, model), BF),
            pltpu.VMEM((width, length), F32),
            pltpu.VMEM((BLOCKS, heads, length, length // BLOCKS), BF),
            pltpu.VMEM((length, model), BF),
            pltpu.SemaphoreType.DMA((BLOCKS + 1,)),
        ],
        compiler_params=params(56),
        cost_estimate=cost(
            8 * length * model * width + 4 * heads * length * length * HEAD_DIM,
            2 * heads * length * length + 10 * length * model,
        ),
        name="back_values",
    )(info, own, oth, rows, outw, att, recip, probs)


def back_keys_kernel(info, qkv, scaled, inner, gvalues, rows, probs, gweight, gqkv, *scratch):
    gsum, buffer, row_buffer, sems = scratch
    copies = load_probs(probs, buffer, sems)
    row_copy = load(rows, row_buffer, sems.at[BLOCKS])
    length = PACKED_LENGTH
    width = scaled.shape[0]
    blk = length // BLOCKS
    gsum[...] = jnp.zeros_like(gsum)
    for index in range(BLOCKS):
        upto = (index + 1) * blk
        cols = slice(index * blk, upto)
        copies[index].wait()
        for head in range(width // HEAD_DIM):
            at = head * HEAD_DIM
            here = slice(at, at + HEAD_DIM)
            kat = slice(width + at, width + at + HEAD_DIM)
            vat = slice(2 * width + at, 2 * width + at + HEAD_DIM)
            gprobs = dot(qkv[vat, 0:upto], scaled[here, cols], 0, 0)
            low = buffer[index, head, 0:upto, :].astype(F32)
            gscores = (low * (gprobs - inner[head : head + 1, cols])).astype(BF)
            gsum[here, 0:upto] += dot(qkv[here, cols], gscores, 1, 1)
            gqueries = dot(qkv[kat, 0:upto], gscores, 1, 0) * HEAD_DIM**-0.5
            gqkv[here, cols] = gqueries.astype(BF)
    gqkv[width : 2 * width, :] = gsum[...].astype(BF)
    gqkv[2 * width :, :] = gvalues[...]
    row_copy.wait()
    gweight[...] = dot(gqkv[0 : 2 * width, :], row_buffer[...], 1, 0).astype(BF)


def back_keys(info, qkv, scaled, inner, gvalues, rows, probs):
    length, model = rows.shape
    width = scaled.shape[0]
    heads = width // HEAD_DIM
    return pl.pallas_call(
        back_keys_kernel,
        out_shape=[
            jax.ShapeDtypeStruct((2 * width, model), BF),
            jax.ShapeDtypeStruct((3 * width, length), BF),
        ],
        in_specs=[smem()] + [vmem()] * 4 + [hbm()] * 2,
        out_specs=[vmem()] * 2,
        scratch_shapes=[
            pltpu.VMEM((width, length), F32),
            pltpu.VMEM((BLOCKS, heads, length, length // BLOCKS), BF),
            pltpu.VMEM((length, model), BF),
            pltpu.SemaphoreType.DMA((BLOCKS + 1,)),
        ],
        compiler_params=params(56),
        cost_estimate=cost(
            4 * length * model * width + 12 * heads * length * length * HEAD_DIM,
            2 * heads * length * length + 10 * length * model,
        ),
        name="back_keys",
    )(info, qkv, scaled, inner, gvalues, rows, probs)


def back_rows_kernel(info, gqkv_a, gqkv_b, weight_a, weight_b, kept, sent):
    half = kept.shape[0]
    parity = info[0]
    for ref, place in ((sent, 1 - parity), (kept, parity)):
        at = pl.ds(pl.multiple_of(place * half, half), half)
        total = dot(gqkv_a[:, at], weight_a[...], 0, 0) + dot(gqkv_b[:, at], weight_b[...], 0, 0)
        ref[...] = total.astype(ref.dtype)


def back_rows(info, gqkv_a, gqkv_b, weight_a, weight_b):
    length = gqkv_a.shape[1]
    model = weight_a.shape[1]
    return pl.pallas_call(
        back_rows_kernel,
        out_shape=[
            jax.ShapeDtypeStruct((length // 2, model), F32),
            jax.ShapeDtypeStruct((length // 2, model), BF),
        ],
        in_specs=[smem()] + [vmem()] * 4,
        out_specs=[vmem()] * 2,
        compiler_params=params(16),
        cost_estimate=cost(4 * length * model * gqkv_a.shape[0], 6 * length * model),
        name="back_rows",
    )(info, gqkv_a, gqkv_b, weight_a, weight_b)


def first_back_kernel(info, tokens, gmid, kept, received, gain, ginput, gvec):
    grad = kept[...] + received[...].astype(F32)
    scaled, inverse = norm_parts(tokens[...].astype(F32))
    ginput[...] = gmid[...] + norm_back(grad, scaled, inverse, gain[...])
    gvec[...] = jnp.zeros_like(gvec)
    gvec[0:1, :] = jnp.sum(grad * scaled, axis=0, keepdims=True)
    gvec[1:2, :] = jnp.sum(grad, axis=0, keepdims=True)


def first_back(info, tokens, gmid, kept, received, gain):
    count, width = tokens.shape
    return pl.pallas_call(
        first_back_kernel,
        out_shape=[
            jax.ShapeDtypeStruct((count, width), F32),
            jax.ShapeDtypeStruct((8, width), F32),
        ],
        in_specs=[smem()] + [vmem()] * 5,
        out_specs=[vmem()] * 2,
        compiler_params=params(16),
        cost_estimate=cost(20 * count * width, 16 * count * width),
        name="first_back",
    )(info, tokens, gmid, kept, received, gain)


def first_sum_kernel(info, mine, theirs, kept, sent):
    half = kept.shape[0]
    k = info[2]
    for ref, which in ((sent, 1 - k), (kept, k)):
        at = pl.ds(pl.multiple_of(which * half, half), half)
        ref[...] = (mine[at, :].astype(F32) + theirs[at, :].astype(F32)).astype(ref.dtype)


def first_sum(info, mine, theirs):
    rows, model = mine.shape
    return pl.pallas_call(
        first_sum_kernel,
        out_shape=[
            jax.ShapeDtypeStruct((rows // 2, model), F32),
            jax.ShapeDtypeStruct((rows // 2, model), BF),
        ],
        in_specs=[smem()] + [vmem()] * 2,
        out_specs=[vmem()] * 2,
        compiler_params=params(16),
        cost_estimate=cost(rows * model, 7 * rows * model),
        name="first_sum",
    )(info, mine, theirs)


def second_sum_kernel(info, kept_vo, got_vo, kept_qk, got_qk, out):
    pieces, rows = out.shape[0], out.shape[1] // 2
    for index in range(pieces):
        at = slice(index * rows, (index + 1) * rows)
        out[index, 0:rows] = (kept_vo[at, :] + got_vo[at, :].astype(F32)).astype(BF)
        out[index, rows:] = (kept_qk[at, :] + got_qk[at, :].astype(F32)).astype(BF)


def second_sum(info, pieces, *operands):
    rows, model = operands[0].shape
    return pl.pallas_call(
        second_sum_kernel,
        out_shape=jax.ShapeDtypeStruct((pieces, 2 * rows // pieces, model), BF),
        in_specs=[smem()] + [vmem()] * 4,
        out_specs=vmem(),
        compiler_params=params(8),
        cost_estimate=cost(rows * model, 16 * rows * model),
        name="second_sum",
    )(info, *operands)


def third_sum_kernel(info, blocks, out):
    total = None
    for index in range(out.shape[0]):
        block = blocks[index].astype(F32)
        total = block if total is None else total + block
    total = total.astype(BF)
    for index in range(out.shape[0]):
        out[index] = total


def third_sum(info, blocks):
    return pl.pallas_call(
        third_sum_kernel,
        out_shape=jax.ShapeDtypeStruct(blocks.shape, BF),
        in_specs=[smem(), vmem()],
        out_specs=vmem(),
        compiler_params=params(8),
        cost_estimate=cost(blocks.size, 4 * blocks.size),
        name="third_sum",
    )(info, blocks)


def last_kernel(info, mine, theirs, qkv, out):
    pieces, rows = mine.shape[0], mine.shape[1] // 2
    width = out.shape[0]
    k = info[2]

    def write(even, odd):
        for index in range(pieces):
            for start, target, source, half in (
                (0, qkv, even, 1),
                (width, qkv, odd, 1),
                (2 * width, qkv, even, 0),
                (0, out, odd, 0),
            ):
                at = slice(start + index * rows, start + (index + 1) * rows)
                target[at, :] = source[index, half * rows : (half + 1) * rows].astype(F32)

    @pl.when(k == 0)
    def even():
        write(mine, theirs)

    @pl.when(k != 0)
    def odd():
        write(theirs, mine)


def last(info, mine, theirs):
    pieces, rows, model = mine.shape
    width = pieces * rows // 2
    return pl.pallas_call(
        last_kernel,
        out_shape=[
            jax.ShapeDtypeStruct((3 * width, model), F32),
            jax.ShapeDtypeStruct((width, model), F32),
        ],
        in_specs=[smem()] + [vmem()] * 2,
        out_specs=[vmem()] * 2,
        compiler_params=params(8),
        cost_estimate=cost(width * model, 24 * width * model),
        name="last",
    )(info, mine, theirs)


def after(values, *others):
    return lax.optimization_barrier((values, *others))[0]


def swap(values, axis, bit):
    pairs = [(i, i ^ bit) for i in range(lax.axis_size(axis))]
    return lax.ppermute(values, axis, pairs)


def exchange(values, count):
    groups = [[2 * e + k for e in range(count)] for k in range(2)]
    shaped = values.reshape(count, -1, values.shape[1])
    moved = lax.all_to_all(shaped, "dp", 0, 0, tiled=True, axis_index_groups=groups)
    return moved.reshape(values.shape)


def exchange_chunks(chunks, count):
    moved = exchange(jnp.concatenate(chunks, axis=0), count)
    size = chunks[0].shape[0]
    return [moved[i * size : (i + 1) * size] for i in range(len(chunks))]


def local(
    tokens,
    first_gain,
    first_bias,
    qkv_weight,
    out_weight,
    second_gain,
    expert_norm_bias,
    up_weight,
    down_weight,
    gate_value,
    expert_ids,
    slot_index,
    segment_ids,
    cotangent,
):
    count, model = tokens.shape
    width = qkv_weight.shape[2]
    tp = lax.axis_index("tp")
    dp = lax.axis_index("dp")
    parity = tp % 2
    row_half = tp // 2 % 2
    k = dp % 2
    experts = lax.axis_size("dp") // 2
    capacity = 2 * count // experts
    paired = experts == CHUNKS
    here = dp // 2 if paired else 0 * dp
    info = jnp.stack([parity, row_half, k, here]).astype(jnp.int32)
    vector = lambda v: v.reshape(1, -1)
    gain, bias = vector(first_gain), vector(first_bias)

    state = [info]

    def run(call, *operands):
        outs = call(state[0], *operands)
        state[0] = after(info, outs[-1] if isinstance(outs, (list, tuple)) else outs)
        return outs

    other_tokens = swap(tokens, "tp", 1)
    other_segments = swap(segment_ids, "tp", 1)
    weight_a = jnp.transpose(qkv_weight, (1, 2, 0)).reshape(3 * width, model)
    weight_b = swap(weight_a, "tp", 2)
    up, down = up_weight[0], down_weight[0]
    near = swap(run(give, up, down), "dp", 1)
    gate = vector(gate_value)
    slots = vector(expert_ids * capacity + slot_index)
    sent_grads = run(grad_dispatch, cotangent, gate, slots)
    grads = exchange(sent_grads, experts).reshape(CHUNKS, -1, model)

    segments = (vector(segment_ids), vector(other_segments))
    rows, att_a, probs_a, qkv_a, recip_a = run(
        attend, True, tokens, other_tokens, gain, bias, weight_a, *segments
    )
    out_b = swap(after(out_weight, recip_a), "tp", 2)
    att_b, probs_b, qkv_b, recip_b = run(
        attend, False, rows, vector(other_segments), gain, bias, weight_b, *segments
    )
    kept, sent = run(project, att_a, att_b, out_weight, out_b)
    received = swap(sent, "tp", 1)
    places = vector((expert_ids ^ here) * capacity + slot_index)
    middle, *sent_rows = run(
        middle_call, tokens, kept, received, vector(second_gain), vector(expert_norm_bias), places
    )

    if paired:
        first, second = lax.optimization_barrier(
            (swap(sent_rows[1], "dp", 2), swap(sent_rows[2], "dp", 4))
        )
        third = swap(after(sent_rows[3], second), "dp", 6)
        inputs = [sent_rows[0], first, second, third]
    else:
        inputs = exchange_chunks(sent_rows, experts)
    far = swap(after(near, inputs[1], grads), "tp", 1)
    weights = (up, down, near, far)
    hiddens, gpres, backs = [[None] * CHUNKS for unused in range(3)]
    results = None
    for index in (*range(1, CHUNKS), 0):
        hiddens[index], gpres[index], backs[index], results = run(
            expert, index, inputs[index], grads, weights, results
        )
    if paired:
        returned = [backs[0]] + [swap(backs[s], "dp", 2 * s) for s in range(1, CHUNKS)]
    else:
        returned = exchange_chunks(backs, experts)
    if paired:
        inputs[0], returned[1] = lax.optimization_barrier((inputs[0], returned[1]))
    stays, *leaves = run(expert_weights, inputs, grads, hiddens, gpres)
    leaves = [swap(leaf, "tp", 1) for leaf in leaves]
    gmid, gvec_two = run(
        second_back, returned, middle, cotangent, vector(second_gain), places
    )
    other_gmid = swap(gmid, "tp", 1)
    outs = exchange(after(results, gmid).reshape(-1, model), experts)

    scaled_b, inner_b, gvalues_b, gvo_b = run(
        back_values, gmid, other_gmid, rows, out_b, att_b, recip_b, probs_b
    )
    theirs_vo = swap(gvo_b, "tp", 2)
    scaled_a, inner_a, gvalues_a, gvo_a = run(
        back_values, gmid, other_gmid, rows, out_weight, att_a, recip_a, probs_a
    )
    kept_pieces, sent_up, sent_down = run(add_pieces, stays, *leaves)
    got_up = swap(sent_up, "dp", 1)
    gqk_b, gqkv_b = run(back_keys, qkv_b, scaled_b, inner_b, gvalues_b, rows, probs_b)
    theirs_qk = swap(gqk_b, "tp", 2)
    vo_kept, vo_sent = run(first_sum, gvo_a, theirs_vo)
    vo_received = swap(vo_sent, "dp", 1)
    gqk_a, gqkv_a = run(back_keys, qkv_a, scaled_a, inner_a, gvalues_a, rows, probs_a)

    got_down = swap(after(sent_down, gqk_a), "tp", 2)

    qk_kept, qk_sent = run(first_sum, gqk_a, theirs_qk)
    qk_received = swap(qk_sent, "dp", 1)
    gkept, gsent = run(back_rows, gqkv_a, gqkv_b, weight_a, weight_b)
    greceived = swap(gsent, "tp", 1)
    pieces = experts if paired else 1
    half = run(
        second_sum, pieces, vo_kept, after(vo_received, outs), qk_kept, qk_received
    )
    if not paired:
        half = half.reshape(2, experts, -1, model).transpose(1, 0, 2, 3)
    blocks = exchange(half.reshape(2 * width, model), experts).reshape(experts, -1, model)
    up_kept, down_kept, sent_up, sent_down = run(more_pieces, kept_pieces, got_up, got_down)
    got_up, got_down = swap(sent_up, "tp", 2), swap(sent_down, "dp", 1)
    grad_input, gvec_one = run(first_back, tokens, gmid, gkept, greceived, gain)
    vectors = gvec_one + jnp.roll(gvec_two, 2, axis=0)
    vectors = vectors + swap(vectors, "tp", 1)
    vectors = vectors + swap(vectors, "tp", 2)
    vectors, blocks = lax.optimization_barrier((vectors, blocks))
    total = run(third_sum, blocks)
    full = exchange(total.reshape(2 * width, model), experts)
    vectors = vectors + swap(vectors, "dp", 1)
    output = run(output_call, outs, middle, gate, slots)
    bit = 2
    while bit < lax.axis_size("dp"):
        vectors = vectors + swap(vectors, "dp", bit)
        bit *= 2
    vectors, full = lax.optimization_barrier((vectors, full))
    other = swap(full, "dp", 1)
    grad_up, grad_down = run(last_pieces, up_kept, down_kept, got_up, got_down)
    if not paired:
        full, other = [
            v.reshape(experts, 2, -1, model).transpose(1, 0, 2, 3) for v in (full, other)
        ]
    shape = (pieces, -1, model)
    grad_qkv, grad_out = run(last, full.reshape(shape), other.reshape(shape))
    grad_qkv = jnp.transpose(grad_qkv.reshape(3, width, model), (2, 0, 1))
    vec_one, vec_two = vectors[0:2], vectors[2:4]
    return (
        output,
        grad_input,
        vec_one[0],
        vec_one[1],
        grad_qkv,
        grad_out,
        vec_two[0],
        vec_two[1],
        grad_up[None],
        grad_down[None],
    )


def solution(mesh):
    placed = (
        P(("dp", "tp"), None),
        P(),
        P(),
        P(None, None, "tp"),
        P("tp", None),
        P(),
        P(),
        P("dp", None, None),
        P("dp", None, None),
        P(("dp", "tp")),
        P(("dp", "tp")),
        P(("dp", "tp")),
        P(("dp", "tp")),
        P(("dp", "tp"), None),
    )
    return jax.shard_map(
        local,
        mesh=mesh,
        in_specs=placed,
        out_specs=(
            P(("dp", "tp"), None),
            P(("dp", "tp"), None),
            P(),
            P(),
            P(None, None, "tp"),
            P("tp", None),
            P(),
            P(),
            P("dp", None, "tp"),
            P("dp", "tp", None),
        ),
        check_vma=False,
    )
```

```python
import functools

import jax
import jax.numpy as jnp
from jax import lax
from jax.experimental import pallas as pl
from jax.experimental.pallas import tpu as pltpu
from jax.sharding import PartitionSpec as P

HEAD_DIM = 64
PACKED_LENGTH = 1024
EPSILON = 1e-05
BF = jnp.bfloat16
F32 = jnp.float32
MASKED = -1e30
CHUNKS = 4


def dot(a, b, ca, cb):
    return lax.dot_general(a, b, (((ca,), (cb,)), ((), ())), preferred_element_type=F32)


def params(mib, **kw):
    return pltpu.CompilerParams(vmem_limit_bytes=mib * 1024 * 1024, **kw)


def cost(flops, nbytes):
    return pl.CostEstimate(flops=int(flops) // 64, bytes_accessed=int(nbytes) // 64, transcendentals=0)


def vmem():
    return pl.BlockSpec(memory_space=pltpu.VMEM)


def hbm():
    return pl.BlockSpec(memory_space=pltpu.HBM)


def smem():
    return pl.BlockSpec(memory_space=pltpu.SMEM)


def norm_parts(values):
    centre = jnp.mean(values, axis=-1, keepdims=True)
    shifted = values - centre
    inverse = lax.rsqrt(jnp.mean(shifted * shifted, axis=-1, keepdims=True) + EPSILON)
    return shifted * inverse, inverse


def norm_back(grad_normed, scaled, inverse, gain):
    grad_scaled = grad_normed * gain
    first = jnp.mean(grad_scaled, axis=-1, keepdims=True)
    second = jnp.mean(grad_scaled * scaled, axis=-1, keepdims=True)
    return inverse * (grad_scaled - first - scaled * second)


def column(row):
    return jnp.transpose(jnp.broadcast_to(row, (8, row.shape[1])))[:, 0:1]


def onehot(places, slots):
    rows = lax.broadcasted_iota(jnp.int32, (slots, places.shape[1]), 0)
    return jnp.where(rows == places, 1.0, 0.0).astype(BF)


def put_chunks(rows, places, outs):
    size = outs[0].shape[0]
    table = onehot(places, size * len(outs))
    for index, out in enumerate(outs):
        out[...] = dot(table[index * size : (index + 1) * size], rows, 1, 0).astype(BF)


def take_chunks(chunks, places):
    size = chunks[0].shape[0]
    table = onehot(places, size * len(chunks))
    total = None
    for index, chunk in enumerate(chunks):
        part = dot(table[index * size : (index + 1) * size], chunk[...], 0, 0)
        total = part if total is None else total + part
    return total


def grad_dispatch_kernel(info, cot_ref, gate_ref, places_ref, out):
    rows = (column(gate_ref[...]) * cot_ref[...].astype(F32)).astype(BF)
    put_chunks(rows, places_ref[...], [out])


def grad_dispatch(info, cotangent, gate, places):
    tokens, width = cotangent.shape
    return pl.pallas_call(
        grad_dispatch_kernel,
        out_shape=jax.ShapeDtypeStruct((2 * tokens, width), BF),
        in_specs=[smem()] + [vmem()] * 3,
        out_specs=vmem(),
        compiler_params=params(12),
        cost_estimate=cost(4 * tokens * tokens * width, 6 * tokens * width),
        name="grad_dispatch",
    )(info, cotangent, gate, places)


PAD = 64


def give_kernel(info, up, down, given, buffer, sems):
    tile = up.shape[0]
    at = pl.ds(pl.multiple_of(info[0] * tile, tile), tile)
    first, second = slice(0, tile), slice(tile, 2 * tile)
    loads = [
        pltpu.make_async_copy(up.at[:, at], buffer.at[first, :], sems.at[0]),
        pltpu.make_async_copy(down.at[at, :], buffer.at[second, :], sems.at[1]),
    ]
    for load in loads:
        load.start()
    stores = []
    for index, part in enumerate((first, second)):
        loads[index].wait()
        store = pltpu.make_async_copy(buffer.at[part, :], given.at[part, :], sems.at[2 + index])
        store.start()
        stores.append(store)
    for store in stores:
        store.wait()


def give(info, up, down):
    hbm = pl.BlockSpec(memory_space=pltpu.HBM)
    return pl.pallas_call(
        give_kernel,
        out_shape=jax.ShapeDtypeStruct((up.shape[1] + PAD, up.shape[0]), BF),
        in_specs=[smem(), hbm, hbm],
        out_specs=hbm,
        scratch_shapes=[
            pltpu.VMEM((up.shape[1], up.shape[0]), BF),
            pltpu.SemaphoreType.DMA((4,)),
        ],
        compiler_params=params(60),
        cost_estimate=cost(1, 4 * up.size),
        name="give",
    )(info, up, down)


BLOCKS = 2


def attend_kernel(first, heads, info, own, oth, gain, bias, weight, seg_own, seg_oth, *refs):
    parity = info[0]
    half = PACKED_LENGTH // 2
    if first:
        rows_out, att, probs, qkv, recip, segr, mask, buffer, sems, rows = refs
        for ref, place in ((own, parity), (oth, 1 - parity)):
            scaled, unused = norm_parts(ref[...].astype(F32))
            normed = (scaled * gain[...] + bias[...]).astype(BF)
            rows[pl.ds(pl.multiple_of(place * half, half), half), :] = normed
        rows_out[...] = rows[...]
    else:
        att, probs, qkv, recip, segr, mask, buffer, sems = refs
        rows = own
    for ref, place in ((seg_own, parity), (seg_oth, 1 - parity)):
        at = pl.ds(pl.multiple_of(place * half, half), half)
        segr[:, at] = jnp.broadcast_to(ref[...].astype(F32), (8, half))
    segc = jnp.transpose(segr[...])[:, 0:1]
    width = heads * HEAD_DIM
    blk = att.shape[1] // BLOCKS
    projected = dot(weight[...], rows[...], 1, 1).astype(BF)
    qkv[...] = projected
    qkv[0:width, :] = projected[0:width] * jnp.asarray(HEAD_DIM**-0.5, BF)
    copies = []
    for index in reversed(range(BLOCKS)):
        upto = (index + 1) * blk
        cols = slice(index * blk, upto)
        keypos = lax.broadcasted_iota(jnp.int32, (upto, blk), 0)
        querypos = lax.broadcasted_iota(jnp.int32, (upto, blk), 1) + index * blk
        allowed = (segc[0:upto, :] == segr[0:1, cols]) & (keypos <= querypos)
        mask[0:upto, :] = jnp.where(allowed, 0.0, MASKED)
        for head in range(heads):
            at = head * HEAD_DIM
            query = qkv[at : at + HEAD_DIM, cols]
            keys = qkv[width + at : width + at + HEAD_DIM, 0:upto]
            values = qkv[2 * width + at : 2 * width + at + HEAD_DIM, 0:upto]
            scores = dot(keys, query, 0, 0) + mask[0:upto, :]
            highest = jnp.max(scores, axis=0, keepdims=True)
            weights = jnp.exp(scores - highest)
            inverse = 1.0 / jnp.sum(weights, axis=0, keepdims=True)
            low = weights.astype(BF)
            buffer[index, head, 0:upto, :] = low
            result = dot(values, low, 1, 0) * inverse
            att[at : at + HEAD_DIM, cols] = result.astype(BF)
            recip[head : head + 1, cols] = inverse
        copy = pltpu.make_async_copy(
            buffer.at[index, :, 0:upto, :], probs.at[index, :, 0:upto, :], sems.at[index]
        )
        copy.start()
        copies.append(copy)
    for copy in copies:
        copy.wait()


def attend(info, first, own, oth, gain, bias, weight, seg_own, seg_oth):
    length = PACKED_LENGTH
    model = own.shape[1]
    width = weight.shape[0] // 3
    heads = width // HEAD_DIM
    blk = length // BLOCKS
    outs = [
        jax.ShapeDtypeStruct((width, length), BF),
        jax.ShapeDtypeStruct((BLOCKS, heads, length, blk), BF),
        jax.ShapeDtypeStruct((3 * width, length), BF),
        jax.ShapeDtypeStruct((8, length), F32),
    ]
    out_specs = [vmem(), pl.BlockSpec(memory_space=pltpu.HBM), vmem(), vmem()]
    scratch = [
        pltpu.VMEM((8, length), F32),
        pltpu.VMEM((length, blk), F32),
        pltpu.VMEM((BLOCKS, heads, length, blk), BF),
        pltpu.SemaphoreType.DMA((BLOCKS,)),
    ]
    if first:
        outs = [jax.ShapeDtypeStruct((length, model), BF)] + outs
        out_specs = [vmem()] + out_specs
        scratch = scratch + [pltpu.VMEM((length, model), BF)]
    operands = (own, oth, gain, bias, weight, seg_own, seg_oth)
    return pl.pallas_call(
        functools.partial(attend_kernel, first, heads),
        out_shape=outs,
        in_specs=[smem()] + [vmem()] * len(operands),
        out_specs=out_specs,
        scratch_shapes=scratch,
        compiler_params=params(56),
        cost_estimate=cost(
            6 * length * model * width + 8 * heads * length * length * HEAD_DIM,
            2 * heads * length * length + 6 * length * model,
        ),
        name="attend",
    )(info, *operands)


def project_kernel(info, att_a, att_b, out_a, out_b, kept, sent):
    half = kept.shape[0]
    parity = info[0]
    for ref, place in ((sent, 1 - parity), (kept, parity)):
        cols = pl.ds(pl.multiple_of(place * half, half), half)
        total = dot(att_a[:, cols], out_a[...], 0, 0) + dot(att_b[:, cols], out_b[...], 0, 0)
        ref[...] = total.astype(ref.dtype)


def project(info, att_a, att_b, out_a, out_b):
    width, length = att_a.shape
    model = out_a.shape[1]
    return pl.pallas_call(
        project_kernel,
        out_shape=[
            jax.ShapeDtypeStruct((length // 2, model), F32),
            jax.ShapeDtypeStruct((length // 2, model), F32),
        ],
        in_specs=[smem()] + [vmem()] * 4,
        out_specs=[vmem()] * 2,
        compiler_params=params(12),
        cost_estimate=cost(4 * length * model * width, 6 * length * model),
        name="project",
    )(info, att_a, att_b, out_a, out_b)


def middle_kernel(info, tokens, kept, received, gain, bias, places, middle, *outs):
    values = tokens[...].astype(F32) + (kept[...] + received[...].astype(F32))
    middle[...] = values
    scaled, unused = norm_parts(values)
    normed = (scaled * gain[...] + bias[...]).astype(BF)
    put_chunks(normed, places[...], outs)


def middle_call(info, tokens, kept, received, gain, bias, places):
    count, width = tokens.shape
    size = 2 * count // CHUNKS
    return pl.pallas_call(
        middle_kernel,
        out_shape=[jax.ShapeDtypeStruct((count, width), F32)]
        + [jax.ShapeDtypeStruct((size, width), BF)] * CHUNKS,
        in_specs=[smem()] + [vmem()] * 6,
        out_specs=[vmem()] * (1 + CHUNKS),
        compiler_params=params(16),
        cost_estimate=cost(4 * count * count * width, 14 * count * width),
        name="middle",
    )(info, tokens, kept, received, gain, bias, places)


def gelu_parts(x):
    z = jnp.abs(x) * (0.5**0.5)
    t = 1.0 / (1.0 + 0.3275911 * z)
    poly = t * (
        0.254829592
        + t * (-0.284496736 + t * (1.421413741 + t * (-1.453152027 + t * 1.061405429)))
    )
    bell = jnp.exp(-0.5 * x * x)
    tail = 0.5 * poly * bell
    phi = jnp.where(x >= 0.0, 1.0 - tail, tail)
    return x * phi, phi + x * bell * 0.3989422804014327


def expert_kernel(chunk, first, info, inputs, grads, own_up, own_down, near, far, *refs):
    if not first:
        refs = refs[1:]
    hidden, gpre, result, given, buffer, grad_buffer, fetched, sems = refs
    size = own_up.shape[0]
    place = info[3] ^ chunk
    copies = [load(grads.at[place], grad_buffer, sems.at[0])]
    copies += [load(ref.at[0 : 2 * size, :], fetched.at[i], sems.at[1 + i]) for i, ref in enumerate((near, far))]
    rows = inputs[...]
    copies[0].wait()
    grad = grad_buffer[...]
    total, forward = None, None
    for tile in range(4):
        if tile < 2:
            at = slice(tile * size, (tile + 1) * size)
            up, down = own_up[:, at], own_down[at, :]
        else:
            copies[tile - 1].wait()
            up, down = fetched[tile - 2, 0:size, :], fetched[tile - 2, size : 2 * size, :]
        at = slice(tile * size, (tile + 1) * size)
        preact = dot(rows, up, 1, 0)
        ghidden = dot(grad, down, 1, 1)
        act, slope = gelu_parts(preact)
        act = act.astype(BF)
        hidden[:, at] = act
        low = (ghidden * slope).astype(BF)
        gpre[:, at] = low
        part = dot(low, up, 1, 1)
        total = part if total is None else total + part
        part = dot(act, down, 1, 0)
        forward = part if forward is None else forward + part
    buffer[...] = forward.astype(BF)
    copy = load(buffer, given.at[place], sems.at[3])
    result[...] = total.astype(BF)
    copy.wait()


def expert(info, chunk, inputs, grads, weights, given=None):
    rows, model = inputs.shape
    tile = weights[0].shape[0]
    operands = [info, inputs, grads, *weights]
    in_specs = [smem(), vmem(), hbm(), vmem(), vmem(), hbm(), hbm()]
    if given is not None:
        operands.append(given)
        in_specs.append(hbm())
    return pl.pallas_call(
        functools.partial(expert_kernel, chunk, given is None),
        out_shape=[
            jax.ShapeDtypeStruct((rows, 4 * tile), BF),
            jax.ShapeDtypeStruct((rows, 4 * tile), BF),
            jax.ShapeDtypeStruct((rows, model), BF),
            jax.ShapeDtypeStruct(grads.shape, BF),
        ],
        in_specs=in_specs,
        out_specs=[vmem()] * 3 + [hbm()],
        scratch_shapes=[
            pltpu.VMEM((rows, model), BF),
            pltpu.VMEM((rows, model), BF),
            pltpu.VMEM((2, 2 * tile, model), BF),
            pltpu.SemaphoreType.DMA((4,)),
        ],
        input_output_aliases={} if given is None else {7: 3},
        compiler_params=params(20),
        cost_estimate=cost(32 * rows * model * tile, 16 * model * tile + 16 * rows * tile),
        name="expert",
    )(*operands)


GIVEN = (3, 3, 2)


def piece_at(theirs, other):
    return 2 * theirs + other, 4 + 2 * other + theirs


def given_at(piece):
    for which, number in enumerate(GIVEN):
        if piece < number:
            return which, piece
        piece -= number


def expert_weights_kernel(info, grads, *refs):
    n = CHUNKS
    inputs, hiddens, gpres = refs[:n], refs[n : 2 * n], refs[2 * n : 3 * n]
    stays, given, up_sum, down_sum = refs[3 * n], refs[3 * n + 1 : 3 * n + 4], *refs[3 * n + 4 :]
    size = up_sum.shape[0]
    sub = size // 2
    parity, row_half, here = info[0], info[1], info[3]
    mine = pl.ds(pl.multiple_of(parity * sub, sub), sub)
    gone = pl.ds(pl.multiple_of((1 - parity) * sub, sub), sub)
    for theirs in range(2):
        for other in range(2):
            tile = other ^ row_half
            if theirs:
                tile = 2 + (tile ^ parity)
            at = pl.ds(pl.multiple_of(tile * size, size), size)
            for index in range(n):
                up_part = dot(gpres[index][:, at], inputs[index][...], 0, 0)
                down_part = dot(hiddens[index][:, at], grads[here ^ index], 0, 0)
                if index == 0:
                    up_sum[...] = up_part
                    down_sum[...] = down_part
                else:
                    up_sum[...] += up_part
                    down_sum[...] += down_part
            for total, piece in zip((up_sum, down_sum), piece_at(theirs, other)):
                stays[piece] = total[mine, :].astype(BF)
                which, place = given_at(piece)
                given[which][place] = total[gone, :].astype(BF)


def expert_weights(info, inputs, grads, hiddens, gpres):
    rows, model = inputs[0].shape
    tile = hiddens[0].shape[1] // 4
    return pl.pallas_call(
        expert_weights_kernel,
        out_shape=[jax.ShapeDtypeStruct((m, tile // 2, model), BF) for m in (8, *GIVEN)],
        in_specs=[smem()] + [vmem()] * (1 + 3 * CHUNKS),
        out_specs=[vmem()] * 4,
        scratch_shapes=[pltpu.VMEM((tile, model), F32), pltpu.VMEM((tile, model), F32)],
        compiler_params=params(24),
        cost_estimate=cost(16 * CHUNKS * rows * model * tile, 32 * model * tile),
        name="expert_weights",
    )(info, grads, *inputs, *hiddens, *gpres)


def pieces_kernel(info, stays, first, second, third, kept, sent_one, sent_two, sent_down):
    received = (first, second, third)
    for ref, pieces in (
        (kept, (0, 1, 4, 5)),
        (sent_one, (2,)),
        (sent_two, (3,)),
        (sent_down, (6, 7)),
    ):
        for index, piece in enumerate(pieces):
            which, place = given_at(piece)
            total = stays[piece].astype(F32) + received[which][place].astype(F32)
            ref[index] = total.astype(BF)


def add_pieces(info, stays, *received):
    n, sub, model = stays.shape
    return pl.pallas_call(
        pieces_kernel,
        out_shape=[jax.ShapeDtypeStruct((m, sub, model), BF) for m in (4, 1, 1, 2)],
        in_specs=[smem()] + [vmem()] * 4,
        out_specs=[vmem()] * 4,
        compiler_params=params(20),
        cost_estimate=cost(stays.size, 6 * stays.size),
        name="add_pieces",
    )(info, stays, *received)


def more_pieces_kernel(info, kept, one, two, got_down, up, down, sent_up, sent_down):
    for index, got, ref in (
        (0, one.at[0], up),
        (1, two.at[0], sent_up),
        (2, got_down.at[0], down),
        (3, got_down.at[1], sent_down),
    ):
        ref[...] = (kept[index].astype(F32) + got[...].astype(F32)).astype(BF)


def more_pieces(info, kept, *got):
    n, sub, model = kept.shape
    return pl.pallas_call(
        more_pieces_kernel,
        out_shape=[jax.ShapeDtypeStruct((sub, model), BF)] * 4,
        in_specs=[smem()] + [vmem()] * 4,
        out_specs=[vmem()] * 4,
        compiler_params=params(60),
        cost_estimate=cost(kept.size, 6 * kept.size),
        name="more_pieces",
    )(info, kept, *got)


def last_pieces_kernel(info, up, down, got_up, got_down, grad_up, grad_down):
    grad_up[...] = jnp.transpose(up[...].astype(F32) + got_up[...].astype(F32))
    grad_down[...] = down[...].astype(F32) + got_down[...].astype(F32)


def last_pieces(info, up, down, got_up, got_down):
    sub, model = up.shape
    return pl.pallas_call(
        last_pieces_kernel,
        out_shape=[
            jax.ShapeDtypeStruct((model, sub), F32),
            jax.ShapeDtypeStruct((sub, model), F32),
        ],
        in_specs=[smem()] + [vmem()] * 4,
        out_specs=[vmem()] * 2,
        compiler_params=params(60),
        cost_estimate=cost(up.size, 16 * up.size),
        name="last_pieces",
    )(info, up, down, got_up, got_down)


def second_back_kernel(info, *refs):
    chunks = refs[:CHUNKS]
    middle, cot, gain, places, gmid, gvec = refs[CHUNKS:]
    grad = take_chunks(chunks, places[...])
    scaled, inverse = norm_parts(middle[...])
    total = cot[...].astype(F32) + norm_back(grad, scaled, inverse, gain[...])
    gmid[...] = total
    gvec[...] = jnp.zeros_like(gvec)
    gvec[0:1, :] = jnp.sum(grad * scaled, axis=0, keepdims=True)
    gvec[1:2, :] = jnp.sum(grad, axis=0, keepdims=True)


def second_back(info, chunks, middle, cotangent, gain, places):
    count, width = cotangent.shape
    return pl.pallas_call(
        second_back_kernel,
        out_shape=[
            jax.ShapeDtypeStruct((count, width), F32),
            jax.ShapeDtypeStruct((8, width), F32),
        ],
        in_specs=[smem()] + [vmem()] * (CHUNKS + 4),
        out_specs=[vmem()] * 2,
        compiler_params=params(16),
        cost_estimate=cost(4 * count * count * width, 16 * count * width),
        name="second_back",
    )(info, *chunks, middle, cotangent, gain, places)


def output_kernel(info, results, middle, gate, places, out):
    total = take_chunks([results], places[...])
    out[...] = (middle[...] + column(gate[...]) * total).astype(BF)


def output_call(info, results, middle, gate, places):
    return pl.pallas_call(
        output_kernel,
        out_shape=jax.ShapeDtypeStruct(middle.shape, BF),
        in_specs=[smem()] + [vmem()] * 4,
        out_specs=vmem(),
        compiler_params=params(60),
        cost_estimate=cost(4 * middle.shape[0] * middle.size, 8 * middle.size),
        name="output",
    )(info, results, middle, gate, places)


def load_probs(probs, buffer, sems):
    copies = []
    blk = buffer.shape[3]
    for index in range(BLOCKS):
        upto = (index + 1) * blk
        copy = pltpu.make_async_copy(
            probs.at[index, :, 0:upto, :], buffer.at[index, :, 0:upto, :], sems.at[index]
        )
        copy.start()
        copies.append(copy)
    return copies


def load(source, target, sem):
    copy = pltpu.make_async_copy(source, target, sem)
    copy.start()
    return copy


def back_values_kernel(info, own, oth, rows, *refs):
    outws, atts, recips, probs = refs[0:2], refs[2:4], refs[4:6], refs[6:8]
    outs = refs[8:16]
    gbranch, gsum, row_buffer, sems = refs[16:18] + refs[20:22]
    buffers = refs[18:20]
    copies = [load_probs(probs[g], buffers[g], sems.at[g]) for g in range(2)]
    row_copy = load(rows, row_buffer, sems.at[0, BLOCKS])
    length = PACKED_LENGTH
    width = atts[0].shape[0]
    blk = length // BLOCKS
    half = length // 2
    parity = info[0]
    for ref, place in ((own, parity), (oth, 1 - parity)):
        gbranch[pl.ds(pl.multiple_of(place * half, half), half), :] = ref[...].astype(BF)
    for g in range(2):
        scaled_ref, inner_ref, gvalues, gweight = outs[4 * g : 4 * g + 4]
        att, recip, buffer = atts[g], recips[g], buffers[g]
        gatt = dot(outws[g][...], gbranch[...], 1, 1).astype(BF).astype(F32)
        for head in range(width // HEAD_DIM):
            at = slice(head * HEAD_DIM, (head + 1) * HEAD_DIM)
            scaled = (gatt[at] * recip[head : head + 1, :]).astype(BF)
            scaled_ref[at, :] = scaled
            inner_ref[head : head + 1, :] = jnp.sum(
                scaled.astype(F32) * att[at, :].astype(F32), axis=0, keepdims=True
            )
        gweight[width:, :] = dot(att[...], gbranch[...], 1, 0).astype(BF)
        gsum[...] = jnp.zeros_like(gsum)
        for index in range(BLOCKS):
            upto = (index + 1) * blk
            cols = slice(index * blk, upto)
            copies[g][index].wait()
            for head in range(width // HEAD_DIM):
                at = slice(head * HEAD_DIM, (head + 1) * HEAD_DIM)
                low = buffer[index, head, 0:upto, :]
                gsum[at, 0:upto] += dot(scaled_ref[at, cols], low, 1, 1)
        low = gsum[...].astype(BF)
        gvalues[...] = low
        if g == 0:
            row_copy.wait()
        gweight[0:width, :] = dot(low, row_buffer[...], 1, 0).astype(BF)


def back_values(info, own, oth, rows, outws, atts, recips, probs):
    length, model = rows.shape
    width = atts[0].shape[0]
    heads = width // HEAD_DIM
    shapes = [((width, length), BF), ((8, length), F32), ((width, length), BF)]
    shapes.append(((2 * width, model), BF))
    shapes = shapes * 2
    kept = pltpu.VMEM((BLOCKS, heads, length, length // BLOCKS), BF)
    outs = pl.pallas_call(
        back_values_kernel,
        out_shape=[jax.ShapeDtypeStruct(s, d) for s, d in shapes],
        in_specs=[smem()] + [vmem()] * 2 + [hbm()] + [vmem()] * 6 + [hbm()] * 2,
        out_specs=[vmem()] * len(shapes),
        scratch_shapes=[
            pltpu.VMEM((length, model), BF),
            pltpu.VMEM((width, length), F32),
            kept,
            kept,
            pltpu.VMEM((length, model), BF),
            pltpu.SemaphoreType.DMA((2, BLOCKS + 1)),
        ],
        compiler_params=params(56),
        cost_estimate=cost(
            16 * length * model * width + 8 * heads * length * length * HEAD_DIM,
            4 * heads * length * length + 10 * length * model,
        ),
        name="back_values",
    )(info, own, oth, rows, *outws, *atts, *recips, *probs)
    return outs


def back_keys_kernel(info, qkv, scaled, inner, gvalues, rows, probs, gweight, gqkv, *scratch):
    gsum, buffer, row_buffer, sems = scratch
    copies = load_probs(probs, buffer, sems)
    row_copy = load(rows, row_buffer, sems.at[BLOCKS])
    length = PACKED_LENGTH
    width = scaled.shape[0]
    blk = length // BLOCKS
    gsum[...] = jnp.zeros_like(gsum)
    for index in range(BLOCKS):
        upto = (index + 1) * blk
        cols = slice(index * blk, upto)
        copies[index].wait()
        for head in range(width // HEAD_DIM):
            at = head * HEAD_DIM
            here = slice(at, at + HEAD_DIM)
            kat = slice(width + at, width + at + HEAD_DIM)
            vat = slice(2 * width + at, 2 * width + at + HEAD_DIM)
            gprobs = dot(qkv[vat, 0:upto], scaled[here, cols], 0, 0)
            low = buffer[index, head, 0:upto, :].astype(F32)
            gscores = (low * (gprobs - inner[head : head + 1, cols])).astype(BF)
            gsum[here, 0:upto] += dot(qkv[here, cols], gscores, 1, 1)
            gqueries = dot(qkv[kat, 0:upto], gscores, 1, 0) * HEAD_DIM**-0.5
            gqkv[here, cols] = gqueries.astype(BF)
    gqkv[width : 2 * width, :] = gsum[...].astype(BF)
    gqkv[2 * width :, :] = gvalues[...]
    row_copy.wait()
    gweight[...] = dot(gqkv[0 : 2 * width, :], row_buffer[...], 1, 0).astype(BF)


def back_keys(info, qkv, scaled, inner, gvalues, rows, probs):
    length, model = rows.shape
    width = scaled.shape[0]
    heads = width // HEAD_DIM
    return pl.pallas_call(
        back_keys_kernel,
        out_shape=[
            jax.ShapeDtypeStruct((2 * width, model), BF),
            jax.ShapeDtypeStruct((3 * width, length), BF),
        ],
        in_specs=[smem()] + [vmem()] * 4 + [hbm()] * 2,
        out_specs=[vmem()] * 2,
        scratch_shapes=[
            pltpu.VMEM((width, length), F32),
            pltpu.VMEM((BLOCKS, heads, length, length // BLOCKS), BF),
            pltpu.VMEM((length, model), BF),
            pltpu.SemaphoreType.DMA((BLOCKS + 1,)),
        ],
        compiler_params=params(56),
        cost_estimate=cost(
            4 * length * model * width + 12 * heads * length * length * HEAD_DIM,
            2 * heads * length * length + 10 * length * model,
        ),
        name="back_keys",
    )(info, qkv, scaled, inner, gvalues, rows, probs)


def back_rows_kernel(info, gqkv_a, gqkv_b, weight_a, weight_b, kept, sent_low, sent_high):
    half = kept.shape[0]
    parity = info[0]
    for refs, place in (((sent_low, sent_high), 1 - parity), ((kept,), parity)):
        at = pl.ds(pl.multiple_of(place * half, half), half)
        total = dot(gqkv_a[:, at], weight_a[...], 0, 0) + dot(gqkv_b[:, at], weight_b[...], 0, 0)
        size = half // len(refs)
        for index, ref in enumerate(refs):
            ref[...] = total[index * size : (index + 1) * size].astype(ref.dtype)


def back_rows(info, gqkv_a, gqkv_b, weight_a, weight_b):
    length = gqkv_a.shape[1]
    model = weight_a.shape[1]
    return pl.pallas_call(
        back_rows_kernel,
        out_shape=[
            jax.ShapeDtypeStruct((length // 2, model), F32),
            jax.ShapeDtypeStruct((length // 4, model), BF),
            jax.ShapeDtypeStruct((length // 4, model), BF),
        ],
        in_specs=[smem()] + [vmem()] * 4,
        out_specs=[vmem()] * 3,
        compiler_params=params(60),
        cost_estimate=cost(4 * length * model * gqkv_a.shape[0], 6 * length * model),
        name="back_rows",
    )(info, gqkv_a, gqkv_b, weight_a, weight_b)


def first_back_kernel(info, tokens, gmid, kept, low, high, gain, second, ginput, gvec):
    received = jnp.concatenate([low[...], high[...]], axis=0)
    grad = kept[...] + received.astype(F32)
    scaled, inverse = norm_parts(tokens[...].astype(F32))
    ginput[...] = gmid[...] + norm_back(grad, scaled, inverse, gain[...])
    gvec[...] = jnp.zeros_like(gvec)
    gvec[2:4, :] = second[0:2, :]
    gvec[0:1, :] = jnp.sum(grad * scaled, axis=0, keepdims=True)
    gvec[1:2, :] = jnp.sum(grad, axis=0, keepdims=True)


def first_back(info, tokens, gmid, kept, low, high, gain, second):
    count, width = tokens.shape
    return pl.pallas_call(
        first_back_kernel,
        out_shape=[
            jax.ShapeDtypeStruct((count, width), F32),
            jax.ShapeDtypeStruct((8, width), F32),
        ],
        in_specs=[smem()] + [vmem()] * 7,
        out_specs=[vmem()] * 2,
        compiler_params=params(60),
        cost_estimate=cost(20 * count * width, 16 * count * width),
        name="first_back",
    )(info, tokens, gmid, kept, low, high, gain, second)


def first_sum_kernel(info, mine, theirs, kept, sent):
    half = kept.shape[0]
    k = info[2]
    for ref, which in ((sent, 1 - k), (kept, k)):
        at = pl.ds(pl.multiple_of(which * half, half), half)
        ref[...] = (mine[at, :].astype(F32) + theirs[at, :].astype(F32)).astype(ref.dtype)


def first_sum(info, mine, theirs):
    rows, model = mine.shape
    return pl.pallas_call(
        first_sum_kernel,
        out_shape=[
            jax.ShapeDtypeStruct((rows // 2, model), F32),
            jax.ShapeDtypeStruct((rows // 2, model), BF),
        ],
        in_specs=[smem()] + [vmem()] * 2,
        out_specs=[vmem()] * 2,
        compiler_params=params(60),
        cost_estimate=cost(rows * model, 7 * rows * model),
        name="first_sum",
    )(info, mine, theirs)


def second_sum_kernel(info, kept, received, out):
    out[...] = (kept[...] + received[...].astype(F32)).astype(BF)


def second_sum(info, kept, received):
    return pl.pallas_call(
        second_sum_kernel,
        out_shape=jax.ShapeDtypeStruct(kept.shape, BF),
        in_specs=[smem()] + [vmem()] * 2,
        out_specs=vmem(),
        compiler_params=params(60),
        cost_estimate=cost(kept.size, 8 * kept.size),
        name="second_sum",
    )(info, kept, received)


def sum_blocks(blocks):
    total = None
    for index in range(blocks.shape[0]):
        block = blocks[index].astype(F32)
        total = block if total is None else total + block
    return total.astype(BF)


def middle_sum_kernel(info, blocks, kept, received, out):
    rows = blocks.shape[1]
    total = sum_blocks(blocks)
    for index in range(out.shape[0]):
        at = slice(index * rows, (index + 1) * rows)
        out[index, 0:rows] = total
        out[index, rows:] = (kept[at, :] + received[at, :].astype(F32)).astype(BF)


def middle_sum(info, blocks, kept, received):
    pieces, rows, model = blocks.shape
    return pl.pallas_call(
        middle_sum_kernel,
        out_shape=jax.ShapeDtypeStruct((pieces, 2 * rows, model), BF),
        in_specs=[smem()] + [vmem()] * 3,
        out_specs=vmem(),
        compiler_params=params(60),
        cost_estimate=cost(kept.size, 8 * kept.size),
        name="middle_sum",
    )(info, blocks, kept, received)


def third_sum_kernel(info, blocks, vectors, more, out, other):
    pieces, rows = other.shape[0:2]
    total = None
    for index in range(pieces):
        other[index] = blocks[index, 0:rows]
        block = blocks[index, rows:].astype(F32)
        total = block if total is None else total + block
    total = total.astype(BF)
    values = vectors[...] + more[...]
    high = values.astype(BF)
    low = (values - high.astype(F32)).astype(BF)
    both = jnp.concatenate([high, low], axis=0)
    for index in range(pieces):
        out[index, 0:rows] = total
        out[index, rows:] = both


def third_sum(info, blocks, vectors, more):
    pieces, rows, model = blocks.shape
    extra = 2 * vectors.shape[0]
    return pl.pallas_call(
        third_sum_kernel,
        out_shape=[
            jax.ShapeDtypeStruct((pieces, rows // 2 + extra, model), BF),
            jax.ShapeDtypeStruct((pieces, rows // 2, model), BF),
        ],
        in_specs=[smem()] + [vmem()] * 3,
        out_specs=[vmem()] * 2,
        compiler_params=params(60),
        cost_estimate=cost(blocks.size, 4 * blocks.size),
        name="third_sum",
    )(info, blocks, vectors, more)


def last_kernel(info, mine_qk, theirs_qk, mine_vo, theirs_vo, qkv, out, vectors):
    width = mine_vo.shape[0]
    pieces, count = mine_qk.shape[0], vectors.shape[0]
    rows = width // pieces
    k = info[2]

    def write(queries, keys, values, outs):
        for index in range(pieces):
            at = index * rows
            qkv[at : at + rows, :] = queries[index, 0:rows].astype(F32)
            qkv[width + at : width + at + rows, :] = keys[index, 0:rows].astype(F32)
        qkv[2 * width :, :] = values[...].astype(F32)
        out[...] = outs[...].astype(F32)

    @pl.when(k == 0)
    def even():
        write(mine_qk, theirs_qk, mine_vo, theirs_vo)

    @pl.when(k != 0)
    def odd():
        write(theirs_qk, mine_qk, theirs_vo, mine_vo)

    sums = []
    for ref in (mine_qk, theirs_qk):
        total = None
        for index in range(pieces):
            both = ref[index, rows:].astype(F32)
            value = both[0:count] + both[count:]
            total = value if total is None else total + value
        sums.append(total)
    vectors[...] = sums[0] + sums[1]


def last(info, mine_qk, theirs_qk, mine_vo, theirs_vo):
    width, model = mine_vo.shape
    count = (mine_qk.shape[1] - width // mine_qk.shape[0]) // 2
    return pl.pallas_call(
        last_kernel,
        out_shape=[
            jax.ShapeDtypeStruct((3 * width, model), F32),
            jax.ShapeDtypeStruct((width, model), F32),
            jax.ShapeDtypeStruct((count, model), F32),
        ],
        in_specs=[smem()] + [vmem()] * 4,
        out_specs=[vmem()] * 3,
        compiler_params=params(60),
        cost_estimate=cost(width * model, 24 * width * model),
        name="last",
    )(info, mine_qk, theirs_qk, mine_vo, theirs_vo)


def after(values, *others):
    return lax.optimization_barrier((values, *others))[0]


def swap(values, axis, bit):
    pairs = [(i, i ^ bit) for i in range(lax.axis_size(axis))]
    return lax.ppermute(values, axis, pairs)


def exchange(values, count):
    groups = [[2 * e + k for e in range(count)] for k in range(2)]
    shaped = values.reshape(count, -1, values.shape[1])
    moved = lax.all_to_all(shaped, "dp", 0, 0, tiled=True, axis_index_groups=groups)
    return moved.reshape(values.shape)


def exchange_chunks(chunks, count):
    moved = exchange(jnp.concatenate(chunks, axis=0), count)
    size = chunks[0].shape[0]
    return [moved[i * size : (i + 1) * size] for i in range(len(chunks))]


def local(
    tokens,
    first_gain,
    first_bias,
    qkv_weight,
    out_weight,
    second_gain,
    expert_norm_bias,
    up_weight,
    down_weight,
    gate_value,
    expert_ids,
    slot_index,
    segment_ids,
    cotangent,
):
    count, model = tokens.shape
    width = qkv_weight.shape[2]
    tp = lax.axis_index("tp")
    dp = lax.axis_index("dp")
    parity = tp % 2
    row_half = tp // 2 % 2
    k = dp % 2
    experts = lax.axis_size("dp") // 2
    capacity = 2 * count // experts
    paired = experts == CHUNKS
    here = dp // 2 if paired else 0 * dp
    info = jnp.stack([parity, row_half, k, here]).astype(jnp.int32)
    vector = lambda v: v.reshape(1, -1)
    gain, bias = first_gain, first_bias

    state = [info]

    def run(call, *operands):
        outs = call(state[0], *operands)
        state[0] = after(info, outs[-1] if isinstance(outs, (list, tuple)) else outs)
        return outs

    other_tokens = swap(tokens, "tp", 1)
    other_segments = swap(segment_ids, "tp", 1)
    weight_a = jnp.transpose(qkv_weight, (1, 2, 0)).reshape(3 * width, model)
    weight_b = swap(weight_a, "tp", 2)
    up, down = up_weight[0], down_weight[0]
    near = swap(run(give, up, down), "dp", 1)
    gate = vector(gate_value)
    slots = vector(expert_ids * capacity + slot_index)
    sent_grads = run(grad_dispatch, cotangent, gate, slots)
    grads = exchange(sent_grads, experts).reshape(CHUNKS, -1, model)

    segments = (vector(segment_ids), vector(other_segments))
    rows, att_a, probs_a, qkv_a, recip_a = run(
        attend, True, tokens, other_tokens, gain, bias, weight_a, *segments
    )
    out_b = swap(after(out_weight, recip_a), "tp", 2)
    att_b, probs_b, qkv_b, recip_b = run(
        attend, False, rows, vector(other_segments), gain, bias, weight_b, *segments
    )
    kept, sent = run(project, att_a, att_b, out_weight, out_b)
    received = swap(sent, "tp", 1)
    places = vector((expert_ids ^ here) * capacity + slot_index)
    middle, *sent_rows = run(
        middle_call, tokens, kept, received, second_gain, expert_norm_bias, places
    )

    if paired:
        first, second = lax.optimization_barrier(
            (swap(sent_rows[1], "dp", 2), swap(sent_rows[2], "dp", 4))
        )
        third = swap(after(sent_rows[3], second), "dp", 6)
        inputs = [sent_rows[0], first, second, third]
    else:
        inputs = exchange_chunks(sent_rows, experts)
    far = swap(after(near, inputs[1], grads), "tp", 1)
    weights = (up, down, near, far)
    hiddens, gpres, backs = [[None] * CHUNKS for unused in range(3)]
    results = None
    for index in (*range(1, CHUNKS), 0):
        hiddens[index], gpres[index], backs[index], results = run(
            expert, index, inputs[index], grads, weights, results
        )
    if paired:
        returned = [backs[0]] + [swap(backs[s], "dp", 2 * s) for s in range(1, CHUNKS)]
    else:
        returned = exchange_chunks(backs, experts)
    if paired:
        inputs[0], returned[1] = lax.optimization_barrier((inputs[0], returned[1]))
    stays, *leaves = run(expert_weights, inputs, grads, hiddens, gpres)
    leaves = [swap(leaf, "tp", 1) for leaf in leaves]
    gmid, gvec_two = run(
        second_back, returned, middle, cotangent, second_gain, places
    )
    other_gmid = swap(gmid, "tp", 1)
    outs = exchange(after(results, gmid).reshape(-1, model), experts)

    values = run(
        back_values, gmid, other_gmid, rows, (out_b, out_weight), (att_b, att_a),
        (recip_b, recip_a), (probs_b, probs_a),
    )
    scaled_b, inner_b, gvalues_b, gvo_b = values[0:4]
    scaled_a, inner_a, gvalues_a, gvo_a = values[4:8]
    theirs_vo = swap(gvo_b, "tp", 2)
    kept_pieces, sent_one, sent_two, sent_down = run(add_pieces, stays, *leaves)
    got_one = swap(sent_one, "dp", 1)
    gqk_b, gqkv_b = run(back_keys, qkv_b, scaled_b, inner_b, gvalues_b, rows, probs_b)
    theirs_qk = swap(gqk_b, "tp", 2)
    vo_kept, vo_sent = run(first_sum, gvo_a, theirs_vo)
    vo_received = swap(vo_sent, "dp", 1)
    gqk_a, gqkv_a = run(back_keys, qkv_a, scaled_a, inner_a, gvalues_a, rows, probs_a)
    got_two = swap(after(sent_two, gqk_a), "dp", 1)
    got_down = swap(after(sent_down, gqk_a), "tp", 2)

    def over_experts(blocks):
        moved = exchange(blocks.reshape(-1, model), experts)
        return moved.reshape(experts, -1, model)

    blocks_vo = over_experts(run(second_sum, vo_kept, after(vo_received, outs, got_one)))
    qk_kept, qk_sent = run(first_sum, gqk_a, theirs_qk)
    qk_received = swap(qk_sent, "dp", 1)
    gkept, *gsent = run(back_rows, gqkv_a, gqkv_b, weight_a, weight_b)
    greceived = [swap(g, "tp", 1) for g in gsent]
    blocks = over_experts(run(middle_sum, after(blocks_vo, got_two), qk_kept, qk_received))
    up_kept, down_kept, sent_up, sent_down = run(
        more_pieces, kept_pieces, got_one, got_two, got_down
    )
    last_down = swap(sent_down, "dp", 1)
    grad_input, vectors = run(first_back, tokens, gmid, gkept, *greceived, gain, gvec_two)
    vectors = vectors + swap(vectors, "tp", 1)
    more_vectors = swap(vectors, "tp", 2)
    last_up = swap(after(sent_up, more_vectors), "tp", 2)
    total_qk, full_vo = run(third_sum, blocks, vectors, more_vectors)
    full_qk = over_experts(total_qk)
    full_vo = full_vo.reshape(width, model)
    other_vo = swap(after(full_vo, last_down), "dp", 1)
    output = run(output_call, outs, middle, gate, slots)
    full_qk, other_vo = lax.optimization_barrier((full_qk, other_vo))
    other_qk = swap(full_qk, "dp", 1)
    grad_up, grad_down = run(last_pieces, up_kept, down_kept, last_up, last_down)
    grad_qkv, grad_out, vectors = run(last, full_qk, other_qk, full_vo, other_vo)
    grad_qkv = jnp.transpose(grad_qkv.reshape(3, width, model), (2, 0, 1))
    vec_one, vec_two = vectors[0:2], vectors[2:4]
    return (
        output,
        grad_input,
        vec_one[0],
        vec_one[1],
        grad_qkv,
        grad_out,
        vec_two[0],
        vec_two[1],
        grad_up[None],
        grad_down[None],
    )


def solution(mesh):
    placed = (
        P(("dp", "tp"), None),
        P(),
        P(),
        P(None, None, "tp"),
        P("tp", None),
        P(),
        P(),
        P("dp", None, None),
        P("dp", None, None),
        P(("dp", "tp")),
        P(("dp", "tp")),
        P(("dp", "tp")),
        P(("dp", "tp")),
        P(("dp", "tp"), None),
    )
    return jax.shard_map(
        local,
        mesh=mesh,
        in_specs=placed,
        out_specs=(
            P(("dp", "tp"), None),
            P(("dp", "tp"), None),
            P(),
            P(),
            P(None, None, "tp"),
            P("tp", None),
            P(),
            P(),
            P("dp", None, "tp"),
            P("dp", "tp", None),
        ),
        check_vma=False,
    )
```

```python
import functools

import jax
import jax.numpy as jnp
from jax import lax
from jax.experimental import pallas as pl
from jax.experimental.pallas import tpu as pltpu
from jax.sharding import PartitionSpec as P

HEAD_DIM = 64
PACKED_LENGTH = 1024
EPSILON = 1e-05
BF = jnp.bfloat16
F32 = jnp.float32
MASKED = -1e30
CHUNKS = 4


def dot(a, b, ca, cb):
    return lax.dot_general(a, b, (((ca,), (cb,)), ((), ())), preferred_element_type=F32)


def params(mib, **kw):
    return pltpu.CompilerParams(vmem_limit_bytes=mib * 1024 * 1024, **kw)


def cost(flops, nbytes):
    return pl.CostEstimate(flops=int(flops) // 64, bytes_accessed=int(nbytes) // 64, transcendentals=0)


def vmem():
    return pl.BlockSpec(memory_space=pltpu.VMEM)


def hbm():
    return pl.BlockSpec(memory_space=pltpu.HBM)


def smem():
    return pl.BlockSpec(memory_space=pltpu.SMEM)


def norm_parts(values):
    centre = jnp.mean(values, axis=-1, keepdims=True)
    shifted = values - centre
    inverse = lax.rsqrt(jnp.mean(shifted * shifted, axis=-1, keepdims=True) + EPSILON)
    return shifted * inverse, inverse


def norm_back(grad_normed, scaled, inverse, gain):
    grad_scaled = grad_normed * gain
    first = jnp.mean(grad_scaled, axis=-1, keepdims=True)
    second = jnp.mean(grad_scaled * scaled, axis=-1, keepdims=True)
    return inverse * (grad_scaled - first - scaled * second)


def column(row):
    return jnp.transpose(jnp.broadcast_to(row, (8, row.shape[1])))[:, 0:1]


def onehot(places, slots):
    rows = lax.broadcasted_iota(jnp.int32, (slots, places.shape[1]), 0)
    return jnp.where(rows == places, 1.0, 0.0).astype(BF)


def put_chunks(rows, places, outs):
    size = outs[0].shape[0]
    table = onehot(places, size * len(outs))
    for index, out in enumerate(outs):
        out[...] = dot(table[index * size : (index + 1) * size], rows, 1, 0).astype(BF)


def take_chunks(chunks, places):
    size = chunks[0].shape[0]
    table = onehot(places, size * len(chunks))
    total = None
    for index, chunk in enumerate(chunks):
        part = dot(table[index * size : (index + 1) * size], chunk[...], 0, 0)
        total = part if total is None else total + part
    return total


def grad_dispatch_kernel(info, cot_ref, gate_ref, places_ref, out):
    rows = (column(gate_ref[...]) * cot_ref[...].astype(F32)).astype(BF)
    put_chunks(rows, places_ref[...], [out])


def grad_dispatch(info, cotangent, gate, places):
    tokens, width = cotangent.shape
    return pl.pallas_call(
        grad_dispatch_kernel,
        out_shape=jax.ShapeDtypeStruct((2 * tokens, width), BF),
        in_specs=[smem()] + [vmem()] * 3,
        out_specs=vmem(),
        compiler_params=params(12),
        cost_estimate=cost(4 * tokens * tokens * width, 6 * tokens * width),
        name="grad_dispatch",
    )(info, cotangent, gate, places)


PAD = 64


def give_kernel(info, up, down, given, buffer, sems):
    tile = up.shape[0]
    at = pl.ds(pl.multiple_of(info[0] * tile, tile), tile)
    first, second = slice(0, tile), slice(tile, 2 * tile)
    loads = [
        pltpu.make_async_copy(up.at[:, at], buffer.at[first, :], sems.at[0]),
        pltpu.make_async_copy(down.at[at, :], buffer.at[second, :], sems.at[1]),
    ]
    for load in loads:
        load.start()
    stores = []
    for index, part in enumerate((first, second)):
        loads[index].wait()
        store = pltpu.make_async_copy(buffer.at[part, :], given.at[part, :], sems.at[2 + index])
        store.start()
        stores.append(store)
    for store in stores:
        store.wait()


def give(info, up, down):
    hbm = pl.BlockSpec(memory_space=pltpu.HBM)
    return pl.pallas_call(
        give_kernel,
        out_shape=jax.ShapeDtypeStruct((up.shape[1] + PAD, up.shape[0]), BF),
        in_specs=[smem(), hbm, hbm],
        out_specs=hbm,
        scratch_shapes=[
            pltpu.VMEM((up.shape[1], up.shape[0]), BF),
            pltpu.SemaphoreType.DMA((4,)),
        ],
        compiler_params=params(60),
        cost_estimate=cost(1, 4 * up.size),
        name="give",
    )(info, up, down)


BLOCKS = 2


def attend_kernel(first, heads, info, own, oth, gain, bias, weight, seg_own, seg_oth, *refs):
    parity = info[0]
    half = PACKED_LENGTH // 2
    if first:
        rows, att, probs, qkv, recip, segr, mask, buffer, sems = refs
        for ref, place in ((own, parity), (oth, 1 - parity)):
            scaled, unused = norm_parts(ref[...].astype(F32))
            normed = (scaled * gain[...] + bias[...]).astype(BF)
            rows[pl.ds(pl.multiple_of(place * half, half), half), :] = normed
    else:
        att, probs, qkv, recip, segr, mask, buffer, sems = refs
        rows = own
    for ref, place in ((seg_own, parity), (seg_oth, 1 - parity)):
        at = pl.ds(pl.multiple_of(place * half, half), half)
        segr[:, at] = jnp.broadcast_to(ref[...].astype(F32), (8, half))
    segc = jnp.transpose(segr[...])[:, 0:1]
    width = heads * HEAD_DIM
    blk = att.shape[1] // BLOCKS
    projected = dot(weight[...], rows[...], 1, 1).astype(BF)
    qkv[...] = projected
    qkv[0:width, :] = projected[0:width] * jnp.asarray(HEAD_DIM**-0.5, BF)
    copies = []
    for index in reversed(range(BLOCKS)):
        upto = (index + 1) * blk
        cols = slice(index * blk, upto)
        keypos = lax.broadcasted_iota(jnp.int32, (upto, blk), 0)
        querypos = lax.broadcasted_iota(jnp.int32, (upto, blk), 1) + index * blk
        allowed = (segc[0:upto, :] == segr[0:1, cols]) & (keypos <= querypos)
        mask[0:upto, :] = jnp.where(allowed, 0.0, MASKED)
        for head in range(heads):
            at = head * HEAD_DIM
            query = qkv[at : at + HEAD_DIM, cols]
            keys = qkv[width + at : width + at + HEAD_DIM, 0:upto]
            values = qkv[2 * width + at : 2 * width + at + HEAD_DIM, 0:upto]
            scores = dot(keys, query, 0, 0) + mask[0:upto, :]
            highest = jnp.max(scores, axis=0, keepdims=True)
            weights = jnp.exp(scores - highest)
            inverse = 1.0 / jnp.sum(weights, axis=0, keepdims=True)
            low = weights.astype(BF)
            buffer[index, head, 0:upto, :] = low
            result = dot(values, low, 1, 0) * inverse
            att[at : at + HEAD_DIM, cols] = result.astype(BF)
            recip[head : head + 1, cols] = inverse
        copy = pltpu.make_async_copy(
            buffer.at[index, :, 0:upto, :], probs.at[index, :, 0:upto, :], sems.at[index]
        )
        copy.start()
        copies.append(copy)
    for copy in copies:
        copy.wait()


def attend(info, first, own, oth, gain, bias, weight, seg_own, seg_oth):
    length = PACKED_LENGTH
    model = own.shape[1]
    width = weight.shape[0] // 3
    heads = width // HEAD_DIM
    blk = length // BLOCKS
    outs = [
        jax.ShapeDtypeStruct((width, length), BF),
        jax.ShapeDtypeStruct((BLOCKS, heads, length, blk), BF),
        jax.ShapeDtypeStruct((3 * width, length), BF),
        jax.ShapeDtypeStruct((8, length), F32),
    ]
    out_specs = [vmem(), pl.BlockSpec(memory_space=pltpu.HBM), vmem(), vmem()]
    scratch = [
        pltpu.VMEM((8, length), F32),
        pltpu.VMEM((length, blk), F32),
        pltpu.VMEM((BLOCKS, heads, length, blk), BF),
        pltpu.SemaphoreType.DMA((BLOCKS,)),
    ]
    if first:
        outs = [jax.ShapeDtypeStruct((length, model), BF)] + outs
        out_specs = [vmem()] + out_specs
    operands = (own, oth, gain, bias, weight, seg_own, seg_oth)
    return pl.pallas_call(
        functools.partial(attend_kernel, first, heads),
        out_shape=outs,
        in_specs=[smem()] + [vmem()] * len(operands),
        out_specs=out_specs,
        scratch_shapes=scratch,
        compiler_params=params(56),
        cost_estimate=cost(
            6 * length * model * width + 8 * heads * length * length * HEAD_DIM,
            2 * heads * length * length + 6 * length * model,
        ),
        name="attend",
    )(info, *operands)


def project_kernel(info, att_a, att_b, out_a, out_b, kept, sent):
    half = kept.shape[0]
    parity = info[0]
    for ref, place in ((sent, 1 - parity), (kept, parity)):
        cols = pl.ds(pl.multiple_of(place * half, half), half)
        total = dot(att_a[:, cols], out_a[...], 0, 0) + dot(att_b[:, cols], out_b[...], 0, 0)
        ref[...] = total.astype(ref.dtype)


def project(info, att_a, att_b, out_a, out_b):
    width, length = att_a.shape
    model = out_a.shape[1]
    return pl.pallas_call(
        project_kernel,
        out_shape=[
            jax.ShapeDtypeStruct((length // 2, model), F32),
            jax.ShapeDtypeStruct((length // 2, model), F32),
        ],
        in_specs=[smem()] + [vmem()] * 4,
        out_specs=[vmem()] * 2,
        compiler_params=params(12),
        cost_estimate=cost(4 * length * model * width, 6 * length * model),
        name="project",
    )(info, att_a, att_b, out_a, out_b)


def middle_kernel(info, tokens, kept, received, gain, bias, places, middle, *outs):
    values = tokens[...].astype(F32) + (kept[...] + received[...].astype(F32))
    middle[...] = values
    scaled, unused = norm_parts(values)
    normed = (scaled * gain[...] + bias[...]).astype(BF)
    put_chunks(normed, places[...], outs)


def middle_call(info, tokens, kept, received, gain, bias, places):
    count, width = tokens.shape
    size = 2 * count // CHUNKS
    return pl.pallas_call(
        middle_kernel,
        out_shape=[jax.ShapeDtypeStruct((count, width), F32)]
        + [jax.ShapeDtypeStruct((size, width), BF)] * CHUNKS,
        in_specs=[smem()] + [vmem()] * 6,
        out_specs=[vmem()] * (1 + CHUNKS),
        compiler_params=params(16),
        cost_estimate=cost(4 * count * count * width, 14 * count * width),
        name="middle",
    )(info, tokens, kept, received, gain, bias, places)


def stage_kernel(info, up, down, up_out, down_out):
    up_out[...] = up[...]
    down_out[...] = down[...]


def stage(info, up, down):
    return pl.pallas_call(
        stage_kernel,
        out_shape=[jax.ShapeDtypeStruct(w.shape, BF) for w in (up, down)],
        in_specs=[smem()] + [vmem()] * 2,
        out_specs=[vmem()] * 2,
        compiler_params=params(12),
        cost_estimate=cost(1, 8 * up.size),
        name="stage",
    )(info, up, down)


def gelu_parts(x):
    z = jnp.abs(x) * (0.5**0.5)
    t = 1.0 / (1.0 + 0.3275911 * z)
    poly = t * (
        0.254829592
        + t * (-0.284496736 + t * (1.421413741 + t * (-1.453152027 + t * 1.061405429)))
    )
    bell = jnp.exp(-0.5 * x * x)
    tail = 0.5 * poly * bell
    phi = jnp.where(x >= 0.0, 1.0 - tail, tail)
    return x * phi, phi + x * bell * 0.3989422804014327


def expert_kernel(chunk, first, info, inputs, grads, own_up, own_down, near, far, *refs):
    if not first:
        refs = refs[1:]
    hidden, gpre, result, given, buffer, grad_buffer, fetched, sems = refs
    size = own_up.shape[0]
    place = info[3] ^ chunk
    copies = [load(grads.at[place], grad_buffer, sems.at[0])]
    copies += [load(ref.at[0 : 2 * size, :], fetched.at[i], sems.at[1 + i]) for i, ref in enumerate((near, far))]
    rows = inputs[...]
    copies[0].wait()
    grad = grad_buffer[...]
    total, forward = None, None
    for tile in range(4):
        if tile < 2:
            at = slice(tile * size, (tile + 1) * size)
            up, down = own_up[:, at], own_down[at, :]
        else:
            copies[tile - 1].wait()
            up, down = fetched[tile - 2, 0:size, :], fetched[tile - 2, size : 2 * size, :]
        at = slice(tile * size, (tile + 1) * size)
        preact = dot(rows, up, 1, 0)
        ghidden = dot(grad, down, 1, 1)
        act, slope = gelu_parts(preact)
        act = act.astype(BF)
        hidden[:, at] = act
        low = (ghidden * slope).astype(BF)
        gpre[:, at] = low
        part = dot(low, up, 1, 1)
        total = part if total is None else total + part
        part = dot(act, down, 1, 0)
        forward = part if forward is None else forward + part
    buffer[...] = forward.astype(BF)
    copy = load(buffer, given.at[place], sems.at[3])
    result[...] = total.astype(BF)
    copy.wait()


def expert(info, chunk, inputs, grads, weights, given=None):
    rows, model = inputs.shape
    tile = weights[0].shape[0]
    operands = [info, inputs, grads, *weights]
    in_specs = [smem(), vmem(), hbm(), vmem(), vmem(), hbm(), hbm()]
    if given is not None:
        operands.append(given)
        in_specs.append(hbm())
    return pl.pallas_call(
        functools.partial(expert_kernel, chunk, given is None),
        out_shape=[
            jax.ShapeDtypeStruct((rows, 4 * tile), BF),
            jax.ShapeDtypeStruct((rows, 4 * tile), BF),
            jax.ShapeDtypeStruct((rows, model), BF),
            jax.ShapeDtypeStruct(grads.shape, BF),
        ],
        in_specs=in_specs,
        out_specs=[vmem()] * 3 + [hbm()],
        scratch_shapes=[
            pltpu.VMEM((rows, model), BF),
            pltpu.VMEM((rows, model), BF),
            pltpu.VMEM((2, 2 * tile, model), BF),
            pltpu.SemaphoreType.DMA((4,)),
        ],
        input_output_aliases={} if given is None else {7: 3},
        compiler_params=params(20),
        cost_estimate=cost(32 * rows * model * tile, 16 * model * tile + 16 * rows * tile),
        name="expert",
    )(*operands)


GIVEN = (3, 3, 2)


def piece_at(theirs, other):
    return 2 * theirs + other, 4 + 2 * other + theirs


def given_at(piece):
    for which, number in enumerate(GIVEN):
        if piece < number:
            return which, piece
        piece -= number


def expert_weights_kernel(info, grads, *refs):
    n = CHUNKS
    inputs, hiddens, gpres = refs[:n], refs[n : 2 * n], refs[2 * n : 3 * n]
    stays, given = refs[3 * n], refs[3 * n + 1 : 3 * n + 4]
    sub = stays.shape[1]
    size = 2 * sub
    parity, row_half, here = info[0], info[1], info[3]
    mine = pl.multiple_of(parity * sub, sub)
    gone = pl.multiple_of((1 - parity) * sub, sub)
    for theirs in range(2):
        for other in range(2):
            tile = other ^ row_half
            if theirs:
                tile = 2 + (tile ^ parity)
            for offset, keeps in ((mine, True), (gone, False)):
                at = pl.ds(pl.multiple_of(tile * size + offset, sub), sub)
                for is_down, piece in enumerate(piece_at(theirs, other)):
                    total = None
                    for index in range(n):
                        source = (hiddens if is_down else gpres)[index][:, at]
                        factor = grads[here ^ index] if is_down else inputs[index][...]
                        part = dot(source, factor, 0, 0)
                        total = part if total is None else total + part
                    which, place = given_at(piece)
                    if keeps:
                        stays[piece] = total.astype(BF)
                    else:
                        given[which][place] = total.astype(BF)


def expert_weights(info, inputs, grads, hiddens, gpres):
    rows, model = inputs[0].shape
    sub = hiddens[0].shape[1] // 8
    return pl.pallas_call(
        expert_weights_kernel,
        out_shape=[jax.ShapeDtypeStruct((m, sub, model), BF) for m in (8, *GIVEN)],
        in_specs=[smem()] + [vmem()] * (1 + 3 * CHUNKS),
        out_specs=[vmem()] * 4,
        compiler_params=params(20),
        cost_estimate=cost(32 * CHUNKS * rows * model * sub, 64 * model * sub),
        name="expert_weights",
    )(info, grads, *inputs, *hiddens, *gpres)


def pieces_kernel(info, stays, first, second, third, kept, sent_one, sent_two, sent_down):
    received = (first, second, third)
    for ref, pieces in (
        (kept, (0, 1, 4, 5)),
        (sent_one, (2,)),
        (sent_two, (3,)),
        (sent_down, (6, 7)),
    ):
        for index, piece in enumerate(pieces):
            which, place = given_at(piece)
            total = stays[piece].astype(F32) + received[which][place].astype(F32)
            ref[index] = total.astype(BF)


def add_pieces(info, stays, *received):
    n, sub, model = stays.shape
    return pl.pallas_call(
        pieces_kernel,
        out_shape=[jax.ShapeDtypeStruct((m, sub, model), BF) for m in (4, 1, 1, 2)],
        in_specs=[smem()] + [vmem()] * 4,
        out_specs=[vmem()] * 4,
        compiler_params=params(20),
        cost_estimate=cost(stays.size, 6 * stays.size),
        name="add_pieces",
    )(info, stays, *received)


def more_pieces_kernel(info, kept, one, two, got_down, up, down, sent_up, sent_down):
    for index, got, ref in (
        (0, one.at[0], up),
        (1, two.at[0], sent_up),
        (2, got_down.at[0], down),
        (3, got_down.at[1], sent_down),
    ):
        ref[...] = (kept[index].astype(F32) + got[...].astype(F32)).astype(BF)


def more_pieces(info, kept, *got):
    n, sub, model = kept.shape
    return pl.pallas_call(
        more_pieces_kernel,
        out_shape=[jax.ShapeDtypeStruct((sub, model), BF)] * 4,
        in_specs=[smem()] + [vmem()] * 4,
        out_specs=[vmem()] * 4,
        compiler_params=params(60),
        cost_estimate=cost(kept.size, 6 * kept.size),
        name="more_pieces",
    )(info, kept, *got)


def last_pieces_kernel(info, up, down, got_up, got_down, grad_up, grad_down):
    grad_up[...] = jnp.transpose(up[...].astype(F32) + got_up[...].astype(F32))
    grad_down[...] = down[...].astype(F32) + got_down[...].astype(F32)


def last_pieces(info, up, down, got_up, got_down):
    sub, model = up.shape
    return pl.pallas_call(
        last_pieces_kernel,
        out_shape=[
            jax.ShapeDtypeStruct((model, sub), F32),
            jax.ShapeDtypeStruct((sub, model), F32),
        ],
        in_specs=[smem()] + [vmem()] * 4,
        out_specs=[vmem()] * 2,
        compiler_params=params(60),
        cost_estimate=cost(up.size, 16 * up.size),
        name="last_pieces",
    )(info, up, down, got_up, got_down)


def second_back_kernel(info, *refs):
    chunks = refs[:CHUNKS]
    middle, cot, gain, places, gmid, gvec = refs[CHUNKS:]
    grad = take_chunks(chunks, places[...])
    scaled, inverse = norm_parts(middle[...])
    total = cot[...].astype(F32) + norm_back(grad, scaled, inverse, gain[...])
    gmid[...] = total
    gvec[...] = jnp.zeros_like(gvec)
    gvec[0:1, :] = jnp.sum(grad * scaled, axis=0, keepdims=True)
    gvec[1:2, :] = jnp.sum(grad, axis=0, keepdims=True)


def second_back(info, chunks, middle, cotangent, gain, places):
    count, width = cotangent.shape
    return pl.pallas_call(
        second_back_kernel,
        out_shape=[
            jax.ShapeDtypeStruct((count, width), F32),
            jax.ShapeDtypeStruct((8, width), F32),
        ],
        in_specs=[smem()] + [vmem()] * (CHUNKS + 4),
        out_specs=[vmem()] * 2,
        compiler_params=params(16),
        cost_estimate=cost(4 * count * count * width, 16 * count * width),
        name="second_back",
    )(info, *chunks, middle, cotangent, gain, places)


def output_kernel(info, results, middle, gate, places, out):
    total = take_chunks([results], places[...])
    out[...] = (middle[...] + column(gate[...]) * total).astype(BF)


def output_call(info, results, middle, gate, places):
    return pl.pallas_call(
        output_kernel,
        out_shape=jax.ShapeDtypeStruct(middle.shape, BF),
        in_specs=[smem()] + [vmem()] * 4,
        out_specs=vmem(),
        compiler_params=params(60),
        cost_estimate=cost(4 * middle.shape[0] * middle.size, 8 * middle.size),
        name="output",
    )(info, results, middle, gate, places)


def load_probs(probs, buffer, sems):
    copies = []
    blk = buffer.shape[3]
    for index in range(BLOCKS):
        upto = (index + 1) * blk
        copy = pltpu.make_async_copy(
            probs.at[index, :, 0:upto, :], buffer.at[index, :, 0:upto, :], sems.at[index]
        )
        copy.start()
        copies.append(copy)
    return copies


def load(source, target, sem):
    copy = pltpu.make_async_copy(source, target, sem)
    copy.start()
    return copy


def back_values_kernel(info, own, oth, rows, *refs):
    outws, atts, recips, probs = refs[0:2], refs[2:4], refs[4:6], refs[6:8]
    outs = refs[8:16]
    gbranch, gsum, row_buffer, sems = refs[16:18] + refs[20:22]
    buffers = refs[18:20]
    copies = [load_probs(probs[g], buffers[g], sems.at[g]) for g in range(2)]
    row_copy = load(rows, row_buffer, sems.at[0, BLOCKS])
    length = PACKED_LENGTH
    width = atts[0].shape[0]
    blk = length // BLOCKS
    half = length // 2
    parity = info[0]
    for ref, place in ((own, parity), (oth, 1 - parity)):
        gbranch[pl.ds(pl.multiple_of(place * half, half), half), :] = ref[...].astype(BF)
    for g in range(2):
        scaled_ref, inner_ref, gvalues, gweight = outs[4 * g : 4 * g + 4]
        att, recip, buffer = atts[g], recips[g], buffers[g]
        gatt = dot(outws[g][...], gbranch[...], 1, 1).astype(BF).astype(F32)
        for head in range(width // HEAD_DIM):
            at = slice(head * HEAD_DIM, (head + 1) * HEAD_DIM)
            scaled = (gatt[at] * recip[head : head + 1, :]).astype(BF)
            scaled_ref[at, :] = scaled
            inner_ref[head : head + 1, :] = jnp.sum(
                scaled.astype(F32) * att[at, :].astype(F32), axis=0, keepdims=True
            )
        gweight[width:, :] = dot(att[...], gbranch[...], 1, 0).astype(BF)
        gsum[...] = jnp.zeros_like(gsum)
        for index in range(BLOCKS):
            upto = (index + 1) * blk
            cols = slice(index * blk, upto)
            copies[g][index].wait()
            for head in range(width // HEAD_DIM):
                at = slice(head * HEAD_DIM, (head + 1) * HEAD_DIM)
                low = buffer[index, head, 0:upto, :]
                gsum[at, 0:upto] += dot(scaled_ref[at, cols], low, 1, 1)
        low = gsum[...].astype(BF)
        gvalues[...] = low
        if g == 0:
            row_copy.wait()
        gweight[0:width, :] = dot(low, row_buffer[...], 1, 0).astype(BF)


def back_values(info, own, oth, rows, outws, atts, recips, probs):
    length, model = rows.shape
    width = atts[0].shape[0]
    heads = width // HEAD_DIM
    shapes = [((width, length), BF), ((8, length), F32), ((width, length), BF)]
    shapes.append(((2 * width, model), BF))
    shapes = shapes * 2
    kept = pltpu.VMEM((BLOCKS, heads, length, length // BLOCKS), BF)
    outs = pl.pallas_call(
        back_values_kernel,
        out_shape=[jax.ShapeDtypeStruct(s, d) for s, d in shapes],
        in_specs=[smem()] + [vmem()] * 2 + [hbm()] + [vmem()] * 6 + [hbm()] * 2,
        out_specs=[vmem()] * len(shapes),
        scratch_shapes=[
            pltpu.VMEM((length, model), BF),
            pltpu.VMEM((width, length), F32),
            kept,
            kept,
            pltpu.VMEM((length, model), BF),
            pltpu.SemaphoreType.DMA((2, BLOCKS + 1)),
        ],
        compiler_params=params(56),
        cost_estimate=cost(
            16 * length * model * width + 8 * heads * length * length * HEAD_DIM,
            4 * heads * length * length + 10 * length * model,
        ),
        name="back_values",
    )(info, own, oth, rows, *outws, *atts, *recips, *probs)
    return outs


def back_keys_kernel(info, qkv, scaled, inner, gvalues, rows, probs, gweight, gqkv, *scratch):
    gsum, buffer, row_buffer, sems = scratch
    copies = load_probs(probs, buffer, sems)
    row_copy = load(rows, row_buffer, sems.at[BLOCKS])
    length = PACKED_LENGTH
    width = scaled.shape[0]
    blk = length // BLOCKS
    gsum[...] = jnp.zeros_like(gsum)
    for index in range(BLOCKS):
        upto = (index + 1) * blk
        cols = slice(index * blk, upto)
        copies[index].wait()
        for head in range(width // HEAD_DIM):
            at = head * HEAD_DIM
            here = slice(at, at + HEAD_DIM)
            kat = slice(width + at, width + at + HEAD_DIM)
            vat = slice(2 * width + at, 2 * width + at + HEAD_DIM)
            gprobs = dot(qkv[vat, 0:upto], scaled[here, cols], 0, 0)
            low = buffer[index, head, 0:upto, :].astype(F32)
            gscores = (low * (gprobs - inner[head : head + 1, cols])).astype(BF)
            gsum[here, 0:upto] += dot(qkv[here, cols], gscores, 1, 1)
            gqueries = dot(qkv[kat, 0:upto], gscores, 1, 0) * HEAD_DIM**-0.5
            gqkv[here, cols] = gqueries.astype(BF)
    gqkv[width : 2 * width, :] = gsum[...].astype(BF)
    gqkv[2 * width :, :] = gvalues[...]
    row_copy.wait()
    gweight[...] = dot(gqkv[0 : 2 * width, :], row_buffer[...], 1, 0).astype(BF)


def back_keys(info, qkv, scaled, inner, gvalues, rows, probs):
    length, model = rows.shape
    width = scaled.shape[0]
    heads = width // HEAD_DIM
    return pl.pallas_call(
        back_keys_kernel,
        out_shape=[
            jax.ShapeDtypeStruct((2 * width, model), BF),
            jax.ShapeDtypeStruct((3 * width, length), BF),
        ],
        in_specs=[smem()] + [vmem()] * 4 + [hbm()] * 2,
        out_specs=[vmem()] * 2,
        scratch_shapes=[
            pltpu.VMEM((width, length), F32),
            pltpu.VMEM((BLOCKS, heads, length, length // BLOCKS), BF),
            pltpu.VMEM((length, model), BF),
            pltpu.SemaphoreType.DMA((BLOCKS + 1,)),
        ],
        compiler_params=params(56),
        cost_estimate=cost(
            4 * length * model * width + 12 * heads * length * length * HEAD_DIM,
            2 * heads * length * length + 10 * length * model,
        ),
        name="back_keys",
    )(info, qkv, scaled, inner, gvalues, rows, probs)


def back_rows_kernel(info, gqkv_a, gqkv_b, weight_a, weight_b, kept, sent_low, sent_high):
    half = kept.shape[0]
    parity = info[0]
    for refs, place in (((sent_low, sent_high), 1 - parity), ((kept,), parity)):
        at = pl.ds(pl.multiple_of(place * half, half), half)
        total = dot(gqkv_a[:, at], weight_a[...], 0, 0) + dot(gqkv_b[:, at], weight_b[...], 0, 0)
        size = half // len(refs)
        for index, ref in enumerate(refs):
            ref[...] = total[index * size : (index + 1) * size].astype(ref.dtype)


def back_rows(info, gqkv_a, gqkv_b, weight_a, weight_b):
    length = gqkv_a.shape[1]
    model = weight_a.shape[1]
    return pl.pallas_call(
        back_rows_kernel,
        out_shape=[
            jax.ShapeDtypeStruct((length // 2, model), BF),
            jax.ShapeDtypeStruct((length // 4, model), BF),
            jax.ShapeDtypeStruct((length // 4, model), BF),
        ],
        in_specs=[smem()] + [vmem()] * 4,
        out_specs=[vmem()] * 3,
        compiler_params=params(60),
        cost_estimate=cost(4 * length * model * gqkv_a.shape[0], 6 * length * model),
        name="back_rows",
    )(info, gqkv_a, gqkv_b, weight_a, weight_b)


def first_back_kernel(info, tokens, gmid, kept, low, high, gain, second, ginput, gvec):
    received = jnp.concatenate([low[...], high[...]], axis=0)
    grad = kept[...].astype(F32) + received.astype(F32)
    scaled, inverse = norm_parts(tokens[...].astype(F32))
    ginput[...] = gmid[...] + norm_back(grad, scaled, inverse, gain[...])
    gvec[...] = jnp.zeros_like(gvec)
    gvec[2:4, :] = second[0:2, :]
    gvec[0:1, :] = jnp.sum(grad * scaled, axis=0, keepdims=True)
    gvec[1:2, :] = jnp.sum(grad, axis=0, keepdims=True)


def first_back(info, tokens, gmid, kept, low, high, gain, second):
    count, width = tokens.shape
    return pl.pallas_call(
        first_back_kernel,
        out_shape=[
            jax.ShapeDtypeStruct((count, width), F32),
            jax.ShapeDtypeStruct((8, width), F32),
        ],
        in_specs=[smem()] + [vmem()] * 7,
        out_specs=[vmem()] * 2,
        compiler_params=params(60),
        cost_estimate=cost(20 * count * width, 16 * count * width),
        name="first_back",
    )(info, tokens, gmid, kept, low, high, gain, second)


def first_sum_kernel(info, mine, theirs, kept, sent):
    half = kept.shape[0]
    k = info[2]
    for ref, which in ((sent, 1 - k), (kept, k)):
        at = pl.ds(pl.multiple_of(which * half, half), half)
        ref[...] = (mine[at, :].astype(F32) + theirs[at, :].astype(F32)).astype(ref.dtype)


def first_sum(info, mine, theirs):
    rows, model = mine.shape
    return pl.pallas_call(
        first_sum_kernel,
        out_shape=[
            jax.ShapeDtypeStruct((rows // 2, model), F32),
            jax.ShapeDtypeStruct((rows // 2, model), BF),
        ],
        in_specs=[smem()] + [vmem()] * 2,
        out_specs=[vmem()] * 2,
        compiler_params=params(60),
        cost_estimate=cost(rows * model, 7 * rows * model),
        name="first_sum",
    )(info, mine, theirs)


def second_sum_kernel(info, kept, received, out):
    out[...] = (kept[...] + received[...].astype(F32)).astype(BF)


def second_sum(info, kept, received):
    return pl.pallas_call(
        second_sum_kernel,
        out_shape=jax.ShapeDtypeStruct(kept.shape, BF),
        in_specs=[smem()] + [vmem()] * 2,
        out_specs=vmem(),
        compiler_params=params(60),
        cost_estimate=cost(kept.size, 8 * kept.size),
        name="second_sum",
    )(info, kept, received)


def sum_blocks(blocks):
    total = None
    for index in range(blocks.shape[0]):
        block = blocks[index].astype(F32)
        total = block if total is None else total + block
    return total.astype(BF)


def middle_sum_kernel(info, blocks, kept, received, out):
    rows = blocks.shape[1]
    total = sum_blocks(blocks)
    for index in range(out.shape[0]):
        at = slice(index * rows, (index + 1) * rows)
        out[index, 0:rows] = total
        out[index, rows:] = (kept[at, :] + received[at, :].astype(F32)).astype(BF)


def middle_sum(info, blocks, kept, received):
    pieces, rows, model = blocks.shape
    return pl.pallas_call(
        middle_sum_kernel,
        out_shape=jax.ShapeDtypeStruct((pieces, 2 * rows, model), BF),
        in_specs=[smem()] + [vmem()] * 3,
        out_specs=vmem(),
        compiler_params=params(60),
        cost_estimate=cost(kept.size, 8 * kept.size),
        name="middle_sum",
    )(info, blocks, kept, received)


def third_sum_kernel(info, blocks, vectors, more, out, other):
    pieces, rows = other.shape[0:2]
    total = None
    for index in range(pieces):
        other[index] = blocks[index, 0:rows]
        block = blocks[index, rows:].astype(F32)
        total = block if total is None else total + block
    total = total.astype(BF)
    values = vectors[...] + more[...]
    high = values.astype(BF)
    low = (values - high.astype(F32)).astype(BF)
    both = jnp.concatenate([high, low], axis=0)
    for index in range(pieces):
        out[index, 0:rows] = total
        out[index, rows:] = both


def third_sum(info, blocks, vectors, more):
    pieces, rows, model = blocks.shape
    extra = 2 * vectors.shape[0]
    return pl.pallas_call(
        third_sum_kernel,
        out_shape=[
            jax.ShapeDtypeStruct((pieces, rows // 2 + extra, model), BF),
            jax.ShapeDtypeStruct((pieces, rows // 2, model), BF),
        ],
        in_specs=[smem()] + [vmem()] * 3,
        out_specs=[vmem()] * 2,
        compiler_params=params(60),
        cost_estimate=cost(blocks.size, 4 * blocks.size),
        name="third_sum",
    )(info, blocks, vectors, more)


def last_kernel(info, mine_qk, theirs_qk, mine_vo, theirs_vo, qkv, out, *vectors):
    width = mine_vo.shape[0]
    pieces = mine_qk.shape[0]
    rows = width // pieces
    count = (mine_qk.shape[1] - rows) // 2
    k = info[2]

    def write(queries, keys, values, outs):
        for index in range(pieces):
            at = index * rows
            qkv[at : at + rows, :] = queries[index, 0:rows].astype(F32)
            qkv[width + at : width + at + rows, :] = keys[index, 0:rows].astype(F32)
        qkv[2 * width :, :] = values[...].astype(F32)
        out[...] = outs[...].astype(F32)

    @pl.when(k == 0)
    def even():
        write(mine_qk, theirs_qk, mine_vo, theirs_vo)

    @pl.when(k != 0)
    def odd():
        write(theirs_qk, mine_qk, theirs_vo, mine_vo)

    sums = []
    for ref in (mine_qk, theirs_qk):
        total = None
        for index in range(pieces):
            both = ref[index, rows:].astype(F32)
            value = both[0:count] + both[count:]
            total = value if total is None else total + value
        sums.append(total)
    for index, ref in enumerate(vectors):
        ref[...] = sums[0][index] + sums[1][index]


def last(info, mine_qk, theirs_qk, mine_vo, theirs_vo):
    width, model = mine_vo.shape
    return pl.pallas_call(
        last_kernel,
        out_shape=[
            jax.ShapeDtypeStruct((3 * width, model), F32),
            jax.ShapeDtypeStruct((width, model), F32),
        ]
        + [jax.ShapeDtypeStruct((model,), F32)] * 4,
        in_specs=[smem()] + [vmem()] * 4,
        out_specs=[vmem()] * 6,
        compiler_params=params(60),
        cost_estimate=cost(width * model, 24 * width * model),
        name="last",
    )(info, mine_qk, theirs_qk, mine_vo, theirs_vo)


def after(values, *others):
    return lax.optimization_barrier((values, *others))[0]


def swap(values, axis, bit):
    pairs = [(i, i ^ bit) for i in range(lax.axis_size(axis))]
    return lax.ppermute(values, axis, pairs)


def exchange(values, count):
    groups = [[2 * e + k for e in range(count)] for k in range(2)]
    shaped = values.reshape(count, -1, values.shape[1])
    moved = lax.all_to_all(shaped, "dp", 0, 0, tiled=True, axis_index_groups=groups)
    return moved.reshape(values.shape)


def exchange_chunks(chunks, count):
    moved = exchange(jnp.concatenate(chunks, axis=0), count)
    size = chunks[0].shape[0]
    return [moved[i * size : (i + 1) * size] for i in range(len(chunks))]


def local(
    tokens,
    first_gain,
    first_bias,
    qkv_weight,
    out_weight,
    second_gain,
    expert_norm_bias,
    up_weight,
    down_weight,
    gate_value,
    expert_ids,
    slot_index,
    segment_ids,
    cotangent,
):
    count, model = tokens.shape
    width = qkv_weight.shape[2]
    tp = lax.axis_index("tp")
    dp = lax.axis_index("dp")
    parity = tp % 2
    row_half = tp // 2 % 2
    k = dp % 2
    experts = lax.axis_size("dp") // 2
    capacity = 2 * count // experts
    paired = experts == CHUNKS
    here = dp // 2 if paired else 0 * dp
    info = jnp.stack([parity, row_half, k, here]).astype(jnp.int32)
    vector = lambda v: v.reshape(1, -1)
    gain, bias = first_gain, first_bias

    state = [info]

    def run(call, *operands):
        outs = call(state[0], *operands)
        state[0] = after(info, outs[-1] if isinstance(outs, (list, tuple)) else outs)
        return outs

    other_tokens = swap(tokens, "tp", 1)
    other_segments = swap(segment_ids, "tp", 1)
    weight_a = jnp.transpose(qkv_weight, (1, 2, 0)).reshape(3 * width, model)
    weight_b = swap(weight_a, "tp", 2)
    up, down = up_weight[0], down_weight[0]
    near = swap(run(give, up, down), "dp", 1)
    gate = vector(gate_value)
    slots = vector(expert_ids * capacity + slot_index)
    sent_grads = run(grad_dispatch, cotangent, gate, slots)
    grads = exchange(sent_grads, experts).reshape(CHUNKS, -1, model)

    segments = (vector(segment_ids), vector(other_segments))
    rows, att_a, probs_a, qkv_a, recip_a = run(
        attend, True, tokens, other_tokens, gain, bias, weight_a, *segments
    )
    out_b = swap(after(out_weight, recip_a), "tp", 2)
    att_b, probs_b, qkv_b, recip_b = run(
        attend, False, rows, vector(other_segments), gain, bias, weight_b, *segments
    )
    kept, sent = run(project, att_a, att_b, out_weight, out_b)
    received = swap(sent, "tp", 1)
    places = vector((expert_ids ^ here) * capacity + slot_index)
    middle, *sent_rows = run(
        middle_call, tokens, kept, received, second_gain, expert_norm_bias, places
    )

    if paired:
        first, second = lax.optimization_barrier(
            (swap(sent_rows[1], "dp", 2), swap(sent_rows[2], "dp", 4))
        )
        third = swap(after(sent_rows[3], second), "dp", 6)
        inputs = [sent_rows[0], first, second, third]
    else:
        inputs = exchange_chunks(sent_rows, experts)
    far = swap(after(near, inputs[1], grads), "tp", 1)
    weights = (*run(stage, up, down), near, far)
    hiddens, gpres, backs = [[None] * CHUNKS for unused in range(3)]
    results = None
    for index in (*range(1, CHUNKS), 0):
        hiddens[index], gpres[index], backs[index], results = run(
            expert, index, inputs[index], grads, weights, results
        )
    if paired:
        returned = [backs[0]] + [swap(backs[s], "dp", 2 * s) for s in range(1, CHUNKS)]
    else:
        returned = exchange_chunks(backs, experts)
    if paired:
        inputs[0], returned[1] = lax.optimization_barrier((inputs[0], returned[1]))
    stays, *leaves = run(expert_weights, inputs, grads, hiddens, gpres)
    leaves = [swap(leaf, "tp", 1) for leaf in leaves]
    gmid, gvec_two = run(
        second_back, returned, middle, cotangent, second_gain, places
    )
    other_gmid = swap(gmid, "tp", 1)
    outs = exchange(after(results, gmid).reshape(-1, model), experts)

    values = run(
        back_values, gmid, other_gmid, rows, (out_b, out_weight), (att_b, att_a),
        (recip_b, recip_a), (probs_b, probs_a),
    )
    scaled_b, inner_b, gvalues_b, gvo_b = values[0:4]
    scaled_a, inner_a, gvalues_a, gvo_a = values[4:8]
    theirs_vo = swap(gvo_b, "tp", 2)
    kept_pieces, sent_one, sent_two, sent_down = run(add_pieces, stays, *leaves)
    got_one = swap(sent_one, "dp", 1)
    gqk_b, gqkv_b = run(back_keys, qkv_b, scaled_b, inner_b, gvalues_b, rows, probs_b)
    theirs_qk = swap(gqk_b, "tp", 2)
    vo_kept, vo_sent = run(first_sum, gvo_a, theirs_vo)
    vo_received = swap(vo_sent, "dp", 1)
    gqk_a, gqkv_a = run(back_keys, qkv_a, scaled_a, inner_a, gvalues_a, rows, probs_a)
    got_two = swap(after(sent_two, gqk_a), "dp", 1)
    got_down = swap(after(sent_down, gqk_a), "tp", 2)

    def over_experts(blocks):
        moved = exchange(blocks.reshape(-1, model), experts)
        return moved.reshape(experts, -1, model)

    blocks_vo = over_experts(run(second_sum, vo_kept, after(vo_received, outs, got_one)))
    qk_kept, qk_sent = run(first_sum, gqk_a, theirs_qk)
    qk_received = swap(qk_sent, "dp", 1)
    gkept, *gsent = run(back_rows, gqkv_a, gqkv_b, weight_a, weight_b)
    greceived = [swap(g, "tp", 1) for g in gsent]
    blocks = over_experts(run(middle_sum, after(blocks_vo, got_two), qk_kept, qk_received))
    up_kept, down_kept, sent_up, sent_down = run(
        more_pieces, kept_pieces, got_one, got_two, got_down
    )
    last_down = swap(sent_down, "dp", 1)
    grad_input, vectors = run(first_back, tokens, gmid, gkept, *greceived, gain, gvec_two)
    vectors = vectors + swap(vectors, "tp", 1)
    more_vectors = swap(vectors, "tp", 2)
    last_up = swap(after(sent_up, more_vectors), "tp", 2)
    total_qk, full_vo = run(third_sum, blocks, vectors, more_vectors)
    full_qk = over_experts(total_qk)
    full_vo = full_vo.reshape(width, model)
    other_vo = swap(after(full_vo, last_down), "dp", 1)
    output = run(output_call, outs, middle, gate, slots)
    full_qk, other_vo = lax.optimization_barrier((full_qk, other_vo))
    other_qk = swap(full_qk, "dp", 1)
    grad_up, grad_down = run(last_pieces, up_kept, down_kept, last_up, last_down)
    grad_qkv, grad_out, *vectors = run(last, full_qk, other_qk, full_vo, other_vo)
    grad_qkv = jnp.transpose(grad_qkv.reshape(3, width, model), (2, 0, 1))
    return (
        output,
        grad_input,
        vectors[0],
        vectors[1],
        grad_qkv,
        grad_out,
        vectors[2],
        vectors[3],
        grad_up[None],
        grad_down[None],
    )


def solution(mesh):
    placed = (
        P(("dp", "tp"), None),
        P(),
        P(),
        P(None, None, "tp"),
        P("tp", None),
        P(),
        P(),
        P("dp", None, None),
        P("dp", None, None),
        P(("dp", "tp")),
        P(("dp", "tp")),
        P(("dp", "tp")),
        P(("dp", "tp")),
        P(("dp", "tp"), None),
    )
    return jax.shard_map(
        local,
        mesh=mesh,
        in_specs=placed,
        out_specs=(
            P(("dp", "tp"), None),
            P(("dp", "tp"), None),
            P(),
            P(),
            P(None, None, "tp"),
            P("tp", None),
            P(),
            P(),
            P("dp", None, "tp"),
            P("dp", "tp", None),
        ),
        check_vma=False,
    )
```

```python
import functools

import jax
import jax.numpy as jnp
from jax import lax
from jax.experimental import pallas as pl
from jax.experimental.pallas import tpu as pltpu
from jax.sharding import PartitionSpec as P

HEAD_DIM = 64
PACKED_LENGTH = 1024
EPSILON = 1e-05
BF = jnp.bfloat16
F32 = jnp.float32
MASKED = -1e30
CHUNKS = 4


def dot(a, b, ca, cb):
    return lax.dot_general(a, b, (((ca,), (cb,)), ((), ())), preferred_element_type=F32)


def params(mib, **kw):
    return pltpu.CompilerParams(vmem_limit_bytes=mib * 1024 * 1024, **kw)


def cost(flops, nbytes):
    return pl.CostEstimate(flops=int(flops) // 64, bytes_accessed=int(nbytes) // 64, transcendentals=0)


def vmem():
    return pl.BlockSpec(memory_space=pltpu.VMEM)


def hbm():
    return pl.BlockSpec(memory_space=pltpu.HBM)


def smem():
    return pl.BlockSpec(memory_space=pltpu.SMEM)


def norm_parts(values):
    centre = jnp.mean(values, axis=-1, keepdims=True)
    shifted = values - centre
    inverse = lax.rsqrt(jnp.mean(shifted * shifted, axis=-1, keepdims=True) + EPSILON)
    return shifted * inverse, inverse


def norm_back(grad_normed, scaled, inverse, gain):
    grad_scaled = grad_normed * gain
    first = jnp.mean(grad_scaled, axis=-1, keepdims=True)
    second = jnp.mean(grad_scaled * scaled, axis=-1, keepdims=True)
    return inverse * (grad_scaled - first - scaled * second)


def column(row):
    return jnp.transpose(jnp.broadcast_to(row, (8, row.shape[1])))[:, 0:1]


def onehot(places, slots):
    rows = lax.broadcasted_iota(jnp.int32, (slots, places.shape[1]), 0)
    return jnp.where(rows == places, 1.0, 0.0).astype(BF)


def put_chunks(rows, places, outs):
    size = outs[0].shape[0]
    table = onehot(places, size * len(outs))
    for index, out in enumerate(outs):
        out[...] = dot(table[index * size : (index + 1) * size], rows, 1, 0).astype(BF)


def take_chunks(chunks, places):
    size = chunks[0].shape[0]
    table = onehot(places, size * len(chunks))
    total = None
    for index, chunk in enumerate(chunks):
        part = dot(table[index * size : (index + 1) * size], chunk[...], 0, 0)
        total = part if total is None else total + part
    return total


PAD = 64


def dispatch_kernel(
    capacity, info, cot, gate, ids, slots, up, down, out, given, buffer, sems
):
    tile = up.shape[0]
    at = pl.ds(pl.multiple_of(info[0] * tile, tile), tile)
    parts = (slice(0, tile), slice(tile, 2 * tile))
    loads = [
        load(up.at[:, at], buffer.at[parts[0], :], sems.at[0]),
        load(down.at[at, :], buffer.at[parts[1], :], sems.at[1]),
    ]
    rows = (column(gate[...]) * cot[...].astype(F32)).astype(BF)
    size = out.shape[0] // 2
    table = onehot(ids[...] * capacity + slots[...], 2 * size)
    out[0:size, :] = dot(table[0:size], rows, 1, 0).astype(BF)
    stores = []
    for index, part in enumerate(parts):
        loads[index].wait()
        stores.append(load(buffer.at[part, :], given.at[part, :], sems.at[2 + index]))
    out[size:, :] = dot(table[size:], rows, 1, 0).astype(BF)
    for store in stores:
        store.wait()


def dispatch(info, capacity, cotangent, gate, ids, slots, up, down):
    tokens, width = cotangent.shape
    tile = up.shape[0]
    return pl.pallas_call(
        functools.partial(dispatch_kernel, capacity),
        out_shape=[
            jax.ShapeDtypeStruct((2 * tokens, width), BF),
            jax.ShapeDtypeStruct((2 * tile + PAD, tile), BF),
        ],
        in_specs=[smem()] + [vmem()] * 4 + [hbm()] * 2,
        out_specs=[vmem(), hbm()],
        scratch_shapes=[pltpu.VMEM((2 * tile, tile), BF), pltpu.SemaphoreType.DMA((4,))],
        compiler_params=params(60),
        cost_estimate=cost(4 * tokens * tokens * width, 6 * tokens * width),
        name="dispatch",
    )(info, cotangent, gate, ids, slots, up, down)


def load(source, target, sem):
    copy = pltpu.make_async_copy(source, target, sem)
    copy.start()
    return copy


BLOCKS = 2


def attend_kernel(first, heads, info, own, oth, gain, bias, weight, seg_own, seg_oth, *refs):
    parity = info[0]
    half = PACKED_LENGTH // 2
    if first:
        rows, att, probs, qkv, recip, segr, mask, buffer, sems = refs
        for ref, place in ((own, parity), (oth, 1 - parity)):
            scaled, unused = norm_parts(ref[...].astype(F32))
            normed = (scaled * gain[...] + bias[...]).astype(BF)
            rows[pl.ds(pl.multiple_of(place * half, half), half), :] = normed
    else:
        att_a, out_a, out_b, att, probs, qkv, recip, kept, sent = refs[:9]
        segr, mask, buffer, sems, att_buffer, out_buffers = refs[9:]
        fetched = [
            load(att_a, att_buffer, sems.at[BLOCKS]),
            load(out_a, out_buffers.at[0], sems.at[BLOCKS + 1]),
            load(out_b, out_buffers.at[1], sems.at[BLOCKS + 2]),
        ]
        rows = own
    for ref, place in ((seg_own, parity), (seg_oth, 1 - parity)):
        at = pl.ds(pl.multiple_of(place * half, half), half)
        segr[:, at] = jnp.broadcast_to(ref[...].astype(F32), (8, half))
    segc = jnp.transpose(segr[...])[:, 0:1]
    width = heads * HEAD_DIM
    blk = att.shape[1] // BLOCKS
    projected = dot(weight[...], rows[...], 1, 1).astype(BF)
    qkv[...] = projected
    qkv[0:width, :] = projected[0:width] * jnp.asarray(HEAD_DIM**-0.5, BF)
    copies = []
    for index in reversed(range(BLOCKS)):
        upto = (index + 1) * blk
        cols = slice(index * blk, upto)
        keypos = lax.broadcasted_iota(jnp.int32, (upto, blk), 0)
        querypos = lax.broadcasted_iota(jnp.int32, (upto, blk), 1) + index * blk
        allowed = (segc[0:upto, :] == segr[0:1, cols]) & (keypos <= querypos)
        mask[0:upto, :] = jnp.where(allowed, 0.0, MASKED)
        for head in range(heads):
            at = head * HEAD_DIM
            query = qkv[at : at + HEAD_DIM, cols]
            keys = qkv[width + at : width + at + HEAD_DIM, 0:upto]
            values = qkv[2 * width + at : 2 * width + at + HEAD_DIM, 0:upto]
            scores = dot(keys, query, 0, 0) + mask[0:upto, :]
            highest = jnp.max(scores, axis=0, keepdims=True)
            weights = jnp.exp(scores - highest)
            inverse = 1.0 / jnp.sum(weights, axis=0, keepdims=True)
            low = weights.astype(BF)
            buffer[index, head, 0:upto, :] = low
            result = dot(values, low, 1, 0) * inverse
            att[at : at + HEAD_DIM, cols] = result.astype(BF)
            recip[head : head + 1, cols] = inverse
        copy = pltpu.make_async_copy(
            buffer.at[index, :, 0:upto, :], probs.at[index, :, 0:upto, :], sems.at[index]
        )
        copy.start()
        copies.append(copy)
    if not first:
        for copy in fetched:
            copy.wait()
        for ref, place in ((sent, 1 - parity), (kept, parity)):
            cols = pl.ds(pl.multiple_of(place * half, half), half)
            total = dot(att_buffer[:, cols], out_buffers[0], 0, 0)
            total = total + dot(att[:, cols], out_buffers[1], 0, 0)
            ref[...] = total.astype(ref.dtype)
    for copy in copies:
        copy.wait()


def attend(info, first, own, oth, gain, bias, weight, seg_own, seg_oth, *others):
    length = PACKED_LENGTH
    model = own.shape[1]
    width = weight.shape[0] // 3
    heads = width // HEAD_DIM
    blk = length // BLOCKS
    outs = [
        jax.ShapeDtypeStruct((width, length), BF),
        jax.ShapeDtypeStruct((BLOCKS, heads, length, blk), BF),
        jax.ShapeDtypeStruct((3 * width, length), BF),
        jax.ShapeDtypeStruct((8, length), F32),
    ]
    out_specs = [vmem(), hbm(), vmem(), vmem()]
    scratch = [
        pltpu.VMEM((8, length), F32),
        pltpu.VMEM((length, blk), F32),
        pltpu.VMEM((BLOCKS, heads, length, blk), BF),
        pltpu.SemaphoreType.DMA((BLOCKS + 3,)),
    ]
    if first:
        outs = [jax.ShapeDtypeStruct((length, model), BF)] + outs
        out_specs = [vmem()] + out_specs
    else:
        outs = outs + [jax.ShapeDtypeStruct((length // 2, model), d) for d in (BF, F32)]
        out_specs = out_specs + [vmem()] * 2
        scratch += [pltpu.VMEM((width, length), BF), pltpu.VMEM((2, width, model), BF)]
    operands = (own, oth, gain, bias, weight, seg_own, seg_oth)
    return pl.pallas_call(
        functools.partial(attend_kernel, first, heads),
        out_shape=outs,
        in_specs=[smem()] + [vmem()] * len(operands) + [hbm()] * len(others),
        out_specs=out_specs,
        scratch_shapes=scratch,
        compiler_params=params(56),
        cost_estimate=cost(
            6 * length * model * width + 8 * heads * length * length * HEAD_DIM,
            2 * heads * length * length + 6 * length * model,
        ),
        name="attend",
    )(info, *operands, *others)


def middle_kernel(info, tokens, kept, received, gain, bias, places, middle, *outs):
    values = tokens[...].astype(F32) + (kept[...].astype(F32) + received[...])
    middle[...] = values
    scaled, unused = norm_parts(values)
    normed = (scaled * gain[...] + bias[...]).astype(BF)
    put_chunks(normed, places[...], outs)


def middle_call(info, tokens, kept, received, gain, bias, places):
    count, width = tokens.shape
    size = 2 * count // CHUNKS
    return pl.pallas_call(
        middle_kernel,
        out_shape=[jax.ShapeDtypeStruct((count, width), F32)]
        + [jax.ShapeDtypeStruct((size, width), BF)] * CHUNKS,
        in_specs=[smem()] + [vmem()] * 6,
        out_specs=[vmem()] * (1 + CHUNKS),
        compiler_params=params(16),
        cost_estimate=cost(4 * count * count * width, 14 * count * width),
        name="middle",
    )(info, tokens, kept, received, gain, bias, places)


def stage_kernel(info, up, down, up_out, down_out):
    up_out[...] = up[...]
    down_out[...] = down[...]


def stage(info, up, down):
    return pl.pallas_call(
        stage_kernel,
        out_shape=[jax.ShapeDtypeStruct(w.shape, BF) for w in (up, down)],
        in_specs=[smem()] + [vmem()] * 2,
        out_specs=[vmem()] * 2,
        compiler_params=params(12),
        cost_estimate=cost(1, 8 * up.size),
        name="stage",
    )(info, up, down)


def gelu_parts(x):
    z = jnp.abs(x) * (0.5**0.5)
    t = 1.0 / (1.0 + 0.3275911 * z)
    poly = t * (
        0.254829592
        + t * (-0.284496736 + t * (1.421413741 + t * (-1.453152027 + t * 1.061405429)))
    )
    bell = jnp.exp(-0.5 * x * x)
    tail = 0.5 * poly * bell
    phi = jnp.where(x >= 0.0, 1.0 - tail, tail)
    return x * phi, phi + x * bell * 0.3989422804014327


def expert_kernel(chunk, first, info, inputs, grads, own_up, own_down, near, far, *refs):
    if not first:
        refs = refs[1:]
    hidden, gpre, result, given, buffer, grad_buffer, fetched, sems = refs
    size = own_up.shape[0]
    place = info[3] ^ chunk
    copies = [load(grads.at[place], grad_buffer, sems.at[0])]
    copies += [load(ref.at[0 : 2 * size, :], fetched.at[i], sems.at[1 + i]) for i, ref in enumerate((near, far))]
    rows = inputs[...]
    copies[0].wait()
    grad = grad_buffer[...]
    total, forward = None, None
    for tile in range(4):
        if tile < 2:
            at = slice(tile * size, (tile + 1) * size)
            up, down = own_up[:, at], own_down[at, :]
        else:
            copies[tile - 1].wait()
            up, down = fetched[tile - 2, 0:size, :], fetched[tile - 2, size : 2 * size, :]
        at = slice(tile * size, (tile + 1) * size)
        preact = dot(rows, up, 1, 0)
        ghidden = dot(grad, down, 1, 1)
        act, slope = gelu_parts(preact)
        act = act.astype(BF)
        hidden[:, at] = act
        low = (ghidden * slope).astype(BF)
        gpre[:, at] = low
        part = dot(low, up, 1, 1)
        total = part if total is None else total + part
        part = dot(act, down, 1, 0)
        forward = part if forward is None else forward + part
    buffer[...] = forward.astype(BF)
    copy = load(buffer, given.at[place], sems.at[3])
    result[...] = total.astype(BF)
    copy.wait()


def expert(info, chunk, inputs, grads, weights, given=None):
    rows, model = inputs.shape
    tile = weights[0].shape[0]
    operands = [info, inputs, grads, *weights]
    in_specs = [smem(), vmem(), hbm(), vmem(), vmem(), hbm(), hbm()]
    if given is not None:
        operands.append(given)
        in_specs.append(hbm())
    return pl.pallas_call(
        functools.partial(expert_kernel, chunk, given is None),
        out_shape=[
            jax.ShapeDtypeStruct((rows, 4 * tile), BF),
            jax.ShapeDtypeStruct((rows, 4 * tile), BF),
            jax.ShapeDtypeStruct((rows, model), BF),
            jax.ShapeDtypeStruct(grads.shape, BF),
        ],
        in_specs=in_specs,
        out_specs=[vmem()] * 3 + [hbm()],
        scratch_shapes=[
            pltpu.VMEM((rows, model), BF),
            pltpu.VMEM((rows, model), BF),
            pltpu.VMEM((2, 2 * tile, model), BF),
            pltpu.SemaphoreType.DMA((4,)),
        ],
        input_output_aliases={} if given is None else {7: 3},
        compiler_params=params(20),
        cost_estimate=cost(32 * rows * model * tile, 16 * model * tile + 16 * rows * tile),
        name="expert",
    )(*operands)


GIVEN = (3, 3, 2)


def piece_at(theirs, other):
    return 2 * theirs + other, 4 + 2 * other + theirs


def given_at(piece):
    for which, number in enumerate(GIVEN):
        if piece < number:
            return which, piece
        piece -= number


def expert_weights_kernel(info, grads, *refs):
    n = CHUNKS
    inputs, hiddens, gpres = refs[:n], refs[n : 2 * n], refs[2 * n : 3 * n]
    stays, given = refs[3 * n], refs[3 * n + 1 : 3 * n + 4]
    sub = stays.shape[1]
    size = 2 * sub
    parity, row_half, here = info[0], info[1], info[3]
    mine = pl.multiple_of(parity * sub, sub)
    gone = pl.multiple_of((1 - parity) * sub, sub)
    for theirs in range(2):
        for other in range(2):
            tile = other ^ row_half
            if theirs:
                tile = 2 + (tile ^ parity)
            for offset, keeps in ((mine, True), (gone, False)):
                at = pl.ds(pl.multiple_of(tile * size + offset, sub), sub)
                for is_down, piece in enumerate(piece_at(theirs, other)):
                    total = None
                    for index in range(n):
                        source = (hiddens if is_down else gpres)[index][:, at]
                        factor = grads[here ^ index] if is_down else inputs[index][...]
                        part = dot(source, factor, 0, 0)
                        total = part if total is None else total + part
                    which, place = given_at(piece)
                    if keeps:
                        stays[piece] = total.astype(BF)
                    else:
                        given[which][place] = total.astype(BF)


def expert_weights(info, inputs, grads, hiddens, gpres):
    rows, model = inputs[0].shape
    sub = hiddens[0].shape[1] // 8
    return pl.pallas_call(
        expert_weights_kernel,
        out_shape=[jax.ShapeDtypeStruct((m, sub, model), BF) for m in (8, *GIVEN)],
        in_specs=[smem()] + [vmem()] * (1 + 3 * CHUNKS),
        out_specs=[vmem()] * 4,
        compiler_params=params(20),
        cost_estimate=cost(32 * CHUNKS * rows * model * sub, 64 * model * sub),
        name="expert_weights",
    )(info, grads, *inputs, *hiddens, *gpres)


def pieces_kernel(info, stays, first, second, third, kept, sent_one, sent_two, sent_down):
    received = (first, second, third)
    for ref, pieces in (
        (kept, (0, 1, 4, 5)),
        (sent_one, (2,)),
        (sent_two, (3,)),
        (sent_down, (6, 7)),
    ):
        for index, piece in enumerate(pieces):
            which, place = given_at(piece)
            total = stays[piece].astype(F32) + received[which][place].astype(F32)
            ref[index] = total.astype(BF)


def add_pieces(info, stays, *received):
    n, sub, model = stays.shape
    return pl.pallas_call(
        pieces_kernel,
        out_shape=[jax.ShapeDtypeStruct((m, sub, model), BF) for m in (4, 1, 1, 2)],
        in_specs=[smem()] + [vmem()] * 4,
        out_specs=[vmem()] * 4,
        compiler_params=params(20),
        cost_estimate=cost(stays.size, 6 * stays.size),
        name="add_pieces",
    )(info, stays, *received)


def more_pieces_kernel(info, kept, one, two, got_down, up, down, sent_up, sent_down):
    for index, got, ref in (
        (0, one.at[0], up),
        (1, two.at[0], sent_up),
        (2, got_down.at[0], down),
        (3, got_down.at[1], sent_down),
    ):
        ref[...] = (kept[index].astype(F32) + got[...].astype(F32)).astype(BF)


def more_pieces(info, kept, *got):
    n, sub, model = kept.shape
    return pl.pallas_call(
        more_pieces_kernel,
        out_shape=[jax.ShapeDtypeStruct((sub, model), BF)] * 4,
        in_specs=[smem()] + [vmem()] * 4,
        out_specs=[vmem()] * 4,
        compiler_params=params(60),
        cost_estimate=cost(kept.size, 6 * kept.size),
        name="more_pieces",
    )(info, kept, *got)


def last_pieces_kernel(info, up, down, got_up, got_down, grad_up, grad_down):
    grad_up[...] = jnp.transpose(up[...].astype(F32) + got_up[...].astype(F32))
    grad_down[...] = down[...].astype(F32) + got_down[...].astype(F32)


def last_pieces(info, up, down, got_up, got_down):
    sub, model = up.shape
    return pl.pallas_call(
        last_pieces_kernel,
        out_shape=[
            jax.ShapeDtypeStruct((model, sub), F32),
            jax.ShapeDtypeStruct((sub, model), F32),
        ],
        in_specs=[smem()] + [vmem()] * 4,
        out_specs=[vmem()] * 2,
        compiler_params=params(60),
        cost_estimate=cost(up.size, 16 * up.size),
        name="last_pieces",
    )(info, up, down, got_up, got_down)


def second_back_kernel(info, *refs):
    chunks = refs[:CHUNKS]
    middle, cot, gain, places, gmid, gvec = refs[CHUNKS:]
    grad = take_chunks(chunks, places[...])
    scaled, inverse = norm_parts(middle[...])
    total = cot[...].astype(F32) + norm_back(grad, scaled, inverse, gain[...])
    gmid[...] = total
    gvec[...] = jnp.zeros_like(gvec)
    gvec[0:1, :] = jnp.sum(grad * scaled, axis=0, keepdims=True)
    gvec[1:2, :] = jnp.sum(grad, axis=0, keepdims=True)


def second_back(info, chunks, middle, cotangent, gain, places):
    count, width = cotangent.shape
    return pl.pallas_call(
        second_back_kernel,
        out_shape=[
            jax.ShapeDtypeStruct((count, width), F32),
            jax.ShapeDtypeStruct((8, width), F32),
        ],
        in_specs=[smem()] + [vmem()] * (CHUNKS + 4),
        out_specs=[vmem()] * 2,
        compiler_params=params(16),
        cost_estimate=cost(4 * count * count * width, 16 * count * width),
        name="second_back",
    )(info, *chunks, middle, cotangent, gain, places)


def output_kernel(info, results, middle, gate, places, out):
    total = take_chunks([results], places[...])
    out[...] = (middle[...] + column(gate[...]) * total).astype(BF)


def output_call(info, results, middle, gate, places):
    return pl.pallas_call(
        output_kernel,
        out_shape=jax.ShapeDtypeStruct(middle.shape, BF),
        in_specs=[smem()] + [vmem()] * 4,
        out_specs=vmem(),
        compiler_params=params(60),
        cost_estimate=cost(4 * middle.shape[0] * middle.size, 8 * middle.size),
        name="output",
    )(info, results, middle, gate, places)


def load_probs(probs, buffer, sems):
    copies = []
    blk = buffer.shape[3]
    for index in range(BLOCKS):
        upto = (index + 1) * blk
        copy = pltpu.make_async_copy(
            probs.at[index, :, 0:upto, :], buffer.at[index, :, 0:upto, :], sems.at[index]
        )
        copy.start()
        copies.append(copy)
    return copies


def back_values_kernel(info, own, oth, rows, *refs):
    outws, atts, recips, probs = refs[0:2], refs[2:4], refs[4:6], refs[6:8]
    outs = refs[8:16]
    gbranch, gsum, row_buffer, sems = refs[16:18] + refs[20:22]
    buffers = refs[18:20]
    copies = [load_probs(probs[g], buffers[g], sems.at[g]) for g in range(2)]
    row_copy = load(rows, row_buffer, sems.at[0, BLOCKS])
    length = PACKED_LENGTH
    width = atts[0].shape[0]
    blk = length // BLOCKS
    half = length // 2
    parity = info[0]
    for ref, place in ((own, parity), (oth, 1 - parity)):
        gbranch[pl.ds(pl.multiple_of(place * half, half), half), :] = ref[...].astype(BF)
    for g in range(2):
        scaled_ref, inner_ref, gvalues, gweight = outs[4 * g : 4 * g + 4]
        att, recip, buffer = atts[g], recips[g], buffers[g]
        gatt = dot(outws[g][...], gbranch[...], 1, 1).astype(BF).astype(F32)
        for head in range(width // HEAD_DIM):
            at = slice(head * HEAD_DIM, (head + 1) * HEAD_DIM)
            scaled = (gatt[at] * recip[head : head + 1, :]).astype(BF)
            scaled_ref[at, :] = scaled
            inner_ref[head : head + 1, :] = jnp.sum(
                scaled.astype(F32) * att[at, :].astype(F32), axis=0, keepdims=True
            )
        gweight[width:, :] = dot(att[...], gbranch[...], 1, 0).astype(BF)
        gsum[...] = jnp.zeros_like(gsum)
        for index in range(BLOCKS):
            upto = (index + 1) * blk
            cols = slice(index * blk, upto)
            copies[g][index].wait()
            for head in range(width // HEAD_DIM):
                at = slice(head * HEAD_DIM, (head + 1) * HEAD_DIM)
                low = buffer[index, head, 0:upto, :]
                gsum[at, 0:upto] += dot(scaled_ref[at, cols], low, 1, 1)
        low = gsum[...].astype(BF)
        gvalues[...] = low
        if g == 0:
            row_copy.wait()
        gweight[0:width, :] = dot(low, row_buffer[...], 1, 0).astype(BF)


def back_values(info, own, oth, rows, outws, atts, recips, probs):
    length, model = rows.shape
    width = atts[0].shape[0]
    heads = width // HEAD_DIM
    shapes = [((width, length), BF), ((8, length), F32), ((width, length), BF)]
    shapes.append(((2 * width, model), BF))
    shapes = shapes * 2
    kept = pltpu.VMEM((BLOCKS, heads, length, length // BLOCKS), BF)
    outs = pl.pallas_call(
        back_values_kernel,
        out_shape=[jax.ShapeDtypeStruct(s, d) for s, d in shapes],
        in_specs=[smem()] + [vmem()] * 2 + [hbm()] + [vmem()] * 6 + [hbm()] * 2,
        out_specs=[vmem()] * len(shapes),
        scratch_shapes=[
            pltpu.VMEM((length, model), BF),
            pltpu.VMEM((width, length), F32),
            kept,
            kept,
            pltpu.VMEM((length, model), BF),
            pltpu.SemaphoreType.DMA((2, BLOCKS + 1)),
        ],
        compiler_params=params(56),
        cost_estimate=cost(
            16 * length * model * width + 8 * heads * length * length * HEAD_DIM,
            4 * heads * length * length + 10 * length * model,
        ),
        name="back_values",
    )(info, own, oth, rows, *outws, *atts, *recips, *probs)
    return outs


def back_keys_kernel(info, qkv, scaled, inner, gvalues, rows, probs, gweight, gqkv, *scratch):
    gsum, buffer, row_buffer, sems = scratch
    copies = load_probs(probs, buffer, sems)
    row_copy = load(rows, row_buffer, sems.at[BLOCKS])
    length = PACKED_LENGTH
    width = scaled.shape[0]
    blk = length // BLOCKS
    gsum[...] = jnp.zeros_like(gsum)
    for index in range(BLOCKS):
        upto = (index + 1) * blk
        cols = slice(index * blk, upto)
        copies[index].wait()
        for head in range(width // HEAD_DIM):
            at = head * HEAD_DIM
            here = slice(at, at + HEAD_DIM)
            kat = slice(width + at, width + at + HEAD_DIM)
            vat = slice(2 * width + at, 2 * width + at + HEAD_DIM)
            gprobs = dot(qkv[vat, 0:upto], scaled[here, cols], 0, 0)
            low = buffer[index, head, 0:upto, :].astype(F32)
            gscores = (low * (gprobs - inner[head : head + 1, cols])).astype(BF)
            gsum[here, 0:upto] += dot(qkv[here, cols], gscores, 1, 1)
            gqueries = dot(qkv[kat, 0:upto], gscores, 1, 0) * HEAD_DIM**-0.5
            gqkv[here, cols] = gqueries.astype(BF)
    gqkv[width : 2 * width, :] = gsum[...].astype(BF)
    gqkv[2 * width :, :] = gvalues[...]
    row_copy.wait()
    gweight[...] = dot(gqkv[0 : 2 * width, :], row_buffer[...], 1, 0).astype(BF)


def back_keys(info, qkv, scaled, inner, gvalues, rows, probs):
    length, model = rows.shape
    width = scaled.shape[0]
    heads = width // HEAD_DIM
    return pl.pallas_call(
        back_keys_kernel,
        out_shape=[
            jax.ShapeDtypeStruct((2 * width, model), BF),
            jax.ShapeDtypeStruct((3 * width, length), BF),
        ],
        in_specs=[smem()] + [vmem()] * 4 + [hbm()] * 2,
        out_specs=[vmem()] * 2,
        scratch_shapes=[
            pltpu.VMEM((width, length), F32),
            pltpu.VMEM((BLOCKS, heads, length, length // BLOCKS), BF),
            pltpu.VMEM((length, model), BF),
            pltpu.SemaphoreType.DMA((BLOCKS + 1,)),
        ],
        compiler_params=params(56),
        cost_estimate=cost(
            4 * length * model * width + 12 * heads * length * length * HEAD_DIM,
            2 * heads * length * length + 10 * length * model,
        ),
        name="back_keys",
    )(info, qkv, scaled, inner, gvalues, rows, probs)


def back_rows_kernel(info, gqkv_a, gqkv_b, weight_a, weight_b, kept, sent_low, sent_high):
    half = kept.shape[0]
    parity = info[0]
    for refs, place in (((sent_low, sent_high), 1 - parity), ((kept,), parity)):
        at = pl.ds(pl.multiple_of(place * half, half), half)
        total = dot(gqkv_a[:, at], weight_a[...], 0, 0) + dot(gqkv_b[:, at], weight_b[...], 0, 0)
        size = half // len(refs)
        for index, ref in enumerate(refs):
            ref[...] = total[index * size : (index + 1) * size].astype(ref.dtype)


def back_rows(info, gqkv_a, gqkv_b, weight_a, weight_b):
    length = gqkv_a.shape[1]
    model = weight_a.shape[1]
    return pl.pallas_call(
        back_rows_kernel,
        out_shape=[
            jax.ShapeDtypeStruct((length // 2, model), BF),
            jax.ShapeDtypeStruct((length // 4, model), BF),
            jax.ShapeDtypeStruct((length // 4, model), BF),
        ],
        in_specs=[smem()] + [vmem()] * 4,
        out_specs=[vmem()] * 3,
        compiler_params=params(60),
        cost_estimate=cost(4 * length * model * gqkv_a.shape[0], 6 * length * model),
        name="back_rows",
    )(info, gqkv_a, gqkv_b, weight_a, weight_b)


def first_back_kernel(info, tokens, gmid, kept, low, high, gain, second, ginput, gvec):
    received = jnp.concatenate([low[...], high[...]], axis=0)
    grad = kept[...].astype(F32) + received.astype(F32)
    scaled, inverse = norm_parts(tokens[...].astype(F32))
    ginput[...] = gmid[...] + norm_back(grad, scaled, inverse, gain[...])
    gvec[...] = jnp.zeros_like(gvec)
    gvec[2:4, :] = second[0:2, :]
    gvec[0:1, :] = jnp.sum(grad * scaled, axis=0, keepdims=True)
    gvec[1:2, :] = jnp.sum(grad, axis=0, keepdims=True)


def first_back(info, tokens, gmid, kept, low, high, gain, second):
    count, width = tokens.shape
    return pl.pallas_call(
        first_back_kernel,
        out_shape=[
            jax.ShapeDtypeStruct((count, width), F32),
            jax.ShapeDtypeStruct((8, width), F32),
        ],
        in_specs=[smem()] + [vmem()] * 7,
        out_specs=[vmem()] * 2,
        compiler_params=params(60),
        cost_estimate=cost(20 * count * width, 16 * count * width),
        name="first_back",
    )(info, tokens, gmid, kept, low, high, gain, second)


def first_sum_kernel(info, mine, theirs, kept, sent):
    half = kept.shape[0]
    k = info[2]
    for ref, which in ((sent, 1 - k), (kept, k)):
        at = pl.ds(pl.multiple_of(which * half, half), half)
        ref[...] = (mine[at, :].astype(F32) + theirs[at, :].astype(F32)).astype(ref.dtype)


def first_sum(info, mine, theirs):
    rows, model = mine.shape
    return pl.pallas_call(
        first_sum_kernel,
        out_shape=[
            jax.ShapeDtypeStruct((rows // 2, model), F32),
            jax.ShapeDtypeStruct((rows // 2, model), BF),
        ],
        in_specs=[smem()] + [vmem()] * 2,
        out_specs=[vmem()] * 2,
        compiler_params=params(60),
        cost_estimate=cost(rows * model, 7 * rows * model),
        name="first_sum",
    )(info, mine, theirs)


def second_sum_kernel(info, kept, received, out):
    out[...] = (kept[...] + received[...].astype(F32)).astype(BF)


def second_sum(info, kept, received):
    return pl.pallas_call(
        second_sum_kernel,
        out_shape=jax.ShapeDtypeStruct(kept.shape, BF),
        in_specs=[smem()] + [vmem()] * 2,
        out_specs=vmem(),
        compiler_params=params(60),
        cost_estimate=cost(kept.size, 8 * kept.size),
        name="second_sum",
    )(info, kept, received)


def sum_blocks(blocks):
    total = None
    for index in range(blocks.shape[0]):
        block = blocks[index].astype(F32)
        total = block if total is None else total + block
    return total.astype(BF)


def middle_sum_kernel(info, blocks, kept, received, out):
    rows = blocks.shape[1]
    total = sum_blocks(blocks)
    for index in range(out.shape[0]):
        at = slice(index * rows, (index + 1) * rows)
        out[index, 0:rows] = total
        out[index, rows:] = (kept[at, :] + received[at, :].astype(F32)).astype(BF)


def middle_sum(info, blocks, kept, received):
    pieces, rows, model = blocks.shape
    return pl.pallas_call(
        middle_sum_kernel,
        out_shape=jax.ShapeDtypeStruct((pieces, 2 * rows, model), BF),
        in_specs=[smem()] + [vmem()] * 3,
        out_specs=vmem(),
        compiler_params=params(60),
        cost_estimate=cost(kept.size, 8 * kept.size),
        name="middle_sum",
    )(info, blocks, kept, received)


def third_sum_kernel(info, blocks, vectors, more, out, other):
    pieces, rows = other.shape[0:2]
    total = None
    for index in range(pieces):
        other[index] = blocks[index, 0:rows]
        block = blocks[index, rows:].astype(F32)
        total = block if total is None else total + block
    total = total.astype(BF)
    values = vectors[...] + more[...]
    high = values.astype(BF)
    low = (values - high.astype(F32)).astype(BF)
    both = jnp.concatenate([high, low], axis=0)
    for index in range(pieces):
        out[index, 0:rows] = total
        out[index, rows:] = both


def third_sum(info, blocks, vectors, more):
    pieces, rows, model = blocks.shape
    extra = 2 * vectors.shape[0]
    return pl.pallas_call(
        third_sum_kernel,
        out_shape=[
            jax.ShapeDtypeStruct((pieces, rows // 2 + extra, model), BF),
            jax.ShapeDtypeStruct((pieces, rows // 2, model), BF),
        ],
        in_specs=[smem()] + [vmem()] * 3,
        out_specs=[vmem()] * 2,
        compiler_params=params(60),
        cost_estimate=cost(blocks.size, 4 * blocks.size),
        name="third_sum",
    )(info, blocks, vectors, more)


def last_kernel(info, mine_qk, theirs_qk, mine_vo, theirs_vo, qkv, out, *vectors):
    width = mine_vo.shape[0]
    pieces = mine_qk.shape[0]
    rows = width // pieces
    count = (mine_qk.shape[1] - rows) // 2
    k = info[2]

    def write(queries, keys, values, outs):
        for index in range(pieces):
            at = index * rows
            qkv[at : at + rows, :] = queries[index, 0:rows].astype(F32)
            qkv[width + at : width + at + rows, :] = keys[index, 0:rows].astype(F32)
        qkv[2 * width :, :] = values[...].astype(F32)
        out[...] = outs[...].astype(F32)

    @pl.when(k == 0)
    def even():
        write(mine_qk, theirs_qk, mine_vo, theirs_vo)

    @pl.when(k != 0)
    def odd():
        write(theirs_qk, mine_qk, theirs_vo, mine_vo)

    sums = []
    for ref in (mine_qk, theirs_qk):
        total = None
        for index in range(pieces):
            both = ref[index, rows:].astype(F32)
            value = both[0:count] + both[count:]
            total = value if total is None else total + value
        sums.append(total)
    for index, ref in enumerate(vectors):
        ref[...] = sums[0][index] + sums[1][index]


def last(info, mine_qk, theirs_qk, mine_vo, theirs_vo):
    width, model = mine_vo.shape
    return pl.pallas_call(
        last_kernel,
        out_shape=[
            jax.ShapeDtypeStruct((3 * width, model), F32),
            jax.ShapeDtypeStruct((width, model), F32),
        ]
        + [jax.ShapeDtypeStruct((model,), F32)] * 4,
        in_specs=[smem()] + [vmem()] * 4,
        out_specs=[vmem()] * 6,
        compiler_params=params(60),
        cost_estimate=cost(width * model, 24 * width * model),
        name="last",
    )(info, mine_qk, theirs_qk, mine_vo, theirs_vo)


def after(values, *others):
    return lax.optimization_barrier((values, *others))[0]


def swap(values, axis, bit):
    pairs = [(i, i ^ bit) for i in range(lax.axis_size(axis))]
    return lax.ppermute(values, axis, pairs)


def exchange(values, count):
    groups = [[2 * e + k for e in range(count)] for k in range(2)]
    shaped = values.reshape(count, -1, values.shape[1])
    moved = lax.all_to_all(shaped, "dp", 0, 0, tiled=True, axis_index_groups=groups)
    return moved.reshape(values.shape)


def exchange_chunks(chunks, count):
    moved = exchange(jnp.concatenate(chunks, axis=0), count)
    size = chunks[0].shape[0]
    return [moved[i * size : (i + 1) * size] for i in range(len(chunks))]


def local(
    tokens,
    first_gain,
    first_bias,
    qkv_weight,
    out_weight,
    second_gain,
    expert_norm_bias,
    up_weight,
    down_weight,
    gate_value,
    expert_ids,
    slot_index,
    segment_ids,
    cotangent,
):
    count, model = tokens.shape
    width = qkv_weight.shape[2]
    tp = lax.axis_index("tp")
    dp = lax.axis_index("dp")
    parity = tp % 2
    row_half = tp // 2 % 2
    k = dp % 2
    experts = lax.axis_size("dp") // 2
    capacity = 2 * count // experts
    paired = experts == CHUNKS
    here = dp // 2 if paired else 0 * dp
    info = jnp.stack([parity, row_half, k, here]).astype(jnp.int32)
    vector = lambda v: v.reshape(1, -1)
    gain, bias = first_gain, first_bias

    state = [info]

    def run(call, *operands):
        outs = call(state[0], *operands)
        state[0] = after(info, outs[-1] if isinstance(outs, (list, tuple)) else outs)
        return outs

    other_tokens = swap(tokens, "tp", 1)
    other_segments = swap(segment_ids, "tp", 1)
    weight_a = jnp.transpose(qkv_weight, (1, 2, 0)).reshape(3 * width, model)
    weight_b = swap(weight_a, "tp", 2)
    out_b = swap(out_weight, "tp", 2)
    up, down = up_weight[0], down_weight[0]
    gate = vector(gate_value)
    slots = vector(expert_ids * capacity + slot_index)
    sent_grads, given = run(
        dispatch, capacity, cotangent, gate, vector(expert_ids), vector(slot_index), up, down
    )
    near = swap(given, "dp", 1)
    grads = exchange(sent_grads, experts).reshape(CHUNKS, -1, model)

    segments = (vector(segment_ids), vector(other_segments))
    rows, att_a, probs_a, qkv_a, recip_a = run(
        attend, True, tokens, other_tokens, gain, bias, weight_a, *segments
    )
    att_b, probs_b, qkv_b, recip_b, kept, sent = run(
        attend, False, rows, vector(other_segments), gain, bias, weight_b, *segments,
        att_a, out_weight, out_b,
    )
    received = swap(sent, "tp", 1)
    places = vector((expert_ids ^ here) * capacity + slot_index)
    middle, *sent_rows = run(
        middle_call, tokens, kept, received, second_gain, expert_norm_bias, places
    )

    if paired:
        first, second = lax.optimization_barrier(
            (swap(sent_rows[1], "dp", 2), swap(sent_rows[2], "dp", 4))
        )
        third = swap(after(sent_rows[3], second), "dp", 6)
        inputs = [sent_rows[0], first, second, third]
    else:
        inputs = exchange_chunks(sent_rows, experts)
    far = swap(after(near, inputs[1], grads), "tp", 1)
    weights = (*run(stage, up, down), near, far)
    hiddens, gpres, backs = [[None] * CHUNKS for unused in range(3)]
    results = None
    for index in (*range(1, CHUNKS), 0):
        hiddens[index], gpres[index], backs[index], results = run(
            expert, index, inputs[index], grads, weights, results
        )
    if paired:
        returned = [backs[0]] + [swap(backs[s], "dp", 2 * s) for s in range(1, CHUNKS)]
    else:
        returned = exchange_chunks(backs, experts)
    if paired:
        inputs[0], returned[1] = lax.optimization_barrier((inputs[0], returned[1]))
    stays, *leaves = run(expert_weights, inputs, grads, hiddens, gpres)
    leaves = [swap(leaf, "tp", 1) for leaf in leaves]
    gmid, gvec_two = run(
        second_back, returned, middle, cotangent, second_gain, places
    )
    other_gmid = swap(gmid, "tp", 1)
    outs = exchange(after(results, gmid).reshape(-1, model), experts)

    values = run(
        back_values, gmid, other_gmid, rows, (out_b, out_weight), (att_b, att_a),
        (recip_b, recip_a), (probs_b, probs_a),
    )
    scaled_b, inner_b, gvalues_b, gvo_b = values[0:4]
    scaled_a, inner_a, gvalues_a, gvo_a = values[4:8]
    theirs_vo = swap(gvo_b, "tp", 2)
    kept_pieces, sent_one, sent_two, sent_down = run(add_pieces, stays, *leaves)
    got_one = swap(sent_one, "dp", 1)
    gqk_b, gqkv_b = run(back_keys, qkv_b, scaled_b, inner_b, gvalues_b, rows, probs_b)
    theirs_qk = swap(gqk_b, "tp", 2)
    vo_kept, vo_sent = run(first_sum, gvo_a, theirs_vo)
    vo_received = swap(vo_sent, "dp", 1)
    gqk_a, gqkv_a = run(back_keys, qkv_a, scaled_a, inner_a, gvalues_a, rows, probs_a)
    got_two = swap(after(sent_two, gqk_a), "dp", 1)
    got_down = swap(after(sent_down, gqk_a), "tp", 2)

    def over_experts(blocks):
        moved = exchange(blocks.reshape(-1, model), experts)
        return moved.reshape(experts, -1, model)

    blocks_vo = over_experts(run(second_sum, vo_kept, after(vo_received, outs, got_one)))
    qk_kept, qk_sent = run(first_sum, gqk_a, theirs_qk)
    qk_received = swap(qk_sent, "dp", 1)
    gkept, *gsent = run(back_rows, gqkv_a, gqkv_b, weight_a, weight_b)
    greceived = [swap(g, "tp", 1) for g in gsent]
    blocks = over_experts(run(middle_sum, after(blocks_vo, got_two), qk_kept, qk_received))
    up_kept, down_kept, sent_up, sent_down = run(
        more_pieces, kept_pieces, got_one, got_two, got_down
    )
    last_down = swap(sent_down, "dp", 1)
    grad_input, vectors = run(first_back, tokens, gmid, gkept, *greceived, gain, gvec_two)
    vectors = vectors + swap(vectors, "tp", 1)
    more_vectors = swap(vectors, "tp", 2)
    last_up = swap(after(sent_up, more_vectors), "tp", 2)
    total_qk, full_vo = run(third_sum, blocks, vectors, more_vectors)
    full_qk = over_experts(total_qk)
    full_vo = full_vo.reshape(width, model)
    other_vo = swap(after(full_vo, last_down), "dp", 1)
    output = run(output_call, outs, middle, gate, slots)
    full_qk, other_vo = lax.optimization_barrier((full_qk, other_vo))
    other_qk = swap(full_qk, "dp", 1)
    grad_up, grad_down = run(last_pieces, up_kept, down_kept, last_up, last_down)
    grad_qkv, grad_out, *vectors = run(last, full_qk, other_qk, full_vo, other_vo)
    grad_qkv = jnp.transpose(grad_qkv.reshape(3, width, model), (2, 0, 1))
    return (
        output,
        grad_input,
        vectors[0],
        vectors[1],
        grad_qkv,
        grad_out,
        vectors[2],
        vectors[3],
        grad_up[None],
        grad_down[None],
    )


def solution(mesh):
    placed = (
        P(("dp", "tp"), None),
        P(),
        P(),
        P(None, None, "tp"),
        P("tp", None),
        P(),
        P(),
        P("dp", None, None),
        P("dp", None, None),
        P(("dp", "tp")),
        P(("dp", "tp")),
        P(("dp", "tp")),
        P(("dp", "tp")),
        P(("dp", "tp"), None),
    )
    return jax.shard_map(
        local,
        mesh=mesh,
        in_specs=placed,
        out_specs=(
            P(("dp", "tp"), None),
            P(("dp", "tp"), None),
            P(),
            P(),
            P(None, None, "tp"),
            P("tp", None),
            P(),
            P(),
            P("dp", None, "tp"),
            P("dp", "tp", None),
        ),
        check_vma=False,
    )
```

```python
import functools

import jax
import jax.numpy as jnp
from jax import lax
from jax.experimental import pallas as pl
from jax.experimental.pallas import tpu as pltpu
from jax.sharding import PartitionSpec as P

HEAD_DIM = 64
PACKED_LENGTH = 1024
EPSILON = 1e-05
BF = jnp.bfloat16
F32 = jnp.float32
MASKED = -1e30
CHUNKS = 4


def dot(a, b, ca, cb):
    return lax.dot_general(a, b, (((ca,), (cb,)), ((), ())), preferred_element_type=F32)


def params(mib, **kw):
    return pltpu.CompilerParams(vmem_limit_bytes=mib * 1024 * 1024, **kw)


def cost(flops, nbytes):
    return pl.CostEstimate(flops=int(flops) // 64, bytes_accessed=int(nbytes) // 64, transcendentals=0)


def vmem():
    return pl.BlockSpec(memory_space=pltpu.VMEM)


def hbm():
    return pl.BlockSpec(memory_space=pltpu.HBM)


def smem():
    return pl.BlockSpec(memory_space=pltpu.SMEM)


def norm_parts(values):
    centre = jnp.mean(values, axis=-1, keepdims=True)
    shifted = values - centre
    inverse = lax.rsqrt(jnp.mean(shifted * shifted, axis=-1, keepdims=True) + EPSILON)
    return shifted * inverse, inverse


def norm_back(grad_normed, scaled, inverse, gain):
    grad_scaled = grad_normed * gain
    first = jnp.mean(grad_scaled, axis=-1, keepdims=True)
    second = jnp.mean(grad_scaled * scaled, axis=-1, keepdims=True)
    return inverse * (grad_scaled - first - scaled * second)


def column(row):
    return jnp.transpose(jnp.broadcast_to(row, (8, row.shape[1])))[:, 0:1]


def onehot(places, slots):
    rows = lax.broadcasted_iota(jnp.int32, (slots, places.shape[1]), 0)
    return jnp.where(rows == places, 1.0, 0.0).astype(BF)


def put_chunks(rows, places, outs):
    size = outs[0].shape[0]
    table = onehot(places, size * len(outs))
    for index, out in enumerate(outs):
        out[...] = dot(table[index * size : (index + 1) * size], rows, 1, 0).astype(BF)


def take_chunks(chunks, places):
    size = chunks[0].shape[0]
    table = onehot(places, size * len(chunks))
    total = None
    for index, chunk in enumerate(chunks):
        part = dot(table[index * size : (index + 1) * size], chunk[...], 0, 0)
        total = part if total is None else total + part
    return total


PAD = 64


def dispatch_kernel(
    capacity, info, cot, gate, ids, slots, up, down, out, given, buffer, sems
):
    tile = up.shape[0]
    at = pl.ds(pl.multiple_of(info[0] * tile, tile), tile)
    parts = (slice(0, tile), slice(tile, 2 * tile))
    loads = [
        load(up.at[:, at], buffer.at[parts[0], :], sems.at[0]),
        load(down.at[at, :], buffer.at[parts[1], :], sems.at[1]),
    ]
    rows = (column(gate[...]) * cot[...].astype(F32)).astype(BF)
    size = out.shape[0] // 2
    table = onehot(ids[...] * capacity + slots[...], 2 * size)
    out[0:size, :] = dot(table[0:size], rows, 1, 0).astype(BF)
    stores = []
    for index, part in enumerate(parts):
        loads[index].wait()
        stores.append(load(buffer.at[part, :], given.at[part, :], sems.at[2 + index]))
    out[size:, :] = dot(table[size:], rows, 1, 0).astype(BF)
    for store in stores:
        store.wait()


def dispatch(info, capacity, cotangent, gate, ids, slots, up, down):
    tokens, width = cotangent.shape
    tile = up.shape[0]
    return pl.pallas_call(
        functools.partial(dispatch_kernel, capacity),
        out_shape=[
            jax.ShapeDtypeStruct((2 * tokens, width), BF),
            jax.ShapeDtypeStruct((2 * tile + PAD, tile), BF),
        ],
        in_specs=[smem()] + [vmem()] * 4 + [hbm()] * 2,
        out_specs=[vmem(), hbm()],
        scratch_shapes=[pltpu.VMEM((2 * tile, tile), BF), pltpu.SemaphoreType.DMA((4,))],
        compiler_params=params(60),
        cost_estimate=cost(4 * tokens * tokens * width, 6 * tokens * width),
        name="dispatch",
    )(info, cotangent, gate, ids, slots, up, down)


def load(source, target, sem):
    copy = pltpu.make_async_copy(source, target, sem)
    copy.start()
    return copy


BLOCKS = 2


def attend_kernel(first, heads, info, own, oth, gain, bias, weight, seg_own, seg_oth, *refs):
    parity = info[0]
    half = PACKED_LENGTH // 2
    if first:
        rows, att, probs, qkv, recip, segr, mask, buffer, sems = refs
        for ref, place in ((own, parity), (oth, 1 - parity)):
            scaled, unused = norm_parts(ref[...].astype(F32))
            normed = (scaled * gain[...] + bias[...]).astype(BF)
            rows[pl.ds(pl.multiple_of(place * half, half), half), :] = normed
    else:
        att_a, out_a, out_b, att, probs, qkv, recip, kept, sent = refs[:9]
        segr, mask, buffer, sems, att_buffer, out_buffers = refs[9:]
        fetched = [
            load(att_a, att_buffer, sems.at[BLOCKS]),
            load(out_a, out_buffers.at[0], sems.at[BLOCKS + 1]),
            load(out_b, out_buffers.at[1], sems.at[BLOCKS + 2]),
        ]
        rows = own
    for ref, place in ((seg_own, parity), (seg_oth, 1 - parity)):
        at = pl.ds(pl.multiple_of(place * half, half), half)
        segr[:, at] = jnp.broadcast_to(ref[...].astype(F32), (8, half))
    segc = jnp.transpose(segr[...])[:, 0:1]
    width = heads * HEAD_DIM
    blk = att.shape[1] // BLOCKS
    projected = dot(weight[...], rows[...], 1, 1).astype(BF)
    qkv[...] = projected
    qkv[0:width, :] = projected[0:width] * jnp.asarray(HEAD_DIM**-0.5, BF)
    copies = []
    for index in reversed(range(BLOCKS)):
        upto = (index + 1) * blk
        cols = slice(index * blk, upto)
        keypos = lax.broadcasted_iota(jnp.int32, (upto, blk), 0)
        querypos = lax.broadcasted_iota(jnp.int32, (upto, blk), 1) + index * blk
        allowed = (segc[0:upto, :] == segr[0:1, cols]) & (keypos <= querypos)
        mask[0:upto, :] = jnp.where(allowed, 0.0, MASKED)
        for head in range(heads):
            at = head * HEAD_DIM
            query = qkv[at : at + HEAD_DIM, cols]
            keys = qkv[width + at : width + at + HEAD_DIM, 0:upto]
            values = qkv[2 * width + at : 2 * width + at + HEAD_DIM, 0:upto]
            scores = dot(keys, query, 0, 0) + mask[0:upto, :]
            highest = jnp.max(scores, axis=0, keepdims=True)
            weights = jnp.exp(scores - highest)
            inverse = 1.0 / jnp.sum(weights, axis=0, keepdims=True)
            low = weights.astype(BF)
            buffer[index, head, 0:upto, :] = low
            result = dot(values, low, 1, 0) * inverse
            att[at : at + HEAD_DIM, cols] = result.astype(BF)
            recip[head : head + 1, cols] = inverse
        copy = pltpu.make_async_copy(
            buffer.at[index, :, 0:upto, :], probs.at[index, :, 0:upto, :], sems.at[index]
        )
        copy.start()
        copies.append(copy)
    if not first:
        for copy in fetched:
            copy.wait()
        for ref, place in ((sent, 1 - parity), (kept, parity)):
            cols = pl.ds(pl.multiple_of(place * half, half), half)
            total = dot(att_buffer[:, cols], out_buffers[0], 0, 0)
            total = total + dot(att[:, cols], out_buffers[1], 0, 0)
            ref[...] = total.astype(ref.dtype)
    for copy in copies:
        copy.wait()


def attend(info, first, own, oth, gain, bias, weight, seg_own, seg_oth, *others):
    length = PACKED_LENGTH
    model = own.shape[1]
    width = weight.shape[0] // 3
    heads = width // HEAD_DIM
    blk = length // BLOCKS
    outs = [
        jax.ShapeDtypeStruct((width, length), BF),
        jax.ShapeDtypeStruct((BLOCKS, heads, length, blk), BF),
        jax.ShapeDtypeStruct((3 * width, length), BF),
        jax.ShapeDtypeStruct((8, length), F32),
    ]
    out_specs = [vmem(), hbm(), vmem(), vmem()]
    scratch = [
        pltpu.VMEM((8, length), F32),
        pltpu.VMEM((length, blk), F32),
        pltpu.VMEM((BLOCKS, heads, length, blk), BF),
        pltpu.SemaphoreType.DMA((BLOCKS + 3,)),
    ]
    if first:
        outs = [jax.ShapeDtypeStruct((length, model), BF)] + outs
        out_specs = [vmem()] + out_specs
    else:
        outs = outs + [jax.ShapeDtypeStruct((length // 2, model), d) for d in (BF, F32)]
        out_specs = out_specs + [vmem()] * 2
        scratch += [pltpu.VMEM((width, length), BF), pltpu.VMEM((2, width, model), BF)]
    operands = (own, oth, gain, bias, weight, seg_own, seg_oth)
    return pl.pallas_call(
        functools.partial(attend_kernel, first, heads),
        out_shape=outs,
        in_specs=[smem()] + [vmem()] * len(operands) + [hbm()] * len(others),
        out_specs=out_specs,
        scratch_shapes=scratch,
        compiler_params=params(56),
        cost_estimate=cost(
            6 * length * model * width + 8 * heads * length * length * HEAD_DIM,
            2 * heads * length * length + 6 * length * model,
        ),
        name="attend",
    )(info, *operands, *others)


def middle_kernel(info, tokens, kept, received, gain, bias, places, middle, *outs):
    values = tokens[...].astype(F32) + (kept[...].astype(F32) + received[...])
    middle[...] = values
    scaled, unused = norm_parts(values)
    normed = (scaled * gain[...] + bias[...]).astype(BF)
    put_chunks(normed, places[...], outs)


def middle_call(info, tokens, kept, received, gain, bias, places):
    count, width = tokens.shape
    size = 2 * count // CHUNKS
    return pl.pallas_call(
        middle_kernel,
        out_shape=[jax.ShapeDtypeStruct((count, width), F32)]
        + [jax.ShapeDtypeStruct((size, width), BF)] * CHUNKS,
        in_specs=[smem()] + [vmem()] * 6,
        out_specs=[vmem()] * (1 + CHUNKS),
        compiler_params=params(16),
        cost_estimate=cost(4 * count * count * width, 14 * count * width),
        name="middle",
    )(info, tokens, kept, received, gain, bias, places)


def stage_kernel(info, up, down, up_out, down_out):
    up_out[...] = up[...]
    down_out[...] = down[...]


def stage(info, up, down):
    return pl.pallas_call(
        stage_kernel,
        out_shape=[jax.ShapeDtypeStruct(w.shape, BF) for w in (up, down)],
        in_specs=[smem()] + [vmem()] * 2,
        out_specs=[vmem()] * 2,
        compiler_params=params(12),
        cost_estimate=cost(1, 8 * up.size),
        name="stage",
    )(info, up, down)


def gelu_parts(x):
    z = jnp.abs(x) * (0.5**0.5)
    t = 1.0 / (1.0 + 0.3275911 * z)
    poly = t * (
        0.254829592
        + t * (-0.284496736 + t * (1.421413741 + t * (-1.453152027 + t * 1.061405429)))
    )
    bell = jnp.exp(-0.5 * x * x)
    tail = 0.5 * poly * bell
    phi = jnp.where(x >= 0.0, 1.0 - tail, tail)
    return x * phi, phi + x * bell * 0.3989422804014327


def expert_kernel(chunk, first, info, inputs, grads, own_up, own_down, near, far, *refs):
    if not first:
        refs = refs[1:]
    hidden, gpre, result, given, buffer, grad_buffer, fetched, sems = refs
    size = own_up.shape[0]
    place = info[3] ^ chunk
    copies = [load(grads.at[place], grad_buffer, sems.at[0])]
    copies += [load(ref.at[0 : 2 * size, :], fetched.at[i], sems.at[1 + i]) for i, ref in enumerate((near, far))]
    rows = inputs[...]
    copies[0].wait()
    grad = grad_buffer[...]
    total, forward = None, None
    for tile in range(4):
        if tile < 2:
            at = slice(tile * size, (tile + 1) * size)
            up, down = own_up[:, at], own_down[at, :]
        else:
            copies[tile - 1].wait()
            up, down = fetched[tile - 2, 0:size, :], fetched[tile - 2, size : 2 * size, :]
        at = slice(tile * size, (tile + 1) * size)
        preact = dot(rows, up, 1, 0)
        ghidden = dot(grad, down, 1, 1)
        act, slope = gelu_parts(preact)
        act = act.astype(BF)
        hidden[:, at] = act
        low = (ghidden * slope).astype(BF)
        gpre[:, at] = low
        part = dot(low, up, 1, 1)
        total = part if total is None else total + part
        part = dot(act, down, 1, 0)
        forward = part if forward is None else forward + part
    buffer[...] = forward.astype(BF)
    copy = load(buffer, given.at[place], sems.at[3])
    result[...] = total.astype(BF)
    copy.wait()


def expert(info, chunk, inputs, grads, weights, given=None):
    rows, model = inputs.shape
    tile = weights[0].shape[0]
    operands = [info, inputs, grads, *weights]
    in_specs = [smem(), vmem(), hbm(), vmem(), vmem(), hbm(), hbm()]
    if given is not None:
        operands.append(given)
        in_specs.append(hbm())
    return pl.pallas_call(
        functools.partial(expert_kernel, chunk, given is None),
        out_shape=[
            jax.ShapeDtypeStruct((rows, 4 * tile), BF),
            jax.ShapeDtypeStruct((rows, 4 * tile), BF),
            jax.ShapeDtypeStruct((rows, model), BF),
            jax.ShapeDtypeStruct(grads.shape, BF),
        ],
        in_specs=in_specs,
        out_specs=[vmem()] * 3 + [hbm()],
        scratch_shapes=[
            pltpu.VMEM((rows, model), BF),
            pltpu.VMEM((rows, model), BF),
            pltpu.VMEM((2, 2 * tile, model), BF),
            pltpu.SemaphoreType.DMA((4,)),
        ],
        input_output_aliases={} if given is None else {7: 3},
        compiler_params=params(20),
        cost_estimate=cost(32 * rows * model * tile, 16 * model * tile + 16 * rows * tile),
        name="expert",
    )(*operands)


GIVEN = (3, 3, 2)


def piece_at(theirs, other):
    return 2 * theirs + other, 4 + 2 * other + theirs


def given_at(piece):
    for which, number in enumerate(GIVEN):
        if piece < number:
            return which, piece
        piece -= number


def expert_weights_kernel(info, grads, *refs):
    n = CHUNKS
    inputs, hiddens, gpres = refs[:n], refs[n : 2 * n], refs[2 * n : 3 * n]
    stays, given = refs[3 * n], refs[3 * n + 1 : 3 * n + 4]
    sub = stays.shape[1]
    size = 2 * sub
    parity, row_half, here = info[0], info[1], info[3]
    mine = pl.multiple_of(parity * sub, sub)
    gone = pl.multiple_of((1 - parity) * sub, sub)
    for theirs in range(2):
        for other in range(2):
            tile = other ^ row_half
            if theirs:
                tile = 2 + (tile ^ parity)
            for offset, keeps in ((mine, True), (gone, False)):
                at = pl.ds(pl.multiple_of(tile * size + offset, sub), sub)
                for is_down, piece in enumerate(piece_at(theirs, other)):
                    total = None
                    for index in range(n):
                        source = (hiddens if is_down else gpres)[index][:, at]
                        factor = grads[here ^ index] if is_down else inputs[index][...]
                        part = dot(source, factor, 0, 0)
                        total = part if total is None else total + part
                    which, place = given_at(piece)
                    if keeps:
                        stays[piece] = total.astype(BF)
                    else:
                        given[which][place] = total.astype(BF)


def expert_weights(info, inputs, grads, hiddens, gpres):
    rows, model = inputs[0].shape
    sub = hiddens[0].shape[1] // 8
    return pl.pallas_call(
        expert_weights_kernel,
        out_shape=[jax.ShapeDtypeStruct((m, sub, model), BF) for m in (8, *GIVEN)],
        in_specs=[smem()] + [vmem()] * (1 + 3 * CHUNKS),
        out_specs=[vmem()] * 4,
        compiler_params=params(20),
        cost_estimate=cost(32 * CHUNKS * rows * model * sub, 64 * model * sub),
        name="expert_weights",
    )(info, grads, *inputs, *hiddens, *gpres)


def pieces_kernel(info, stays, first, second, third, kept, sent_one, sent_two, sent_down):
    received = (first, second, third)
    for ref, pieces in (
        (kept, (0, 1, 4, 5)),
        (sent_one, (2,)),
        (sent_two, (3,)),
        (sent_down, (6, 7)),
    ):
        for index, piece in enumerate(pieces):
            which, place = given_at(piece)
            total = stays[piece].astype(F32) + received[which][place].astype(F32)
            ref[index] = total.astype(BF)


def add_pieces(info, stays, *received):
    n, sub, model = stays.shape
    return pl.pallas_call(
        pieces_kernel,
        out_shape=[jax.ShapeDtypeStruct((m, sub, model), BF) for m in (4, 1, 1, 2)],
        in_specs=[smem()] + [vmem()] * 4,
        out_specs=[vmem()] * 4,
        compiler_params=params(20),
        cost_estimate=cost(stays.size, 6 * stays.size),
        name="add_pieces",
    )(info, stays, *received)


def more_pieces_kernel(info, kept, one, two, got_down, up, down, sent_up, sent_down):
    for index, got, ref in (
        (0, one.at[0], up),
        (1, two.at[0], sent_up),
        (2, got_down.at[0], down),
        (3, got_down.at[1], sent_down),
    ):
        ref[...] = (kept[index].astype(F32) + got[...].astype(F32)).astype(BF)


def more_pieces(info, kept, *got):
    n, sub, model = kept.shape
    return pl.pallas_call(
        more_pieces_kernel,
        out_shape=[jax.ShapeDtypeStruct((sub, model), BF)] * 4,
        in_specs=[smem()] + [vmem()] * 4,
        out_specs=[vmem()] * 4,
        compiler_params=params(60),
        cost_estimate=cost(kept.size, 6 * kept.size),
        name="more_pieces",
    )(info, kept, *got)


def last_pieces_kernel(info, up, down, got_up, got_down, grad_up, grad_down):
    grad_up[...] = jnp.transpose(up[...].astype(F32) + got_up[...].astype(F32))
    grad_down[...] = down[...].astype(F32) + got_down[...].astype(F32)


def last_pieces(info, up, down, got_up, got_down):
    sub, model = up.shape
    return pl.pallas_call(
        last_pieces_kernel,
        out_shape=[
            jax.ShapeDtypeStruct((model, sub), F32),
            jax.ShapeDtypeStruct((sub, model), F32),
        ],
        in_specs=[smem()] + [vmem()] * 4,
        out_specs=[vmem()] * 2,
        compiler_params=params(60),
        cost_estimate=cost(up.size, 16 * up.size),
        name="last_pieces",
    )(info, up, down, got_up, got_down)


def second_back_kernel(info, *refs):
    chunks = refs[:CHUNKS]
    middle, cot, gain, places, gmid, gvec = refs[CHUNKS:]
    grad = take_chunks(chunks, places[...])
    scaled, inverse = norm_parts(middle[...])
    total = cot[...].astype(F32) + norm_back(grad, scaled, inverse, gain[...])
    gmid[...] = total
    gvec[...] = jnp.zeros_like(gvec)
    gvec[0:1, :] = jnp.sum(grad * scaled, axis=0, keepdims=True)
    gvec[1:2, :] = jnp.sum(grad, axis=0, keepdims=True)


def second_back(info, chunks, middle, cotangent, gain, places):
    count, width = cotangent.shape
    return pl.pallas_call(
        second_back_kernel,
        out_shape=[
            jax.ShapeDtypeStruct((count, width), F32),
            jax.ShapeDtypeStruct((8, width), F32),
        ],
        in_specs=[smem()] + [vmem()] * (CHUNKS + 4),
        out_specs=[vmem()] * 2,
        compiler_params=params(16),
        cost_estimate=cost(4 * count * count * width, 16 * count * width),
        name="second_back",
    )(info, *chunks, middle, cotangent, gain, places)


def output_kernel(info, results, middle, gate, places, out):
    total = take_chunks([results], places[...])
    out[...] = (middle[...] + column(gate[...]) * total).astype(BF)


def output_call(info, results, middle, gate, places):
    return pl.pallas_call(
        output_kernel,
        out_shape=jax.ShapeDtypeStruct(middle.shape, BF),
        in_specs=[smem()] + [vmem()] * 4,
        out_specs=vmem(),
        compiler_params=params(60),
        cost_estimate=cost(4 * middle.shape[0] * middle.size, 8 * middle.size),
        name="output",
    )(info, results, middle, gate, places)


def load_probs(probs, buffer, sems):
    copies = []
    blk = buffer.shape[3]
    for index in range(BLOCKS):
        upto = (index + 1) * blk
        copy = pltpu.make_async_copy(
            probs.at[index, :, 0:upto, :], buffer.at[index, :, 0:upto, :], sems.at[index]
        )
        copy.start()
        copies.append(copy)
    return copies


def back_values_kernel(info, own, oth, rows, *refs):
    outws, atts, recips, probs = refs[0:2], refs[2:4], refs[4:6], refs[6:8]
    outs = refs[8:16]
    gbranch, gsum, row_buffer, sems = refs[16:18] + refs[20:22]
    buffers = refs[18:20]
    copies = [load_probs(probs[g], buffers[g], sems.at[g]) for g in range(2)]
    row_copy = load(rows, row_buffer, sems.at[0, BLOCKS])
    length = PACKED_LENGTH
    width = atts[0].shape[0]
    blk = length // BLOCKS
    half = length // 2
    parity = info[0]
    for ref, place in ((own, parity), (oth, 1 - parity)):
        gbranch[pl.ds(pl.multiple_of(place * half, half), half), :] = ref[...].astype(BF)
    for g in range(2):
        scaled_ref, inner_ref, gvalues, gweight = outs[4 * g : 4 * g + 4]
        att, recip, buffer = atts[g], recips[g], buffers[g]
        gatt = dot(outws[g][...], gbranch[...], 1, 1).astype(BF).astype(F32)
        for head in range(width // HEAD_DIM):
            at = slice(head * HEAD_DIM, (head + 1) * HEAD_DIM)
            scaled = (gatt[at] * recip[head : head + 1, :]).astype(BF)
            scaled_ref[at, :] = scaled
            inner_ref[head : head + 1, :] = jnp.sum(
                scaled.astype(F32) * att[at, :].astype(F32), axis=0, keepdims=True
            )
        gweight[width:, :] = dot(att[...], gbranch[...], 1, 0).astype(BF)
        gsum[...] = jnp.zeros_like(gsum)
        for index in range(BLOCKS):
            upto = (index + 1) * blk
            cols = slice(index * blk, upto)
            copies[g][index].wait()
            for head in range(width // HEAD_DIM):
                at = slice(head * HEAD_DIM, (head + 1) * HEAD_DIM)
                low = buffer[index, head, 0:upto, :]
                gsum[at, 0:upto] += dot(scaled_ref[at, cols], low, 1, 1)
        low = gsum[...].astype(BF)
        gvalues[...] = low
        if g == 0:
            row_copy.wait()
        gweight[0:width, :] = dot(low, row_buffer[...], 1, 0).astype(BF)


def back_values(info, own, oth, rows, outws, atts, recips, probs):
    length, model = rows.shape
    width = atts[0].shape[0]
    heads = width // HEAD_DIM
    shapes = [((width, length), BF), ((8, length), F32), ((width, length), BF)]
    shapes.append(((2 * width, model), BF))
    shapes = shapes * 2
    kept = pltpu.VMEM((BLOCKS, heads, length, length // BLOCKS), BF)
    outs = pl.pallas_call(
        back_values_kernel,
        out_shape=[jax.ShapeDtypeStruct(s, d) for s, d in shapes],
        in_specs=[smem()] + [vmem()] * 2 + [hbm()] + [vmem()] * 6 + [hbm()] * 2,
        out_specs=[vmem()] * len(shapes),
        scratch_shapes=[
            pltpu.VMEM((length, model), BF),
            pltpu.VMEM((width, length), F32),
            kept,
            kept,
            pltpu.VMEM((length, model), BF),
            pltpu.SemaphoreType.DMA((2, BLOCKS + 1)),
        ],
        compiler_params=params(56),
        cost_estimate=cost(
            16 * length * model * width + 8 * heads * length * length * HEAD_DIM,
            4 * heads * length * length + 10 * length * model,
        ),
        name="back_values",
    )(info, own, oth, rows, *outws, *atts, *recips, *probs)
    return outs


def back_keys_kernel(info, qkv, scaled, inner, gvalues, rows, probs, gweight, gqkv, *scratch):
    gsum, buffer, row_buffer, sems = scratch
    copies = load_probs(probs, buffer, sems)
    row_copy = load(rows, row_buffer, sems.at[BLOCKS])
    length = PACKED_LENGTH
    width = scaled.shape[0]
    blk = length // BLOCKS
    gsum[...] = jnp.zeros_like(gsum)
    for index in range(BLOCKS):
        upto = (index + 1) * blk
        cols = slice(index * blk, upto)
        copies[index].wait()
        for head in range(width // HEAD_DIM):
            at = head * HEAD_DIM
            here = slice(at, at + HEAD_DIM)
            kat = slice(width + at, width + at + HEAD_DIM)
            vat = slice(2 * width + at, 2 * width + at + HEAD_DIM)
            gprobs = dot(qkv[vat, 0:upto], scaled[here, cols], 0, 0)
            low = buffer[index, head, 0:upto, :].astype(F32)
            gscores = (low * (gprobs - inner[head : head + 1, cols])).astype(BF)
            gsum[here, 0:upto] += dot(qkv[here, cols], gscores, 1, 1)
            gqueries = dot(qkv[kat, 0:upto], gscores, 1, 0) * HEAD_DIM**-0.5
            gqkv[here, cols] = gqueries.astype(BF)
    gqkv[width : 2 * width, :] = gsum[...].astype(BF)
    gqkv[2 * width :, :] = gvalues[...]
    row_copy.wait()
    gweight[...] = dot(gqkv[0 : 2 * width, :], row_buffer[...], 1, 0).astype(BF)


def back_keys(info, qkv, scaled, inner, gvalues, rows, probs):
    length, model = rows.shape
    width = scaled.shape[0]
    heads = width // HEAD_DIM
    return pl.pallas_call(
        back_keys_kernel,
        out_shape=[
            jax.ShapeDtypeStruct((2 * width, model), BF),
            jax.ShapeDtypeStruct((3 * width, length), BF),
        ],
        in_specs=[smem()] + [vmem()] * 4 + [hbm()] * 2,
        out_specs=[vmem()] * 2,
        scratch_shapes=[
            pltpu.VMEM((width, length), F32),
            pltpu.VMEM((BLOCKS, heads, length, length // BLOCKS), BF),
            pltpu.VMEM((length, model), BF),
            pltpu.SemaphoreType.DMA((BLOCKS + 1,)),
        ],
        compiler_params=params(56),
        cost_estimate=cost(
            4 * length * model * width + 12 * heads * length * length * HEAD_DIM,
            2 * heads * length * length + 10 * length * model,
        ),
        name="back_keys",
    )(info, qkv, scaled, inner, gvalues, rows, probs)


def back_rows_kernel(info, gqkv_a, gqkv_b, weight_a, weight_b, kept, sent_low, sent_high):
    half = kept.shape[0]
    parity = info[0]
    for refs, place in (((sent_low, sent_high), 1 - parity), ((kept,), parity)):
        at = pl.ds(pl.multiple_of(place * half, half), half)
        total = dot(gqkv_a[:, at], weight_a[...], 0, 0) + dot(gqkv_b[:, at], weight_b[...], 0, 0)
        size = half // len(refs)
        for index, ref in enumerate(refs):
            ref[...] = total[index * size : (index + 1) * size].astype(ref.dtype)


def back_rows(info, gqkv_a, gqkv_b, weight_a, weight_b):
    length = gqkv_a.shape[1]
    model = weight_a.shape[1]
    return pl.pallas_call(
        back_rows_kernel,
        out_shape=[
            jax.ShapeDtypeStruct((length // 2, model), BF),
            jax.ShapeDtypeStruct((length // 4, model), BF),
            jax.ShapeDtypeStruct((length // 4, model), BF),
        ],
        in_specs=[smem()] + [vmem()] * 4,
        out_specs=[vmem()] * 3,
        compiler_params=params(60),
        cost_estimate=cost(4 * length * model * gqkv_a.shape[0], 6 * length * model),
        name="back_rows",
    )(info, gqkv_a, gqkv_b, weight_a, weight_b)


def first_back_kernel(info, tokens, gmid, kept, low, high, gain, second, ginput, gvec):
    received = jnp.concatenate([low[...], high[...]], axis=0)
    grad = kept[...].astype(F32) + received.astype(F32)
    scaled, inverse = norm_parts(tokens[...].astype(F32))
    ginput[...] = gmid[...] + norm_back(grad, scaled, inverse, gain[...])
    gvec[...] = jnp.zeros_like(gvec)
    gvec[2:4, :] = second[0:2, :]
    gvec[0:1, :] = jnp.sum(grad * scaled, axis=0, keepdims=True)
    gvec[1:2, :] = jnp.sum(grad, axis=0, keepdims=True)


def first_back(info, tokens, gmid, kept, low, high, gain, second):
    count, width = tokens.shape
    return pl.pallas_call(
        first_back_kernel,
        out_shape=[
            jax.ShapeDtypeStruct((count, width), F32),
            jax.ShapeDtypeStruct((8, width), F32),
        ],
        in_specs=[smem()] + [vmem()] * 7,
        out_specs=[vmem()] * 2,
        compiler_params=params(60),
        cost_estimate=cost(20 * count * width, 16 * count * width),
        name="first_back",
    )(info, tokens, gmid, kept, low, high, gain, second)


def first_sum_kernel(info, mine, theirs, kept, sent):
    half = kept.shape[0]
    k = info[2]
    for ref, which in ((sent, 1 - k), (kept, k)):
        at = pl.ds(pl.multiple_of(which * half, half), half)
        ref[...] = (mine[at, :].astype(F32) + theirs[at, :].astype(F32)).astype(ref.dtype)


def first_sum(info, mine, theirs):
    rows, model = mine.shape
    return pl.pallas_call(
        first_sum_kernel,
        out_shape=[
            jax.ShapeDtypeStruct((rows // 2, model), F32),
            jax.ShapeDtypeStruct((rows // 2, model), BF),
        ],
        in_specs=[smem()] + [vmem()] * 2,
        out_specs=[vmem()] * 2,
        compiler_params=params(60),
        cost_estimate=cost(rows * model, 7 * rows * model),
        name="first_sum",
    )(info, mine, theirs)


def second_sum_kernel(info, kept, received, out):
    out[...] = (kept[...] + received[...].astype(F32)).astype(BF)


def second_sum(info, kept, received):
    return pl.pallas_call(
        second_sum_kernel,
        out_shape=jax.ShapeDtypeStruct(kept.shape, BF),
        in_specs=[smem()] + [vmem()] * 2,
        out_specs=vmem(),
        compiler_params=params(60),
        cost_estimate=cost(kept.size, 8 * kept.size),
        name="second_sum",
    )(info, kept, received)


def sum_blocks(blocks):
    total = None
    for index in range(blocks.shape[0]):
        block = blocks[index].astype(F32)
        total = block if total is None else total + block
    return total.astype(BF)


def middle_sum_kernel(info, blocks, kept, received, out):
    rows = blocks.shape[1]
    total = sum_blocks(blocks)
    for index in range(out.shape[0]):
        at = slice(index * rows, (index + 1) * rows)
        out[index, 0:rows] = total
        out[index, rows:] = (kept[at, :] + received[at, :].astype(F32)).astype(BF)


def middle_sum(info, blocks, kept, received):
    pieces, rows, model = blocks.shape
    return pl.pallas_call(
        middle_sum_kernel,
        out_shape=jax.ShapeDtypeStruct((pieces, 2 * rows, model), BF),
        in_specs=[smem()] + [vmem()] * 3,
        out_specs=vmem(),
        compiler_params=params(60),
        cost_estimate=cost(kept.size, 8 * kept.size),
        name="middle_sum",
    )(info, blocks, kept, received)


def third_sum_kernel(info, blocks, vectors, core, row, both_ways, out, other):
    pieces, rows = other.shape[0:2]
    total = None
    for index in range(pieces):
        other[index] = blocks[index, 0:rows]
        block = blocks[index, rows:].astype(F32)
        total = block if total is None else total + block
    total = total.astype(BF)
    values = (vectors[...] + core[...]) + (row[...] + both_ways[...])
    high = values.astype(BF)
    low = (values - high.astype(F32)).astype(BF)
    both = jnp.concatenate([high, low], axis=0)
    for index in range(pieces):
        out[index, 0:rows] = total
        out[index, rows:] = both


def third_sum(info, blocks, vectors, *others):
    pieces, rows, model = blocks.shape
    extra = 2 * vectors.shape[0]
    return pl.pallas_call(
        third_sum_kernel,
        out_shape=[
            jax.ShapeDtypeStruct((pieces, rows // 2 + extra, model), BF),
            jax.ShapeDtypeStruct((pieces, rows // 2, model), BF),
        ],
        in_specs=[smem()] + [vmem()] * 5,
        out_specs=[vmem()] * 2,
        compiler_params=params(60),
        cost_estimate=cost(blocks.size, 4 * blocks.size),
        name="third_sum",
    )(info, blocks, vectors, *others)


def last_kernel(info, mine_qk, theirs_qk, mine_vo, theirs_vo, qkv, out, *vectors):
    width = mine_vo.shape[0]
    pieces = mine_qk.shape[0]
    rows = width // pieces
    count = (mine_qk.shape[1] - rows) // 2
    k = info[2]

    def write(queries, keys, values, outs):
        for index in range(pieces):
            at = index * rows
            qkv[at : at + rows, :] = queries[index, 0:rows].astype(F32)
            qkv[width + at : width + at + rows, :] = keys[index, 0:rows].astype(F32)
        qkv[2 * width :, :] = values[...].astype(F32)
        out[...] = outs[...].astype(F32)

    @pl.when(k == 0)
    def even():
        write(mine_qk, theirs_qk, mine_vo, theirs_vo)

    @pl.when(k != 0)
    def odd():
        write(theirs_qk, mine_qk, theirs_vo, mine_vo)

    sums = []
    for ref in (mine_qk, theirs_qk):
        total = None
        for index in range(pieces):
            both = ref[index, rows:].astype(F32)
            value = both[0:count] + both[count:]
            total = value if total is None else total + value
        sums.append(total)
    for index, ref in enumerate(vectors):
        ref[...] = sums[0][index] + sums[1][index]


def last(info, mine_qk, theirs_qk, mine_vo, theirs_vo):
    width, model = mine_vo.shape
    return pl.pallas_call(
        last_kernel,
        out_shape=[
            jax.ShapeDtypeStruct((3 * width, model), F32),
            jax.ShapeDtypeStruct((width, model), F32),
        ]
        + [jax.ShapeDtypeStruct((model,), F32)] * 4,
        in_specs=[smem()] + [vmem()] * 4,
        out_specs=[vmem()] * 6,
        compiler_params=params(60),
        cost_estimate=cost(width * model, 24 * width * model),
        name="last",
    )(info, mine_qk, theirs_qk, mine_vo, theirs_vo)


def after(values, *others):
    return lax.optimization_barrier((values, *others))[0]


def swap(values, axis, bit):
    pairs = [(i, i ^ bit) for i in range(lax.axis_size(axis))]
    return lax.ppermute(values, axis, pairs)


def exchange(values, count):
    groups = [[2 * e + k for e in range(count)] for k in range(2)]
    shaped = values.reshape(count, -1, values.shape[1])
    moved = lax.all_to_all(shaped, "dp", 0, 0, tiled=True, axis_index_groups=groups)
    return moved.reshape(values.shape)


def exchange_chunks(chunks, count):
    moved = exchange(jnp.concatenate(chunks, axis=0), count)
    size = chunks[0].shape[0]
    return [moved[i * size : (i + 1) * size] for i in range(len(chunks))]


def local(
    tokens,
    first_gain,
    first_bias,
    qkv_weight,
    out_weight,
    second_gain,
    expert_norm_bias,
    up_weight,
    down_weight,
    gate_value,
    expert_ids,
    slot_index,
    segment_ids,
    cotangent,
):
    count, model = tokens.shape
    width = qkv_weight.shape[2]
    tp = lax.axis_index("tp")
    dp = lax.axis_index("dp")
    parity = tp % 2
    row_half = tp // 2 % 2
    k = dp % 2
    experts = lax.axis_size("dp") // 2
    capacity = 2 * count // experts
    paired = experts == CHUNKS
    here = dp // 2 if paired else 0 * dp
    info = jnp.stack([parity, row_half, k, here]).astype(jnp.int32)
    vector = lambda v: v.reshape(1, -1)
    gain, bias = first_gain, first_bias

    state = [info]

    def run(call, *operands):
        outs = call(state[0], *operands)
        state[0] = after(info, outs[-1] if isinstance(outs, (list, tuple)) else outs)
        return outs

    other_tokens = swap(tokens, "tp", 1)
    other_segments = swap(segment_ids, "tp", 1)
    weight_a = jnp.transpose(qkv_weight, (1, 2, 0)).reshape(3 * width, model)
    weight_b = swap(weight_a, "tp", 2)
    out_b = swap(out_weight, "tp", 2)
    up, down = up_weight[0], down_weight[0]
    gate = vector(gate_value)
    slots = vector(expert_ids * capacity + slot_index)
    sent_grads, given = run(
        dispatch, capacity, cotangent, gate, vector(expert_ids), vector(slot_index), up, down
    )
    near = swap(given, "dp", 1)
    grads = exchange(sent_grads, experts).reshape(CHUNKS, -1, model)

    segments = (vector(segment_ids), vector(other_segments))
    rows, att_a, probs_a, qkv_a, recip_a = run(
        attend, True, tokens, other_tokens, gain, bias, weight_a, *segments
    )
    att_b, probs_b, qkv_b, recip_b, kept, sent = run(
        attend, False, rows, vector(other_segments), gain, bias, weight_b, *segments,
        att_a, out_weight, out_b,
    )
    received = swap(sent, "tp", 1)
    places = vector((expert_ids ^ here) * capacity + slot_index)
    middle, *sent_rows = run(
        middle_call, tokens, kept, received, second_gain, expert_norm_bias, places
    )

    if paired:
        first, second = lax.optimization_barrier(
            (swap(sent_rows[1], "dp", 2), swap(sent_rows[2], "dp", 4))
        )
        third = swap(after(sent_rows[3], second), "dp", 6)
        inputs = [sent_rows[0], first, second, third]
    else:
        inputs = exchange_chunks(sent_rows, experts)
    far = swap(after(near, inputs[1], grads), "tp", 1)
    weights = (*run(stage, up, down), near, far)
    hiddens, gpres, backs = [[None] * CHUNKS for unused in range(3)]
    results = None
    for index in (*range(1, CHUNKS), 0):
        hiddens[index], gpres[index], backs[index], results = run(
            expert, index, inputs[index], grads, weights, results
        )
    if paired:
        returned = [backs[0]] + [swap(backs[s], "dp", 2 * s) for s in range(1, CHUNKS)]
    else:
        returned = exchange_chunks(backs, experts)
    if paired:
        inputs[0], returned[1] = lax.optimization_barrier((inputs[0], returned[1]))
    stays, *leaves = run(expert_weights, inputs, grads, hiddens, gpres)
    leaves = [swap(leaf, "tp", 1) for leaf in leaves]
    gmid, gvec_two = run(
        second_back, returned, middle, cotangent, second_gain, places
    )
    other_gmid = swap(gmid, "tp", 1)
    outs = exchange(after(results, gmid).reshape(-1, model), experts)

    values = run(
        back_values, gmid, other_gmid, rows, (out_b, out_weight), (att_b, att_a),
        (recip_b, recip_a), (probs_b, probs_a),
    )
    scaled_b, inner_b, gvalues_b, gvo_b = values[0:4]
    scaled_a, inner_a, gvalues_a, gvo_a = values[4:8]
    theirs_vo = swap(gvo_b, "tp", 2)
    kept_pieces, sent_one, sent_two, sent_down = run(add_pieces, stays, *leaves)
    got_one = swap(sent_one, "dp", 1)
    gqk_b, gqkv_b = run(back_keys, qkv_b, scaled_b, inner_b, gvalues_b, rows, probs_b)
    theirs_qk = swap(gqk_b, "tp", 2)
    vo_kept, vo_sent = run(first_sum, gvo_a, theirs_vo)
    vo_received = swap(vo_sent, "dp", 1)
    gqk_a, gqkv_a = run(back_keys, qkv_a, scaled_a, inner_a, gvalues_a, rows, probs_a)
    got_two = swap(after(sent_two, gqk_a), "dp", 1)
    got_down = swap(after(sent_down, gqk_a), "tp", 2)

    def over_experts(blocks):
        moved = exchange(blocks.reshape(-1, model), experts)
        return moved.reshape(experts, -1, model)

    blocks_vo = over_experts(run(second_sum, vo_kept, after(vo_received, outs, got_one)))
    qk_kept, qk_sent = run(first_sum, gqk_a, theirs_qk)
    qk_received = swap(qk_sent, "dp", 1)
    gkept, *gsent = run(back_rows, gqkv_a, gqkv_b, weight_a, weight_b)
    greceived = [swap(g, "tp", 1) for g in gsent]
    blocks = over_experts(run(middle_sum, after(blocks_vo, got_two), qk_kept, qk_received))
    up_kept, down_kept, sent_up, sent_down = run(
        more_pieces, kept_pieces, got_one, got_two, got_down
    )
    last_down = swap(sent_down, "dp", 1)
    grad_input, vectors = run(first_back, tokens, gmid, gkept, *greceived, gain, gvec_two)
    others = [swap(vectors, "tp", bit) for bit in (1, 2, 3)]
    last_up = swap(after(sent_up, *others), "tp", 2)
    total_qk, full_vo = run(third_sum, blocks, vectors, *others)
    full_qk = over_experts(total_qk)
    full_vo = full_vo.reshape(width, model)
    other_vo = swap(after(full_vo, last_down), "dp", 1)
    output = run(output_call, outs, middle, gate, slots)
    full_qk, other_vo = lax.optimization_barrier((full_qk, other_vo))
    other_qk = swap(full_qk, "dp", 1)
    grad_up, grad_down = run(last_pieces, up_kept, down_kept, last_up, last_down)
    grad_qkv, grad_out, *vectors = run(last, full_qk, other_qk, full_vo, other_vo)
    grad_qkv = jnp.transpose(grad_qkv.reshape(3, width, model), (2, 0, 1))
    return (
        output,
        grad_input,
        vectors[0],
        vectors[1],
        grad_qkv,
        grad_out,
        vectors[2],
        vectors[3],
        grad_up[None],
        grad_down[None],
    )


def solution(mesh):
    placed = (
        P(("dp", "tp"), None),
        P(),
        P(),
        P(None, None, "tp"),
        P("tp", None),
        P(),
        P(),
        P("dp", None, None),
        P("dp", None, None),
        P(("dp", "tp")),
        P(("dp", "tp")),
        P(("dp", "tp")),
        P(("dp", "tp")),
        P(("dp", "tp"), None),
    )
    return jax.shard_map(
        local,
        mesh=mesh,
        in_specs=placed,
        out_specs=(
            P(("dp", "tp"), None),
            P(("dp", "tp"), None),
            P(),
            P(),
            P(None, None, "tp"),
            P("tp", None),
            P(),
            P(),
            P("dp", None, "tp"),
            P("dp", "tp", None),
        ),
        check_vma=False,
    )
```
